32 devices in a mesh: req: 8 (over z, y), kv: 4 (over x, core).
Axes of the slice: x: 2, y: 2, z: 4, core: 2. Of those that a mesh axis runs over, the one named last changes fastest.
Arguments:
- hidden_in: bfloat16 [8192, 2048], P(('req', 'kv')), may hold values from -6 to 6
- slot_tokens: int32 [8192], replicated, may hold values from 0 to 8191, as said below
- cache_len: int32 [64], P('req'), may hold values from 1 to 2048, 32768 in all
- prefill_start: int32 [8], P('req'), may hold values from 0 to 2048
- key_cache: bfloat16 [64, 2048, 1024], P('req', None, 'kv')
- value_cache: bfloat16 [64, 2048, 1024], P('req', None, 'kv'), may hold values from -18 to 18
- key_prefix: bfloat16 [8, 2048, 1024], P('req', None, 'kv')
- value_prefix: bfloat16 [8, 2048, 1024], P('req', None, 'kv'), may hold values from -18 to 18
- attn_gain: float32 [2048], replicated, may hold values from 0.25 to 1.75
- q_proj: bfloat16 [2048, 2048], P(None, 'kv'), may hold values from -0.125 to 0.125
- k_proj: bfloat16 [2048, 1024], P(None, 'kv'), may hold values from -0.125 to 0.125
- v_proj: bfloat16 [2048, 1024], P(None, 'kv'), may hold values from -0.125 to 0.125
- q_gain: float32 [128], replicated, may hold values from 0.25 to 1.75
- k_gain: float32 [128], replicated, may hold values from 0.25 to 1.75
- o_proj: bfloat16 [2048, 2048], P('kv'), may hold values from -0.125 to 0.125
- ffn_gain: float32 [2048], replicated, may hold values from 0.25 to 1.75
- w_gate: bfloat16 [2048, 6144], P(None, 'req'), may hold values from -0.125 to 0.125
- w_up: bfloat16 [2048, 6144], P(None, 'req'), may hold values from -0.125 to 0.125
- w_down: bfloat16 [6144, 2048], P('req'), may hold values from -0.078125 to 0.078125
- final_gain: float32 [2048], replicated, may hold values from 0.25 to 1.75
- lm_head: bfloat16 [2048, 151936], P(None, ('req', 'kv')), may hold values from -0.375 to 0.375
Outputs:
- layer_out: bfloat16 [8192, 2048], P(('req', 'kv'))
- max_logit: float32 [72], replicated
The draws below stay inside these ranges and needn't reach their ends.
Inputs may be any that keep to these rules, and one draw needn't show every extreme that they name: slot_tokens is a permutation of the batch's tokens; each device's 256 consecutive slots take exactly 8 tokens from each device's 256 consecutive batch tokens.
All inputs are finite; a program needn't handle non-finite values. No bound on the sum of `cache_len` on one device may be relied on, other than what follows from the above.
Results may differ from the reference program's by a relative error of at most 0.0085.
The reference program's roundings to bfloat16 on the way count: a program that leaves them out, or rounds other values in their place, can miss the bound.
Values may be sent and summed in bfloat16 or wider, within the bound.
No kernel may reach another device: no remote copies, remote signals or barrier semaphores. Data moves between devices by JAX's collectives and lax.ppermute only.
A program may use at most 192 MiB of HBM per device.

```python
import math
import jax
import jax.numpy as jnp
import numpy as np
from jax import lax

D = 2048
HEADS = 16
KV_HEADS = 8
HEAD_DIM = 128
FF = 6144
VOCAB = 151936
DEC_DEV = 8
TOK_REQ = 1024
CACHE = 2048
PREFIX = 2048
PREFILL_TOK = 1016
ROWS = 256
TOKENS = 8192
DEC = 64
LOGIT_ROWS = 72
N_REQ = 8


def draw_slot_tokens(key, part):
    devices = TOKENS // ROWS
    per_pair = ROWS // devices
    first_keys = jax.random.split(jax.random.fold_in(key, 11), devices)
    shuffled = jax.vmap(lambda sub_key: jax.random.permutation(sub_key, ROWS))(first_keys).astype(jnp.int32)
    tokens_by = shuffled + (jnp.arange(devices, dtype=jnp.int32) * ROWS)[:, None]
    grouped = tokens_by.reshape(devices, devices, per_pair).transpose(1, 0, 2).reshape(devices, ROWS)
    second_keys = jax.random.split(jax.random.fold_in(key, 12), devices)
    orders = jax.vmap(lambda sub_key: jax.random.permutation(sub_key, ROWS))(second_keys).astype(jnp.int32)
    return jnp.take_along_axis(grouped, orders, axis=1).reshape(TOKENS).astype(jnp.int32)


def draw_prefill_start(key, part):
    base_draw = jax.random.randint(jax.random.fold_in(key, 21), (N_REQ,), 0, PREFIX + 1).astype(jnp.int32)
    skewed = base_draw * base_draw // PREFIX
    chosen = jax.random.randint(jax.random.fold_in(key, 22), (), 0, N_REQ)
    return skewed.at[chosen].set(PREFIX).astype(jnp.int32)


def shifted_keys(key, lead, slots):
    shape = (lead, slots, KV_HEADS, HEAD_DIM)
    noise = 3.0 * jnp.clip(jax.random.normal(key, shape, jnp.float32), -6.0, 6.0)
    offset = 40.0 * float(HEAD_DIM) ** 0.5
    lift = jnp.where(jnp.arange(HEAD_DIM, dtype=jnp.int32) == 0, offset, 0.0).astype(jnp.float32)
    return (noise + lift).reshape(lead, slots, KV_HEADS * HEAD_DIM).astype(jnp.bfloat16)


def draw_key_cache(key, part):
    return shifted_keys(jax.random.fold_in(key, 31), DEC, CACHE)


def draw_key_prefix(key, part):
    return shifted_keys(jax.random.fold_in(key, 32), N_REQ, PREFIX)


def block_levels(key, shape, shards, low, top_value):
    level = 1.0
    for axis_at, blocks in shards:
        steps = jax.random.uniform(jax.random.fold_in(jax.random.fold_in(key, 6), axis_at), (blocks,), jnp.float32, low / len(shards), top_value / len(shards))
        level = level * jnp.repeat(jnp.exp(steps), shape[axis_at] // blocks).reshape((-1,) + (1,) * (len(shape) - 1 - axis_at))
    return level


def split_up(number_of, total, reach, slope):
    weights = [(1 << 20) // math.isqrt(standing ** slope) + 1 for standing in range(2, number_of + 1)]
    spare, counts = total - reach - (number_of - 1), [1] * (number_of - 1)
    while spare > 0:
        movable = [i for i in range(number_of - 1) if counts[i] < reach]
        pool, left = sum([weights[i] for i in movable]), spare
        for i in movable:
            addition = min(reach - counts[i], max(1, left * weights[i] // pool), spare)
            counts[i] = counts[i] + addition
            spare = spare - addition
    return np.array([reach] + counts)


def ragged_sizes(own_key, count, total, most, lean):
    if count == 2:
        one = jax.random.randint(own_key, (), max(1, total - most), min(most, total - 1) + 1)
        return jnp.stack([one, total - one])
    sizes = jnp.asarray(split_up(count, total, most, lean), jnp.int32)
    twos = (count - 1) // 2
    source_of, receiver = sizes[1:1 + 2 * twos:2], sizes[2:2 + 2 * twos:2]
    margin = jnp.minimum(source_of - 1, most - receiver)
    shifted = jax.random.randint(jax.random.fold_in(own_key, 1), (twos,), 0, 1 << 20) % (margin + 1)
    sizes = sizes.at[1:1 + 2 * twos:2].set(source_of - shifted).at[2:2 + 2 * twos:2].set(receiver + shifted)
    return sizes[jax.random.permutation(jax.random.fold_in(own_key, 2), count)]


def centred(stream_key, dims, spread, reach, cuts=(), kind=jnp.bfloat16):
    entries = spread * jax.random.normal(stream_key, dims, jnp.float32)
    if cuts:
        entries = entries * block_levels(stream_key, dims, cuts, -0.22, 0.18)
    return jnp.clip(entries, -reach, reach).astype(kind)


def setup_inputs(seed: int = 0) -> dict:
    streams_of = jax.random.split(jax.random.key(seed), 22)
    hidden_in = centred(streams_of[0], (TOKENS, D), 1.0, 6.0, ((0, 32),))
    slot_tokens = draw_slot_tokens(jax.random.fold_in(streams_of[21], 71), 0)
    cache_len = ragged_sizes(streams_of[2], DEC, DEC * CACHE // 4, CACHE, 2).astype(jnp.int32)
    prefill_start = draw_prefill_start(jax.random.fold_in(streams_of[21], 71), 0)
    key_cache = draw_key_cache(jax.random.fold_in(streams_of[21], 71), 0)
    value_cache = centred(streams_of[5], (DEC, CACHE, KV_HEADS * HEAD_DIM), 3.0, 18.0, ((0, 8), (2, 4)))
    key_prefix = draw_key_prefix(jax.random.fold_in(streams_of[21], 71), 0)
    value_prefix = centred(streams_of[7], (N_REQ, PREFIX, KV_HEADS * HEAD_DIM), 3.0, 18.0, ((0, 8), (2, 4)))
    attn_gain = jnp.clip(1.0 + 0.15 * jax.random.normal(streams_of[8], (D,), jnp.float32), 0.25, 1.75)
    q_proj = centred(streams_of[9], (D, HEADS * HEAD_DIM), D ** -0.5, 0.125, ((1, 4),))
    k_proj = centred(streams_of[10], (D, KV_HEADS * HEAD_DIM), D ** -0.5, 0.125, ((1, 4),))
    v_proj = centred(streams_of[11], (D, KV_HEADS * HEAD_DIM), D ** -0.5, 0.125, ((1, 4),))
    q_gain = jnp.clip(1.0 + 0.15 * jax.random.normal(streams_of[12], (HEAD_DIM,), jnp.float32), 0.25, 1.75)
    k_gain = jnp.clip(1.0 + 0.15 * jax.random.normal(streams_of[13], (HEAD_DIM,), jnp.float32), 0.25, 1.75)
    o_proj = centred(streams_of[14], (HEADS * HEAD_DIM, D), (HEADS * HEAD_DIM) ** -0.5, 0.125, ((0, 4),))
    ffn_gain = jnp.clip(1.0 + 0.15 * jax.random.normal(streams_of[15], (D,), jnp.float32), 0.25, 1.75)
    w_gate = centred(streams_of[16], (D, FF), D ** -0.5, 0.125, ((1, 8),))
    w_up = centred(streams_of[17], (D, FF), D ** -0.5, 0.125, ((1, 8),))
    w_down = centred(streams_of[18], (FF, D), FF ** -0.5, 0.078125, ((0, 8),))
    final_gain = jnp.clip(1.0 + 0.15 * jax.random.normal(streams_of[19], (D,), jnp.float32), 0.25, 1.75)
    lm_head = centred(streams_of[20], (D, VOCAB), (D // 9) ** -0.5, 0.375, ((1, 32),))
    return {"hidden_in": hidden_in, "slot_tokens": slot_tokens, "cache_len": cache_len, "prefill_start": prefill_start, "key_cache": key_cache, "value_cache": value_cache, "key_prefix": key_prefix, "value_prefix": value_prefix, "attn_gain": attn_gain, "q_proj": q_proj, "k_proj": k_proj, "v_proj": v_proj, "q_gain": q_gain, "k_gain": k_gain, "o_proj": o_proj, "ffn_gain": ffn_gain, "w_gate": w_gate, "w_up": w_up, "w_down": w_down, "final_gain": final_gain, "lm_head": lm_head}


EPS = 1e-06
NEG = -1e+30

def norm_rows(values, gain_vec):
    wide = values.astype(jnp.float32)
    return wide * lax.rsqrt(lax.optimization_barrier(jnp.mean(wide * wide, axis=-1, keepdims=True)) + EPS) * gain_vec

def rotate(values, places):
    half_dim = values.shape[-1] // 2
    freqs = 1000000.0 ** (-(jnp.arange(half_dim, dtype=jnp.float32) * 2.0 / values.shape[-1]))
    angles = places[:, None] * freqs[None, :]
    cosine = jnp.cos(angles)[:, None, :]
    sine = jnp.sin(angles)[:, None, :]
    first_half = values[..., :half_dim]
    second_half = values[..., half_dim:]
    return jnp.concatenate([first_half * cosine - second_half * sine, second_half * cosine + first_half * sine], axis=-1)

def prefill_attend(q_heads, key_old, value_old, key_new, value_new, start_at):
    old_len = key_old.shape[0]
    fresh_rows = q_heads.shape[0]
    factor = q_heads.shape[-1] ** (-0.5)
    all_keys = jnp.concatenate([key_old, key_new], axis=0).astype(jnp.float32)
    all_values = jnp.concatenate([value_old, value_new], axis=0).astype(jnp.float32)
    scores = jnp.einsum('cgd,kd->gck', q_heads.astype(jnp.float32), all_keys) * factor
    key_index = jnp.arange(old_len + fresh_rows, dtype=jnp.int32)[None, :]
    row_index = jnp.arange(fresh_rows, dtype=jnp.int32)[:, None]
    allowed = jnp.where(key_index < old_len, key_index < start_at, key_index - old_len <= row_index)
    scores = jnp.where(allowed[None], scores, NEG)
    row_peak = lax.optimization_barrier(jnp.max(scores, axis=-1, keepdims=True))
    expd = jnp.exp(scores - row_peak)
    weights = (expd / lax.optimization_barrier(jnp.sum(expd, axis=-1, keepdims=True))).astype(jnp.bfloat16)
    return jnp.einsum('gck,kd->cgd', weights.astype(jnp.float32), all_values).astype(jnp.bfloat16)

def decode_attend(q_heads, key_old, value_old, key_self, value_self, lengths):
    factor = q_heads.shape[-1] ** (-0.5)
    past = jnp.einsum('bgd,bld->bgl', q_heads.astype(jnp.float32), key_old.astype(jnp.float32)) * factor
    slot_index = jnp.arange(key_old.shape[1], dtype=jnp.int32)
    past = jnp.where(slot_index[None, None, :] < lengths[:, None, None], past, NEG)
    own_score = jnp.einsum('bgd,bd->bg', q_heads.astype(jnp.float32), key_self.astype(jnp.float32)) * factor
    row_peak = jnp.maximum(lax.optimization_barrier(jnp.max(past, axis=-1)), own_score)
    past_exp = jnp.exp(past - row_peak[..., None])
    own_exp = jnp.exp(own_score - row_peak)
    row_total = lax.optimization_barrier(jnp.sum(past_exp, axis=-1)) + own_exp
    past_w = (past_exp / row_total[..., None]).astype(jnp.bfloat16)
    own_w = (own_exp / row_total).astype(jnp.bfloat16)
    summed = jnp.einsum('bgl,bld->bgd', past_w.astype(jnp.float32), value_old.astype(jnp.float32))
    summed = summed + own_w.astype(jnp.float32)[..., None] * value_self.astype(jnp.float32)[:, None, :]
    return summed.astype(jnp.bfloat16)

def reference(hidden_in, slot_tokens, cache_len, prefill_start, key_cache, value_cache, key_prefix, value_prefix, attn_gain, q_proj, k_proj, v_proj, q_gain, k_gain, o_proj, ffn_gain, w_gate, w_up, w_down, final_gain, lm_head):
    owner_rows = hidden_in[slot_tokens]
    normed = norm_rows(owner_rows, attn_gain).astype(jnp.bfloat16)
    q_raw = jnp.dot(normed, q_proj, preferred_element_type=jnp.float32).reshape(TOKENS, HEADS, HEAD_DIM)
    k_raw = jnp.dot(normed, k_proj, preferred_element_type=jnp.float32).reshape(TOKENS, KV_HEADS, HEAD_DIM)
    v_new = jnp.dot(normed, v_proj, preferred_element_type=jnp.float32).astype(jnp.bfloat16).reshape(N_REQ, TOK_REQ, KV_HEADS, HEAD_DIM)
    fresh_pos = prefill_start[:, None] + jnp.arange(PREFILL_TOK, dtype=jnp.int32)[None, :]
    places = jnp.concatenate([fresh_pos, cache_len.reshape(N_REQ, DEC_DEV)], axis=1).astype(jnp.float32).reshape(TOKENS)
    queries = rotate(norm_rows(q_raw, q_gain), places).astype(jnp.bfloat16).reshape(N_REQ, TOK_REQ, HEADS, HEAD_DIM)
    keys_new = rotate(norm_rows(k_raw, k_gain), places).astype(jnp.bfloat16).reshape(N_REQ, TOK_REQ, KV_HEADS, HEAD_DIM)
    group_size = HEADS // KV_HEADS
    dec_keys = key_cache.reshape(N_REQ, DEC_DEV, CACHE, KV_HEADS * HEAD_DIM)
    dec_values = value_cache.reshape(N_REQ, DEC_DEV, CACHE, KV_HEADS * HEAD_DIM)
    dec_lengths = cache_len.reshape(N_REQ, DEC_DEV)

    def one_owner(inputs):
        q_own, k_own, v_own, key_dec, value_dec, key_pre, value_pre, lengths, start_at = inputs
        pieces = []
        for head_id in range(KV_HEADS):
            cols = slice(head_id * HEAD_DIM, (head_id + 1) * HEAD_DIM)
            q_group = q_own[:, head_id * group_size:(head_id + 1) * group_size]
            pre_out = prefill_attend(q_group[:PREFILL_TOK], key_pre[:, cols], value_pre[:, cols], k_own[:PREFILL_TOK, head_id], v_own[:PREFILL_TOK, head_id], start_at)
            dec_out = decode_attend(q_group[PREFILL_TOK:], key_dec[:, :, cols], value_dec[:, :, cols], k_own[PREFILL_TOK:, head_id], v_own[PREFILL_TOK:, head_id], lengths)
            pieces.append(jnp.concatenate([pre_out, dec_out], axis=0))
        return jnp.concatenate(pieces, axis=1).reshape(TOK_REQ, HEADS * HEAD_DIM)
    attended = lax.map(one_owner, (queries, keys_new, v_new, dec_keys, dec_values, key_prefix, value_prefix, dec_lengths, prefill_start))
    attended = attended.reshape(TOKENS, HEADS * HEAD_DIM)
    resid = (owner_rows.astype(jnp.float32) + jnp.dot(attended, o_proj, preferred_element_type=jnp.float32)).astype(jnp.bfloat16)
    ffn_in = norm_rows(resid, ffn_gain).astype(jnp.bfloat16)

    def ffn_block(rows_block):
        gate_part = jnp.dot(rows_block, w_gate, preferred_element_type=jnp.float32)
        up_part = jnp.dot(rows_block, w_up, preferred_element_type=jnp.float32)
        hidden_act = (jax.nn.silu(gate_part) * up_part).astype(jnp.bfloat16)
        return jnp.dot(hidden_act, w_down, preferred_element_type=jnp.float32)
    ffn_part = lax.map(ffn_block, ffn_in.reshape(N_REQ, TOK_REQ, D)).reshape(TOKENS, D)
    out_rows = (resid.astype(jnp.float32) + ffn_part).astype(jnp.bfloat16)
    layer_out = jnp.zeros_like(hidden_in).at[slot_tokens].set(out_rows)
    tail_rows = out_rows.reshape(N_REQ, TOK_REQ, D)[:, PREFILL_TOK - 1:].reshape(LOGIT_ROWS, D)
    tail_rows = norm_rows(tail_rows, final_gain).astype(jnp.bfloat16)
    logits = jnp.dot(tail_rows, lm_head, preferred_element_type=jnp.float32)
    max_logit = lax.optimization_barrier(jnp.max(logits, axis=1))
    return (layer_out, max_logit)
```

```python
import jax
import jax.numpy as jnp
from jax import lax
from jax.sharding import PartitionSpec as P

EPS = 1e-06
NEG = -1e30
GROUP = 4


def swap(value, axis, bit):
    size = lax.axis_size(axis)
    return lax.ppermute(value, axis, [(i, i ^ bit) for i in range(size)])


def bits_below(size):
    return [1 << i for i in range(size.bit_length() - 1)]


def gather_xor(value, axis, bits):
    held = {0: value}
    for bit in bits:
        held.update({diff ^ bit: swap(block, axis, bit) for diff, block in list(held.items())})
    return held


def zero_after(value):
    first = value[(0,) * value.ndim]
    return (first != first).astype(jnp.int32)


def norm_rows(values, gain_vec):
    wide = values.astype(jnp.float32)
    return wide * lax.rsqrt(jnp.mean(wide * wide, axis=-1, keepdims=True) + EPS) * gain_vec


def angle_tables(places, head_dim):
    half_dim = head_dim // 2
    freqs = 1000000.0 ** (-(jnp.arange(half_dim, dtype=jnp.float32) * 2.0 / head_dim))
    angles = places[:, None] * freqs[None, :]
    return jnp.cos(angles), jnp.sin(angles)


def rotate(values, cosine, sine):
    half_dim = values.shape[-1] // 2
    cosine, sine = cosine[:, None, :], sine[:, None, :]
    first_half = values[..., :half_dim]
    second_half = values[..., half_dim:]
    return jnp.concatenate(
        [first_half * cosine - second_half * sine, second_half * cosine + first_half * sine],
        axis=-1,
    )


def prefill_full(q_heads, key_old, value_old, key_new, value_new, start_at, order):
    old_len = key_old.shape[0]
    fresh_rows = q_heads.shape[0]
    factor = q_heads.shape[-1] ** (-0.5)
    all_keys = jnp.concatenate([key_old, key_new], axis=0)
    all_values = jnp.concatenate([value_old, value_new], axis=0)
    scores = (
        jnp.einsum("cgd,kd->gck", q_heads, all_keys, preferred_element_type=jnp.float32) * factor
    )
    key_index = jnp.arange(old_len + fresh_rows, dtype=jnp.int32)[None, :]
    key_order = jnp.concatenate([jnp.zeros((old_len,), jnp.int32), order])[None, :]
    allowed = jnp.where(key_index < old_len, key_index < start_at, key_order <= order[:, None])
    scores = jnp.where(allowed[None], scores, NEG)
    row_peak = jnp.max(scores, axis=-1, keepdims=True)
    expd = jnp.exp(scores - row_peak)
    weights = (expd / jnp.sum(expd, axis=-1, keepdims=True)).astype(jnp.bfloat16)
    return jnp.einsum(
        "gck,kd->cgd", weights, all_values, preferred_element_type=jnp.float32
    ).astype(jnp.bfloat16)


def decode_attend(q_heads, key_old, value_old, key_self, value_self, lengths):
    factor = q_heads.shape[-1] ** (-0.5)
    past = jnp.einsum("bgd,bld->bgl", q_heads, key_old, preferred_element_type=jnp.float32) * factor
    slot_index = jnp.arange(key_old.shape[1], dtype=jnp.int32)
    past = jnp.where(slot_index[None, None, :] < lengths[:, None, None], past, NEG)
    own_score = (
        jnp.einsum("bgd,bd->bg", q_heads, key_self, preferred_element_type=jnp.float32) * factor
    )
    row_peak = jnp.maximum(jnp.max(past, axis=-1), own_score)
    past_exp = jnp.exp(past - row_peak[..., None])
    own_exp = jnp.exp(own_score - row_peak)
    row_total = jnp.sum(past_exp, axis=-1) + own_exp
    past_w = (past_exp / row_total[..., None]).astype(jnp.bfloat16)
    own_w = (own_exp / row_total).astype(jnp.bfloat16)
    summed = jnp.einsum("bgl,bld->bgd", past_w, value_old, preferred_element_type=jnp.float32)
    summed = (
        summed + own_w.astype(jnp.float32)[..., None] * value_self.astype(jnp.float32)[:, None, :]
    )
    return summed.astype(jnp.bfloat16)


def regroup(rows_in):
    return lax.all_to_all(rows_in, ("req", "kv"), split_axis=0, concat_axis=0, tiled=True)


def matmul(left, right):
    return jnp.dot(left, right, preferred_element_type=jnp.float32)


def routes(slot_tokens, self_index, devices, rows_dev):
    per_pair = rows_dev // devices
    slot_table = slot_tokens.reshape(devices, rows_dev)
    source = slot_table // rows_dev
    places = jnp.arange(rows_dev, dtype=jnp.int32)
    before = (places[:, None] < places[None, :]).astype(jnp.bfloat16)
    from_self = source == self_index
    rank = matmul(from_self.astype(jnp.bfloat16), before).astype(jnp.int32)
    local = slot_table - self_index * rows_dev
    ranked = jnp.where(from_self, rank, -1)[:, None, :] == jnp.arange(per_pair, dtype=jnp.int32)[None, :, None]
    send_rows = jnp.sum(jnp.where(ranked, local[:, None, :], 0), axis=2).reshape(-1)
    send_hot = (send_rows[:, None] == places[None, :]).astype(jnp.bfloat16)
    own = lax.dynamic_index_in_dim(source, self_index, 0, keepdims=False)
    earlier = (own[:, None] == own[None, :]) & (places[:, None] > places[None, :])
    own_rank = jnp.sum(earlier.astype(jnp.int32), axis=1)
    slot_hot = ((own * per_pair + own_rank)[:, None] == places[None, :]).astype(jnp.bfloat16)
    return send_hot, slot_hot


def pick(hot, rows, transposed=False):
    if transposed:
        return lax.dot_general(
            hot, rows, (((0,), (0,)), ((), ())), preferred_element_type=jnp.float32
        ).astype(rows.dtype)
    return matmul(hot, rows).astype(rows.dtype)


def feed_forward(rows, weights):
    total = None
    for w_gate, w_up, w_down in weights:
        gate = matmul(rows, w_gate)
        up = matmul(rows, w_up)
        hidden_act = (jax.nn.silu(gate) * up).astype(jnp.bfloat16)
        part = matmul(hidden_act, w_down)
        total = part if total is None else total + part
    return total


def shards(
    hidden_in,
    slot_tokens,
    cache_len,
    prefill_start,
    key_cache,
    value_cache,
    key_prefix,
    value_prefix,
    attn_gain,
    q_proj,
    k_proj,
    v_proj,
    q_gain,
    k_gain,
    o_proj,
    ffn_gain,
    w_gate,
    w_up,
    w_down,
    final_gain,
    lm_head,
):
    req_count = lax.axis_size("req")
    kv_count = lax.axis_size("kv")
    devices = req_count * kv_count
    rows_dev, width = hidden_in.shape
    kv_index = lax.axis_index("kv")
    self_index = lax.axis_index("req") * kv_count + kv_index
    kv_bits = bits_below(kv_count)
    near_bits = [bit for bit in bits_below(req_count) if bit < GROUP]
    far_bits = [bit for bit in bits_below(req_count) if bit >= GROUP]

    send_hot, slot_hot = routes(slot_tokens, self_index, devices, rows_dev)
    arrived = regroup(pick(send_hot, hidden_in))
    owner_rows = pick(slot_hot, arrived)

    turn = kv_index + zero_after(arrived)
    share = width // kv_count
    down_share = w_down.shape[0] // kv_count
    gate_up_share = jnp.concatenate(
        [
            lax.dynamic_slice_in_dim(w_gate, turn * share, share, 0),
            lax.dynamic_slice_in_dim(w_up, turn * share, share, 0),
        ],
        axis=1,
    )
    down_part = lax.dynamic_slice_in_dim(w_down, turn * down_share, down_share, 0)
    far_gate_up = gather_xor(gate_up_share, "req", far_bits)
    far_down = gather_xor(down_part, "req", far_bits)

    blocks = gather_xor(owner_rows, "kv", kv_bits[::-1])
    head_dim = q_gain.shape[0]
    dec_count = cache_len.shape[0]
    tok_req = rows_dev * kv_count
    fresh_count = tok_req - dec_count
    q_cols = q_proj.shape[1]
    kv_cols = k_proj.shape[1]
    places = jnp.concatenate(
        [prefill_start[0] + jnp.arange(fresh_count, dtype=jnp.int32), cache_len]
    ).astype(jnp.float32)
    cosines, sines = angle_tables(places, head_dim)
    q_blocks, k_blocks, v_blocks, orders = [], [], [], []
    for diff in range(kv_count):
        block_at = (kv_index ^ diff) * rows_dev
        cosine = lax.dynamic_slice_in_dim(cosines, block_at, rows_dev, 0)
        sine = lax.dynamic_slice_in_dim(sines, block_at, rows_dev, 0)
        normed = norm_rows(blocks[diff], attn_gain).astype(jnp.bfloat16)
        q_raw = matmul(normed, q_proj).reshape(rows_dev, q_cols // head_dim, head_dim)
        k_raw = matmul(normed, k_proj).reshape(rows_dev, kv_cols // head_dim, head_dim)
        v_blocks.append(
            matmul(normed, v_proj)
            .astype(jnp.bfloat16)
            .reshape(rows_dev, kv_cols // head_dim, head_dim)
        )
        q_blocks.append(rotate(norm_rows(q_raw, q_gain), cosine, sine).astype(jnp.bfloat16))
        k_blocks.append(rotate(norm_rows(k_raw, k_gain), cosine, sine).astype(jnp.bfloat16))
        orders.append(block_at + jnp.arange(rows_dev, dtype=jnp.int32))
    queries = jnp.concatenate(q_blocks, axis=0)
    keys_new = jnp.concatenate(k_blocks, axis=0)
    v_new = jnp.concatenate(v_blocks, axis=0)
    order = jnp.concatenate(orders)

    o_whole = lax.all_gather(
        lax.dynamic_slice_in_dim(o_proj, zero_after(blocks[kv_count - 1]), o_proj.shape[0], 0),
        "kv",
        axis=0,
        tiled=True,
    )
    ffn_weights = [(w_gate, w_up, w_down)]
    for diff in far_gate_up:
        if diff:
            whole = lax.all_gather(far_gate_up[diff], "kv", axis=0, tiled=True)
            cut = w_gate.shape[1]
            ffn_weights.append(
                (
                    whole[:, :cut],
                    whole[:, cut:],
                    lax.all_gather(far_down[diff], "kv", axis=0, tiled=True),
                )
            )

    kv_local = kv_cols // head_dim
    group_size = q_cols // head_dim // kv_local
    last_block = (kv_index ^ (kv_count - 1)) * rows_dev
    dec_at = last_block + rows_dev - dec_count
    pieces = []
    for head_id in range(kv_local):
        col_lo = head_id * head_dim
        col_hi = col_lo + head_dim
        q_group = queries[:, head_id * group_size : (head_id + 1) * group_size]
        pre_out = prefill_full(
            q_group,
            key_prefix[0, :, col_lo:col_hi],
            value_prefix[0, :, col_lo:col_hi],
            keys_new[:, head_id],
            v_new[:, head_id],
            prefill_start[0],
            order,
        )
        dec_out = decode_attend(
            lax.dynamic_slice_in_dim(q_group, dec_at, dec_count, 0),
            key_cache[:, :, col_lo:col_hi],
            value_cache[:, :, col_lo:col_hi],
            lax.dynamic_slice_in_dim(keys_new[:, head_id], dec_at, dec_count, 0),
            lax.dynamic_slice_in_dim(v_new[:, head_id], dec_at, dec_count, 0),
            cache_len,
        )
        pieces.append(lax.dynamic_update_slice_in_dim(pre_out, dec_out, dec_at, 0))
    attended = jnp.concatenate(pieces, axis=1).reshape(tok_req, q_cols)

    own_heads = jnp.zeros((rows_dev, q_cols * kv_count), jnp.bfloat16)
    for diff in range(kv_count):
        block = attended[diff * rows_dev : (diff + 1) * rows_dev]
        if diff:
            block = swap(block, "kv", diff)
        own_heads = lax.dynamic_update_slice_in_dim(own_heads, block, (kv_index ^ diff) * q_cols, 1)
    resid = (owner_rows.astype(jnp.float32) + matmul(own_heads, o_whole)).astype(jnp.bfloat16)
    ffn_in = norm_rows(resid, ffn_gain).astype(jnp.bfloat16)

    tail_count = dec_count + 1
    tail_raw = jnp.zeros((tail_count, width), jnp.bfloat16)
    for diff in range(kv_count):
        is_last = (kv_index ^ diff) == kv_count - 1
        tail_raw = jnp.where(is_last, blocks[diff][rows_dev - tail_count :], tail_raw)
    tail_share = jnp.concatenate(
        [
            lax.dynamic_slice_in_dim(attended, dec_at - 1, tail_count, 0),
            lax.dynamic_slice_in_dim(tail_raw, kv_index * share, share, 1),
        ],
        axis=1,
    )
    tails = lax.all_gather(tail_share, ("req", "kv"), axis=0, tiled=True).reshape(
        req_count, kv_count, tail_count, -1
    )
    tails = tails.transpose(0, 2, 1, 3)
    score_rows = req_count * tail_count
    tail_heads = tails[..., :q_cols].reshape(score_rows, -1)
    tail_rows = tails[..., q_cols:].reshape(score_rows, -1)
    tail_resid = (tail_rows.astype(jnp.float32) + matmul(tail_heads, o_whole)).astype(jnp.bfloat16)
    tail_in = norm_rows(tail_resid, ffn_gain).astype(jnp.bfloat16)
    tail_part = feed_forward(tail_in, ffn_weights)
    tail_sent = tail_part.astype(jnp.bfloat16)
    for diff in range(1, GROUP):
        tail_part = tail_part + swap(tail_sent, "req", diff).astype(jnp.float32)
    tail_out = (tail_resid.astype(jnp.float32) + tail_part).astype(jnp.bfloat16)
    tail_normed = norm_rows(tail_out, final_gain).astype(jnp.bfloat16)
    peaks = jnp.max(matmul(tail_normed, lm_head), axis=1)[None, :]
    for axis, bits in (("kv", kv_bits), ("req", bits_below(req_count))):
        for bit in bits:
            peaks = jnp.maximum(peaks, swap(peaks, axis, bit))

    near = gather_xor(ffn_in, "req", near_bits)
    ffn_part = feed_forward(near[0], ffn_weights)
    for diff in range(1, GROUP):
        part = feed_forward(near[diff], ffn_weights).astype(jnp.bfloat16)
        ffn_part = ffn_part + swap(part, "req", diff).astype(jnp.float32)
    out_rows = (resid.astype(jnp.float32) + ffn_part).astype(jnp.bfloat16)
    returned = regroup(pick(slot_hot, out_rows, transposed=True))
    layer_out = pick(send_hot, returned, transposed=True)
    return (layer_out, peaks[0])


def solution(mesh):
    placed = (
        P(("req", "kv"), None),
        P(),
        P("req"),
        P("req"),
        P("req", None, "kv"),
        P("req", None, "kv"),
        P("req", None, "kv"),
        P("req", None, "kv"),
        P(),
        P(None, "kv"),
        P(None, "kv"),
        P(None, "kv"),
        P(),
        P(),
        P("kv", None),
        P(),
        P(None, "req"),
        P(None, "req"),
        P("req", None),
        P(),
        P(None, ("req", "kv")),
    )
    return jax.shard_map(
        shards, mesh=mesh, in_specs=placed, out_specs=(P(("req", "kv"), None), P()), check_vma=False
    )
```

```python
import functools
import math

import jax
import jax.numpy as jnp
from jax import lax
from jax.experimental import pallas as pl
from jax.experimental.pallas import tpu as pltpu
from jax.sharding import PartitionSpec as P

EPS = 1e-06
NEG = -1e30
GROUP = 4
TAIL = 16
KEY_BLOCK = 512
VMEM_LIMIT = 56 * 1024 * 1024


def swap(value, axis, bit):
    size = lax.axis_size(axis)
    return lax.ppermute(value, axis, [(i, i ^ bit) for i in range(size)])


def bits_below(size):
    return [1 << i for i in range(size.bit_length() - 1)]


def gather_xor(value, axis, bits):
    held = {0: value}
    for bit in bits:
        held.update({diff ^ bit: swap(block, axis, bit) for diff, block in list(held.items())})
    return held


def after(value, *others):
    return lax.optimization_barrier((value, *others))[0]


def zero_after(value):
    first = value[(0,) * value.ndim]
    return (first != first).astype(jnp.int32)


def norm_rows(values, gain_vec):
    wide = values.astype(jnp.float32)
    return wide * lax.rsqrt(jnp.mean(wide * wide, axis=-1, keepdims=True) + EPS) * gain_vec


def angle_tables(places, head_dim):
    half_dim = head_dim // 2
    freqs = 1000000.0 ** (-(jnp.arange(half_dim, dtype=jnp.float32) * 2.0 / head_dim))
    angles = places[:, None] * freqs[None, :]
    return jnp.cos(angles), jnp.sin(angles)


def contract_last(left, right):
    return lax.dot_general(left, right, (((1,), (1,)), ((), ())), preferred_element_type=jnp.float32)


def whole_spec(shape):
    return pl.BlockSpec(shape, lambda *_: (0,) * len(shape))


def project_kernel(block_count, head_dim, *refs):
    row_refs = refs[:block_count]
    (gain_ref, cos_ref, sin_ref, q_gain_ref, k_gain_ref, wq_hbm, wk_hbm, wv_hbm) = refs[
        block_count : block_count + 8
    ]
    q_ref, k_ref, v_ref, wq, wk, wv, sems = refs[-7:]
    copies = [
        pltpu.make_async_copy(hbm, vmem, sems.at[at])
        for at, (hbm, vmem) in enumerate(((wq_hbm, wq), (wk_hbm, wk), (wv_hbm, wv)))
    ]
    for copy in copies:
        copy.start()
    normed = []
    for ref in row_refs:
        wide = ref[...].astype(jnp.float32)
        scale = lax.rsqrt(jnp.mean(wide * wide, axis=-1, keepdims=True) + EPS)
        normed.append((wide * scale * gain_ref[...]).astype(jnp.bfloat16))
    rows = jnp.concatenate(normed, axis=0)
    cosine, sine = cos_ref[...], sin_ref[...]

    def heads(raw, gain, out_ref):
        for at in range(raw.shape[1] // head_dim):
            head = raw[:, at * head_dim : (at + 1) * head_dim]
            scale = lax.rsqrt(jnp.mean(head * head, axis=-1, keepdims=True) + EPS)
            head = head * scale * gain
            turned = head * cosine + pltpu.roll(head, head_dim // 2, 1) * sine
            out_ref[:, at * head_dim : (at + 1) * head_dim] = turned.astype(jnp.bfloat16)

    copies[0].wait()
    heads(matmul(rows, wq[...]), q_gain_ref[...], q_ref)
    copies[1].wait()
    heads(matmul(rows, wk[...]), k_gain_ref[...], k_ref)
    copies[2].wait()
    v_ref[...] = matmul(rows, wv[...]).astype(jnp.bfloat16)


def project(blocks, gain, cosine, sine, q_gain, k_gain, q_proj, k_proj, v_proj):
    head_dim = q_gain.shape[0]
    rows = sum(block.shape[0] for block in blocks)
    width = q_proj.shape[0]
    outs = (q_proj.shape[1], k_proj.shape[1], v_proj.shape[1])
    vectors = (gain[None, :], cosine, sine, q_gain[None, :], k_gain[None, :])
    return pl.pallas_call(
        functools.partial(project_kernel, len(blocks), head_dim),
        out_shape=[jax.ShapeDtypeStruct((rows, cols), jnp.bfloat16) for cols in outs],
        in_specs=[whole_spec(block.shape) for block in blocks]
        + [whole_spec(vector.shape) for vector in vectors]
        + [pl.BlockSpec(memory_space=pl.ANY)] * 3,
        out_specs=[whole_spec((rows, cols)) for cols in outs],
        grid=(1,),
        scratch_shapes=[pltpu.VMEM((width, cols), jnp.bfloat16) for cols in outs]
        + [pltpu.SemaphoreType.DMA((3,))],
        compiler_params=pltpu.CompilerParams(vmem_limit_bytes=VMEM_LIMIT),
        cost_estimate=pl.CostEstimate(
            flops=2 * rows * width * sum(outs),
            bytes_accessed=2 * width * (rows + sum(outs)) + 2 * rows * sum(outs),
            transcendentals=0,
        ),
    )(*blocks, *vectors, q_proj, k_proj, v_proj)


def attend_kernel(
    block_count,
    head_dim,
    lens_ref,
    q_refs,
    k_refs,
    v_refs,
    kp_ref,
    vp_ref,
    kc_hbm,
    vc_hbm,
    out_ref,
    q_all,
    k_all,
    v_all,
    peak,
    acc,
    kc,
    vc,
    dec_q,
    dec_out,
    sems,
):
    step = pl.program_id(0)
    steps = pl.num_programs(0)
    kv_index, start = lens_ref[0], lens_ref[1]
    dec_count, slots, kv_cols = kc.shape
    kv_heads = kv_cols // head_dim
    tok_req, q_cols = q_all.shape
    group = q_cols // kv_cols
    rows = tok_req // block_count
    scale = head_dim**-0.5 * math.log2(math.e)
    sizes = (slots // 4, slots // 2, slots)

    def by_size(request, act):
        length = lens_ref[2 + request]
        for at, size in enumerate(sizes):
            fits = length <= size
            if at:
                fits = fits & (length > sizes[at - 1])
            pl.when(fits)(functools.partial(act, request, size))

    def cache_copies(request, size):
        return (
            pltpu.make_async_copy(
                kc_hbm.at[request, pl.ds(0, size)], kc.at[request, pl.ds(0, size)], sems.at[0, request]
            ),
            pltpu.make_async_copy(
                vc_hbm.at[request, pl.ds(0, size)], vc.at[request, pl.ds(0, size)], sems.at[1, request]
            ),
        )

    def start_copies(request, size):
        for copy in cache_copies(request, size):
            copy.start()

    @pl.when(step == 0)
    def _():
        def one(request, carry):
            by_size(request, start_copies)
            return carry

        lax.fori_loop(0, dec_count, one, 0)
        for refs, whole in ((q_refs, q_all), (k_refs, k_all), (v_refs, v_all)):
            at = 0
            for ref in refs:
                whole[at : at + ref.shape[0], :] = ref[...]
                at += ref.shape[0]

    row_at = pl.multiple_of(step * rows, rows)
    mine = kv_index ^ step
    row_ids = lax.broadcasted_iota(jnp.int32, (rows, rows), 0)
    col_ids = lax.broadcasted_iota(jnp.int32, (rows, rows), 1)

    for head in range(kv_heads):
        lanes = slice(head * head_dim, (head + 1) * head_dim)
        queries = [
            q_all[pl.ds(row_at, rows), (head * group + g) * head_dim : (head * group + g + 1) * head_dim]
            for g in range(group)
        ]
        peak[...] = jnp.full(peak.shape, NEG, jnp.float32)
        acc[...] = jnp.zeros(acc.shape, jnp.float32)

        def absorb(keys, values, allowed):
            wide = jnp.concatenate([values, jnp.ones_like(values)], axis=1)
            for g in range(group):
                scores = contract_last(queries[g], keys)
                if allowed is not None:
                    scores = jnp.where(allowed, scores, NEG)
                old = peak[g][:, :1]
                new = jnp.maximum(old, jnp.max(scores, axis=1, keepdims=True))
                weights = jnp.exp2((scores - new) * scale).astype(jnp.bfloat16)
                acc[g] = acc[g] * jnp.exp2((old - new) * scale) + matmul(weights, wide)
                peak[g] = jnp.broadcast_to(new, peak.shape[1:])

        full = start // KEY_BLOCK

        def prefix_block(at, carry):
            place = pl.multiple_of(at * KEY_BLOCK, KEY_BLOCK)
            absorb(kp_ref[pl.ds(place, KEY_BLOCK), lanes], vp_ref[pl.ds(place, KEY_BLOCK), lanes], None)
            return carry

        lax.fori_loop(0, full, prefix_block, 0)

        @pl.when(full * KEY_BLOCK < start)
        def _():
            place = pl.multiple_of(full * KEY_BLOCK, KEY_BLOCK)
            ids = lax.broadcasted_iota(jnp.int32, (rows, KEY_BLOCK), 1)
            absorb(
                kp_ref[pl.ds(place, KEY_BLOCK), lanes],
                vp_ref[pl.ds(place, KEY_BLOCK), lanes],
                ids < start - place,
            )

        def fresh_block(at, carry):
            @pl.when((kv_index ^ at) < mine)
            def _():
                place = pl.multiple_of(at * rows, rows)
                absorb(k_all[pl.ds(place, rows), lanes], v_all[pl.ds(place, rows), lanes], None)

            return carry

        lax.fori_loop(0, block_count, fresh_block, 0)
        absorb(
            k_all[pl.ds(row_at, rows), lanes], v_all[pl.ds(row_at, rows), lanes], col_ids <= row_ids
        )
        for g in range(group):
            at = (head * group + g) * head_dim
            out_ref[pl.ds(row_at, rows), at : at + head_dim] = (
                acc[g][:, :head_dim] / acc[g][:, head_dim:]
            ).astype(jnp.bfloat16)

    @pl.when(step == steps - 1)
    def _():
        last = (kv_index ^ (block_count - 1)) * rows
        tail = pl.ds(pl.multiple_of(last + rows - 16, 16), 16)
        q_dec = q_all[tail, :][16 - dec_count :].astype(jnp.float32)
        k_dec = k_all[tail, :][16 - dec_count :].astype(jnp.float32)
        v_dec = v_all[tail, :][16 - dec_count :].astype(jnp.float32)
        for request in range(dec_count):
            at = slice(request, request + 1)
            dec_q[request] = jnp.concatenate([q_dec[at], k_dec[at], v_dec[at]], axis=1)

        def attend_one(request, size):
            for copy in cache_copies(request, size):
                copy.wait()
            row = dec_q[request]
            empty = jnp.zeros((1, head_dim), jnp.float32)
            spread = []
            for at in range(q_cols // head_dim):
                parts = [empty] * kv_heads
                parts[at // group] = row[:, at * head_dim : (at + 1) * head_dim]
                spread.append(jnp.concatenate(parts, axis=1))
            spread += [jnp.zeros((1, kv_cols), jnp.float32)] * (8 - len(spread))
            q_rows = jnp.concatenate(spread, axis=0)
            key_self = row[:, q_cols : q_cols + kv_cols]
            value_self = row[:, q_cols + kv_cols :]
            past = contract_last(q_rows.astype(jnp.bfloat16), kc[request, :size, :])
            ids = lax.broadcasted_iota(jnp.int32, past.shape, 1)
            past = jnp.where(ids < lens_ref[2 + request], past, NEG)
            own = jnp.sum(q_rows * key_self, axis=1, keepdims=True)
            top = jnp.maximum(jnp.max(past, axis=1, keepdims=True), own)
            past = jnp.exp2((past - top) * scale)
            own = jnp.exp2((own - top) * scale)
            total = jnp.sum(past, axis=1, keepdims=True) + own
            past = (past / total).astype(jnp.bfloat16)
            own = (own / total).astype(jnp.bfloat16).astype(jnp.float32)
            summed = matmul(past, vc[request, :size, :]) + own * value_self
            outs = []
            for at in range(q_cols // head_dim):
                lane = (at // group) * head_dim
                outs.append(summed[at : at + 1, lane : lane + head_dim])
            dec_out[request] = jnp.concatenate(outs, axis=1)

        def one(request, carry):
            by_size(request, attend_one)
            return carry

        lax.fori_loop(0, dec_count, one, 0)
        kept = out_ref[tail, :][: 16 - dec_count]
        done = jnp.concatenate([dec_out[request] for request in range(dec_count)], axis=0)
        out_ref[tail, :] = jnp.concatenate([kept, done.astype(jnp.bfloat16)], axis=0)


def attend(lens, parts, head_dim, key_prefix, value_prefix, key_cache, value_cache):
    count = len(parts)
    block_count = lax.axis_size("kv")
    queries, keys, values = [[part[at] for part in parts] for at in range(3)]
    tok_req = sum(part.shape[0] for part in queries)
    q_cols, kv_cols = queries[0].shape[1], keys[0].shape[1]
    dec_count, slots = key_cache.shape[:2]
    rows = tok_req // block_count
    group = q_cols // kv_cols

    def kernel(lens_ref, *refs):
        cuts = [refs[at * count : (at + 1) * count] for at in range(3)]
        attend_kernel(block_count, head_dim, lens_ref, *cuts, *refs[3 * count :])

    return pl.pallas_call(
        kernel,
        out_shape=jax.ShapeDtypeStruct((tok_req, q_cols), jnp.bfloat16),
        grid_spec=pltpu.PrefetchScalarGridSpec(
            num_scalar_prefetch=1,
            grid=(block_count,),
            in_specs=[whole_spec(part.shape) for part in queries + keys + values]
            + [whole_spec(key_prefix.shape), whole_spec(value_prefix.shape)]
            + [pl.BlockSpec(memory_space=pl.ANY)] * 2,
            out_specs=whole_spec((tok_req, q_cols)),
            scratch_shapes=[
                pltpu.VMEM((tok_req, q_cols), jnp.bfloat16),
                pltpu.VMEM((tok_req, kv_cols), jnp.bfloat16),
                pltpu.VMEM((tok_req, kv_cols), jnp.bfloat16),
                pltpu.VMEM((group, rows, head_dim), jnp.float32),
                pltpu.VMEM((group, rows, 2 * head_dim), jnp.float32),
                pltpu.VMEM((dec_count, slots, kv_cols), jnp.bfloat16),
                pltpu.VMEM((dec_count, slots, kv_cols), jnp.bfloat16),
                pltpu.VMEM((dec_count, 1, q_cols + 2 * kv_cols), jnp.float32),
                pltpu.VMEM((dec_count, 1, q_cols), jnp.float32),
                pltpu.SemaphoreType.DMA((2, dec_count)),
            ],
        ),
        compiler_params=pltpu.CompilerParams(vmem_limit_bytes=VMEM_LIMIT),
        cost_estimate=pl.CostEstimate(
            flops=8 * tok_req * 1024 * q_cols,
            bytes_accessed=8 * slots * kv_cols + 8 * slots * kv_cols,
            transcendentals=tok_req * 1024 * q_cols // head_dim,
        ),
    )(lens, *queries, *keys, *values, key_prefix, value_prefix, key_cache, value_cache)


def join_kernel(count, kv_ref, *refs):
    pieces = refs[:count]
    weight_ref, rows_ref, gain_ref, resid_ref, normed_ref, total = refs[count:]
    step = pl.program_id(0)
    for at in range(count):

        @pl.when(step == at)
        def _():
            part = matmul(pieces[at][...], weight_ref[...])
            total[...] = part if at == 0 else total[...] + part

    @pl.when(step == count - 1)
    def _():
        resid = (rows_ref[...].astype(jnp.float32) + total[...]).astype(jnp.bfloat16)
        resid_ref[...] = resid
        wide = resid.astype(jnp.float32)
        scale = lax.rsqrt(jnp.mean(wide * wide, axis=-1, keepdims=True) + EPS)
        normed_ref[...] = (wide * scale * gain_ref[...]).astype(jnp.bfloat16)


def join_heads(pieces, o_whole, rows, gain, index):
    count = len(pieces)
    size, cols = pieces[0].shape
    shape = rows.shape
    out = jax.ShapeDtypeStruct(shape, jnp.bfloat16)
    return pl.pallas_call(
        functools.partial(join_kernel, count),
        out_shape=[out, out],
        grid_spec=pltpu.PrefetchScalarGridSpec(
            num_scalar_prefetch=1,
            grid=(count,),
            in_specs=[whole_spec(piece.shape) for piece in pieces]
            + [
                pl.BlockSpec((cols, shape[1]), lambda at, index_ref: (index_ref[0] ^ at, 0)),
                whole_spec(shape),
                whole_spec((1, shape[1])),
            ],
            out_specs=[whole_spec(shape), whole_spec(shape)],
            scratch_shapes=[pltpu.VMEM(shape, jnp.float32)],
        ),
        compiler_params=pltpu.CompilerParams(vmem_limit_bytes=VMEM_LIMIT),
        cost_estimate=pl.CostEstimate(
            flops=2 * size * o_whole.size,
            bytes_accessed=2 * o_whole.size + 8 * size * shape[1],
            transcendentals=0,
        ),
    )(index, *pieces, o_whole, rows, gain[None, :])


def feed_kernel(sets, tiles, *refs):
    x_ref = refs[0]
    out_ref, total = refs[-2:]
    step = pl.program_id(0)

    @pl.when(step == 0)
    def _():
        total[...] = jnp.zeros_like(total)

    for at in range(sets):
        gate_ref, up_ref, down_ref = refs[1 + 3 * at : 4 + 3 * at]

        @pl.when(step // tiles == at)
        def _():
            gate = matmul(x_ref[...], gate_ref[...])
            up = matmul(x_ref[...], up_ref[...])
            act = (gate / (1.0 + jnp.exp(-gate)) * up).astype(jnp.bfloat16)
            total[...] += matmul(act, down_ref[...])

    @pl.when(step == sets * tiles - 1)
    def _():
        out_ref[...] = total[...].astype(out_ref.dtype)


def feed_forward(rows, weights, dtype):
    size, width = rows.shape
    hidden = weights[0][3].shape[0]
    tile = 256 if hidden % 256 == 0 else 128
    tiles = hidden // tile
    sets = len(weights)
    specs, operands = [], []
    for at, (gate, up, up_at, down) in enumerate(weights):

        def place(step, at=at):
            return jnp.clip(step - at * tiles, 0, tiles - 1)

        specs += [
            pl.BlockSpec((width, tile), lambda step, place=place: (0, place(step))),
            pl.BlockSpec(
                (width, tile), lambda step, place=place, up_at=up_at: (0, place(step) + up_at // tile)
            ),
            pl.BlockSpec((tile, width), lambda step, place=place: (place(step), 0)),
        ]
        operands += [gate, up, down]
    return pl.pallas_call(
        functools.partial(feed_kernel, sets, tiles),
        out_shape=jax.ShapeDtypeStruct((size, width), dtype),
        grid=(sets * tiles,),
        in_specs=[whole_spec((size, width))] + specs,
        out_specs=whole_spec((size, width)),
        scratch_shapes=[pltpu.VMEM((size, width), jnp.float32)],
        compiler_params=pltpu.CompilerParams(vmem_limit_bytes=VMEM_LIMIT),
        cost_estimate=pl.CostEstimate(
            flops=6 * size * width * hidden * sets,
            bytes_accessed=6 * width * hidden * sets + 4 * size * width,
            transcendentals=size * hidden * sets,
        ),
    )(rows, *operands)


def regroup(rows_in):
    return lax.all_to_all(rows_in, ("req", "kv"), split_axis=0, concat_axis=0, tiled=True)


def matmul(left, right):
    return jnp.dot(left, right, preferred_element_type=jnp.float32)


def routes(slot_tokens, self_index, devices, rows_dev):
    per_pair = rows_dev // devices
    slot_table = slot_tokens.reshape(devices, rows_dev)
    source = slot_table // rows_dev
    places = jnp.arange(rows_dev, dtype=jnp.int32)
    before = (places[:, None] < places[None, :]).astype(jnp.bfloat16)
    from_self = source == self_index
    rank = matmul(from_self.astype(jnp.bfloat16), before).astype(jnp.int32)
    local = slot_table - self_index * rows_dev
    ranked = jnp.where(from_self, rank, -1)[:, None, :] == jnp.arange(per_pair, dtype=jnp.int32)[None, :, None]
    send_rows = jnp.sum(jnp.where(ranked, local[:, None, :], 0), axis=2).reshape(-1)
    send_hot = (send_rows[:, None] == places[None, :]).astype(jnp.bfloat16)
    own = lax.dynamic_index_in_dim(source, self_index, 0, keepdims=False)
    earlier = (own[:, None] == own[None, :]) & (places[:, None] > places[None, :])
    own_rank = jnp.sum(earlier.astype(jnp.int32), axis=1)
    slot_hot = ((own * per_pair + own_rank)[:, None] == places[None, :]).astype(jnp.bfloat16)
    return send_hot, slot_hot


def pick(hot, rows, transposed=False):
    if transposed:
        return lax.dot_general(
            hot, rows, (((0,), (0,)), ((), ())), preferred_element_type=jnp.float32
        ).astype(rows.dtype)
    return matmul(hot, rows).astype(rows.dtype)


def shards(
    hidden_in,
    slot_tokens,
    cache_len,
    prefill_start,
    key_cache,
    value_cache,
    key_prefix,
    value_prefix,
    attn_gain,
    q_proj,
    k_proj,
    v_proj,
    q_gain,
    k_gain,
    o_proj,
    ffn_gain,
    w_gate,
    w_up,
    w_down,
    final_gain,
    lm_head,
):
    req_count = lax.axis_size("req")
    kv_count = lax.axis_size("kv")
    devices = req_count * kv_count
    rows_dev, width = hidden_in.shape
    kv_index = lax.axis_index("kv")
    self_index = lax.axis_index("req") * kv_count + kv_index
    kv_bits = bits_below(kv_count)
    near_bits = [bit for bit in bits_below(req_count) if bit < GROUP]
    far_bits = [bit for bit in bits_below(req_count) if bit >= GROUP]

    send_hot, slot_hot = routes(slot_tokens, self_index, devices, rows_dev)
    arrived = regroup(pick(send_hot, hidden_in))
    owner_rows = pick(slot_hot, arrived)

    turn = kv_index + zero_after(arrived)
    share = width // kv_count
    down_share = w_down.shape[0] // kv_count
    gate_up_share = jnp.concatenate(
        [
            lax.dynamic_slice_in_dim(w_gate, turn * share, share, 0),
            lax.dynamic_slice_in_dim(w_up, turn * share, share, 0),
        ],
        axis=1,
    )
    down_part = lax.dynamic_slice_in_dim(w_down, turn * down_share, down_share, 0)
    far_gate_up = gather_xor(gate_up_share, "req", far_bits)
    far_down = gather_xor(down_part, "req", far_bits)

    blocks = gather_xor(owner_rows, "kv", kv_bits[::-1])
    head_dim = q_gain.shape[0]
    dec_count = cache_len.shape[0]
    tok_req = rows_dev * kv_count
    fresh_count = tok_req - dec_count
    q_cols = q_proj.shape[1]
    kv_cols = k_proj.shape[1]
    places = jnp.concatenate(
        [prefill_start[0] + jnp.arange(fresh_count, dtype=jnp.int32), cache_len]
    ).astype(jnp.float32)
    cosines, sines = angle_tables(places, head_dim)
    cosines = jnp.concatenate([cosines, cosines], axis=1)
    sines = jnp.concatenate([-sines, sines], axis=1)
    parts = []
    for diff in range(0, kv_count, 2):
        tables = [
            jnp.concatenate(
                [
                    lax.dynamic_slice_in_dim(table, (kv_index ^ at) * rows_dev, rows_dev, 0)
                    for at in (diff, diff + 1)
                ],
                axis=0,
            )
            for table in (cosines, sines)
        ]
        parts.append(
            project(
                [blocks[diff], blocks[diff + 1]],
                attn_gain,
                *tables,
                q_gain,
                k_gain,
                q_proj,
                k_proj,
                v_proj,
            )
        )

    o_whole = lax.all_gather(after(o_proj, blocks[kv_count - 1]), "kv", axis=0, tiled=True)
    lens = jnp.concatenate([kv_index[None], prefill_start, cache_len]).astype(jnp.int32)
    attended = attend(
        lens, parts, head_dim, key_prefix[0], value_prefix[0], key_cache, value_cache
    )
    last_at = (kv_index ^ (kv_count - 1)) * rows_dev + rows_dev - TAIL
    last_rows = lax.dynamic_slice_in_dim(attended, last_at, TAIL, 0)
    last_raw = blocks[0][rows_dev - TAIL :]
    pieces = []
    for diff in range(kv_count):
        block = jnp.concatenate([attended[diff * rows_dev : (diff + 1) * rows_dev], last_rows], axis=0)
        pieces.append(swap(block, "kv", diff) if diff else block)
        is_last = (kv_index ^ diff) == kv_count - 1
        last_raw = jnp.where(is_last, blocks[diff][rows_dev - TAIL :], last_raw)
    resid, ffn_in = join_heads(
        pieces, o_whole, jnp.concatenate([owner_rows, last_raw], axis=0), ffn_gain, lens[:1]
    )

    ffn_weights = [(w_gate, w_up, 0, w_down)]
    for diff in far_gate_up:
        if diff:
            whole = lax.all_gather(after(far_gate_up[diff], attended), "kv", axis=0, tiled=True)
            whole_down = lax.all_gather(after(far_down[diff], attended), "kv", axis=0, tiled=True)
            ffn_weights.append((whole, whole, w_gate.shape[1], whole_down))

    near = gather_xor(ffn_in, "req", near_bits)
    ffn_part = feed_forward(near[0], ffn_weights, jnp.float32)
    for diff in range(1, GROUP):
        part = feed_forward(near[diff], ffn_weights, jnp.bfloat16)
        ffn_part = ffn_part + swap(part, "req", diff).astype(jnp.float32)
    out_rows = (resid.astype(jnp.float32) + ffn_part).astype(jnp.bfloat16)
    returned = regroup(pick(slot_hot, out_rows[:rows_dev], transposed=True))
    layer_out = pick(send_hot, returned, transposed=True)

    tail_count = dec_count + 1
    tail_rows = norm_rows(out_rows[rows_dev + TAIL - tail_count :], final_gain).astype(jnp.bfloat16)
    req_bits = bits_below(req_count)
    tails = gather_xor(tail_rows[None], "req", req_bits)
    tails = jnp.concatenate([tails[diff] for diff in range(req_count)], axis=0)
    scores = matmul(tails.reshape(req_count * tail_count, width), lm_head)
    peaks = jnp.max(scores, axis=1).reshape(req_count, tail_count)
    owners = jnp.arange(req_count, dtype=jnp.int32)
    found = (owners[:, None] ^ owners[None, :]) == lax.axis_index("req")
    peaks = jnp.sum(jnp.where(found[:, :, None], peaks[None], 0.0), axis=1).reshape(1, -1)
    for axis, bits in (("kv", kv_bits), ("req", req_bits)):
        for bit in bits:
            peaks = jnp.maximum(peaks, swap(peaks, axis, bit))
    return (layer_out, peaks[0])


def solution(mesh):
    placed = (
        P(("req", "kv"), None),
        P(),
        P("req"),
        P("req"),
        P("req", None, "kv"),
        P("req", None, "kv"),
        P("req", None, "kv"),
        P("req", None, "kv"),
        P(),
        P(None, "kv"),
        P(None, "kv"),
        P(None, "kv"),
        P(),
        P(),
        P("kv", None),
        P(),
        P(None, "req"),
        P(None, "req"),
        P("req", None),
        P(),
        P(None, ("req", "kv")),
    )
    return jax.shard_map(
        shards, mesh=mesh, in_specs=placed, out_specs=(P(("req", "kv"), None), P()), check_vma=False
    )
```

```python
import functools
import math

import jax
import jax.numpy as jnp
from jax import lax
from jax.experimental import pallas as pl
from jax.experimental.pallas import tpu as pltpu
from jax.sharding import PartitionSpec as P

EPS = 1e-06
NEG = -1e30
GROUP = 4
TAIL = 16
DECODE_GROUP = 4
KEY_BLOCK = 512
VMEM_LIMIT = 56 * 1024 * 1024
BRIEF = pl.CostEstimate(flops=1, bytes_accessed=1, transcendentals=0)


def swap(value, axis, bit):
    size = lax.axis_size(axis)
    return lax.ppermute(value, axis, [(i, i ^ bit) for i in range(size)])


def bits_below(size):
    return [1 << i for i in range(size.bit_length() - 1)]


def gather_xor(value, axis, bits):
    held = {0: value}
    for bit in bits:
        held.update({diff ^ bit: swap(block, axis, bit) for diff, block in list(held.items())})
    return held


def zero_after(value):
    first = value[(0,) * value.ndim]
    return (first != first).astype(jnp.int32)


def held_until(value, other):
    return value + zero_after(other).astype(value.dtype)


def norm_rows(values, gain_vec):
    wide = values.astype(jnp.float32)
    return wide * lax.rsqrt(jnp.mean(wide * wide, axis=-1, keepdims=True) + EPS) * gain_vec


def angle_tables(places, head_dim):
    half_dim = head_dim // 2
    freqs = 1000000.0 ** (-(jnp.arange(half_dim, dtype=jnp.float32) * 2.0 / head_dim))
    angles = places[:, None] * freqs[None, :]
    return jnp.cos(angles), jnp.sin(angles)


def contract_last(left, right):
    return lax.dot_general(left, right, (((1,), (1,)), ((), ())), preferred_element_type=jnp.float32)


def whole_spec(shape):
    return pl.BlockSpec(shape, lambda *_: (0,) * len(shape))


def project_kernel(block_count, head_dim, *refs):
    row_refs = refs[:block_count]
    (gain_ref, cos_ref, sin_ref, q_gain_ref, k_gain_ref, wq_hbm, wk_hbm, wv_hbm) = refs[
        block_count : block_count + 8
    ]
    q_ref, k_ref, v_ref, wq, wk, wv, sems = refs[-7:]
    copies = [
        pltpu.make_async_copy(hbm, vmem, sems.at[at])
        for at, (hbm, vmem) in enumerate(((wq_hbm, wq), (wk_hbm, wk), (wv_hbm, wv)))
    ]
    for copy in copies:
        copy.start()
    normed = []
    for ref in row_refs:
        wide = ref[...].astype(jnp.float32)
        scale = lax.rsqrt(jnp.mean(wide * wide, axis=-1, keepdims=True) + EPS)
        normed.append((wide * scale * gain_ref[...]).astype(jnp.bfloat16))
    rows = jnp.concatenate(normed, axis=0)
    cosine, sine = cos_ref[...], sin_ref[...]

    def heads(raw, gain, out_ref):
        for at in range(raw.shape[1] // head_dim):
            head = raw[:, at * head_dim : (at + 1) * head_dim]
            scale = lax.rsqrt(jnp.mean(head * head, axis=-1, keepdims=True) + EPS)
            head = head * scale * gain
            turned = head * cosine + pltpu.roll(head, head_dim // 2, 1) * sine
            out_ref[:, at * head_dim : (at + 1) * head_dim] = turned.astype(jnp.bfloat16)

    copies[0].wait()
    heads(matmul(rows, wq[...]), q_gain_ref[...], q_ref)
    copies[1].wait()
    heads(matmul(rows, wk[...]), k_gain_ref[...], k_ref)
    copies[2].wait()
    v_ref[...] = matmul(rows, wv[...]).astype(jnp.bfloat16)


def project(blocks, gain, cosine, sine, q_gain, k_gain, q_proj, k_proj, v_proj):
    head_dim = q_gain.shape[0]
    rows = sum(block.shape[0] for block in blocks)
    width = q_proj.shape[0]
    outs = (q_proj.shape[1], k_proj.shape[1], v_proj.shape[1])
    vectors = (gain[None, :], cosine, sine, q_gain[None, :], k_gain[None, :])
    return pl.pallas_call(
        functools.partial(project_kernel, len(blocks), head_dim),
        out_shape=[jax.ShapeDtypeStruct((rows, cols), jnp.bfloat16) for cols in outs],
        in_specs=[whole_spec(block.shape) for block in blocks]
        + [whole_spec(vector.shape) for vector in vectors]
        + [pl.BlockSpec(memory_space=pl.ANY)] * 3,
        out_specs=[whole_spec((rows, cols)) for cols in outs],
        grid=(1,),
        scratch_shapes=[pltpu.VMEM((width, cols), jnp.bfloat16) for cols in outs]
        + [pltpu.SemaphoreType.DMA((3,))],
        compiler_params=pltpu.CompilerParams(vmem_limit_bytes=VMEM_LIMIT),
        cost_estimate=BRIEF,
    )(*blocks, *vectors, q_proj, k_proj, v_proj)


def attend_kernel(
    block_count,
    head_dim,
    lens_ref,
    q_refs,
    k_refs,
    v_refs,
    kp_ref,
    vp_ref,
    kc_hbm,
    vc_hbm,
    out_ref,
    q_all,
    k_all,
    v_all,
    peak,
    acc,
    kc,
    vc,
    dec_q,
    dec_out,
    sems,
):
    step = pl.program_id(0)
    steps = pl.num_programs(0)
    kv_index, start = lens_ref[0], lens_ref[1]
    dec_count, slots, kv_cols = kc.shape
    kv_heads = kv_cols // head_dim
    tok_req, q_cols = q_all.shape
    group = q_cols // kv_cols
    rows = tok_req // block_count
    scale = head_dim**-0.5 * math.log2(math.e)
    sizes = (slots // 4, slots // 2, slots)

    def by_size(together, act):
        first = together * DECODE_GROUP
        length = lens_ref[2 + first]
        for at in range(1, DECODE_GROUP):
            length = jnp.maximum(length, lens_ref[2 + first + at])
        for at, size in enumerate(sizes):
            fits = length <= size
            if at:
                fits = fits & (length > sizes[at - 1])
            pl.when(fits)(functools.partial(act, first, size))

    def cache_copies(request, size):
        return (
            pltpu.make_async_copy(
                kc_hbm.at[request, pl.ds(0, size)], kc.at[request, pl.ds(0, size)], sems.at[0, request]
            ),
            pltpu.make_async_copy(
                vc_hbm.at[request, pl.ds(0, size)], vc.at[request, pl.ds(0, size)], sems.at[1, request]
            ),
        )

    def start_copies(first, size):
        for at in range(DECODE_GROUP):
            for copy in cache_copies(first + at, size):
                copy.start()

    @pl.when(step == 0)
    def _():
        for together in range(dec_count // DECODE_GROUP):
            by_size(together, start_copies)
        for refs, whole in ((q_refs, q_all), (k_refs, k_all), (v_refs, v_all)):
            at = 0
            for ref in refs:
                whole[at : at + ref.shape[0], :] = ref[...]
                at += ref.shape[0]

    span = 2 * rows
    row_at = pl.multiple_of(step * span, span)
    mine = (kv_index // 2) ^ step
    heads = q_cols // head_dim
    queries = [
        q_all[pl.ds(row_at, span), head * head_dim : (head + 1) * head_dim] for head in range(heads)
    ]
    peak[...] = jnp.full(peak.shape, NEG, jnp.float32)
    acc[...] = jnp.zeros(acc.shape, jnp.float32)

    def absorb(keys_ref, values_ref, place, size, allowed):
        for head in range(heads):
            lanes = slice(head // group * head_dim, (head // group + 1) * head_dim)
            keys = keys_ref[pl.ds(place, size), lanes]
            values = values_ref[pl.ds(place, size), lanes]
            wide = jnp.concatenate([values, jnp.ones_like(values)], axis=1)
            scores = contract_last(queries[head], keys)
            if allowed is not None:
                scores = jnp.where(allowed, scores, NEG)
            old = peak[head][:, :1]
            new = jnp.maximum(old, jnp.max(scores, axis=1, keepdims=True))
            weights = jnp.exp2((scores - new) * scale).astype(jnp.bfloat16)
            acc[head] = acc[head] * jnp.exp2((old - new) * scale) + matmul(weights, wide)
            peak[head] = jnp.broadcast_to(new, peak.shape[1:])

    full = start // KEY_BLOCK

    def prefix_block(at, carry):
        absorb(kp_ref, vp_ref, pl.multiple_of(at * KEY_BLOCK, KEY_BLOCK), KEY_BLOCK, None)
        return carry

    lax.fori_loop(0, full, prefix_block, 0)

    @pl.when(full * KEY_BLOCK < start)
    def _():
        place = pl.multiple_of(full * KEY_BLOCK, KEY_BLOCK)
        ids = lax.broadcasted_iota(jnp.int32, (span, KEY_BLOCK), 1)
        absorb(kp_ref, vp_ref, place, KEY_BLOCK, ids < start - place)

    def fresh_block(at, carry):
        @pl.when(((kv_index // 2) ^ at) < mine)
        def _():
            absorb(k_all, v_all, pl.multiple_of(at * span, span), span, None)

        return carry

    lax.fori_loop(0, steps, fresh_block, 0)
    turned = kv_index % 2

    def order(axis):
        ids = lax.broadcasted_iota(jnp.int32, (span, span), axis)
        swapped = jnp.where(ids < rows, ids + rows, ids - rows)
        return jnp.where(turned == 1, swapped, ids)

    absorb(k_all, v_all, row_at, span, order(1) <= order(0))
    for head in range(heads):
        at = head * head_dim
        out_ref[pl.ds(row_at, span), at : at + head_dim] = (
            acc[head][:, :head_dim] / acc[head][:, head_dim:]
        ).astype(jnp.bfloat16)

    @pl.when(step == steps - 1)
    def _():
        last = (kv_index ^ (block_count - 1)) * rows
        tail = pl.ds(pl.multiple_of(last + rows - 16, 16), 16)
        q_dec = q_all[tail, :][16 - dec_count :].astype(jnp.float32)
        k_dec = k_all[tail, :][16 - dec_count :].astype(jnp.float32)
        v_dec = v_all[tail, :][16 - dec_count :].astype(jnp.float32)
        for request in range(dec_count):
            at = slice(request, request + 1)
            dec_q[request] = jnp.concatenate([q_dec[at], k_dec[at], v_dec[at]], axis=1)

        def attend_some(first, size):
            for at in range(DECODE_GROUP):
                attend_one(first + at, size)

        def attend_one(request, size):
            for copy in cache_copies(request, size):
                copy.wait()
            row = dec_q[request]
            empty = jnp.zeros((1, head_dim), jnp.float32)
            spread = []
            for at in range(heads):
                parts = [empty] * kv_heads
                parts[at // group] = row[:, at * head_dim : (at + 1) * head_dim]
                spread.append(jnp.concatenate(parts, axis=1))
            spread += [jnp.zeros((1, kv_cols), jnp.float32)] * (8 - len(spread))
            q_rows = jnp.concatenate(spread, axis=0)
            key_self = row[:, q_cols : q_cols + kv_cols]
            value_self = row[:, q_cols + kv_cols :]
            past = contract_last(q_rows.astype(jnp.bfloat16), kc[request, :size, :])
            ids = lax.broadcasted_iota(jnp.int32, past.shape, 1)
            past = jnp.where(ids < lens_ref[2 + request], past, NEG)
            own = jnp.sum(q_rows * key_self, axis=1, keepdims=True)
            top = jnp.maximum(jnp.max(past, axis=1, keepdims=True), own)
            past = jnp.exp2((past - top) * scale)
            own = jnp.exp2((own - top) * scale)
            total = jnp.sum(past, axis=1, keepdims=True) + own
            past = (past / total).astype(jnp.bfloat16)
            own = (own / total).astype(jnp.bfloat16).astype(jnp.float32)
            summed = matmul(past, vc[request, :size, :]) + own * value_self
            outs = []
            for at in range(heads):
                lane = (at // group) * head_dim
                outs.append(summed[at : at + 1, lane : lane + head_dim])
            dec_out[request] = jnp.concatenate(outs, axis=1)

        for together in range(dec_count // DECODE_GROUP):
            by_size(together, attend_some)
        kept = out_ref[tail, :][: 16 - dec_count]
        done = jnp.concatenate([dec_out[request] for request in range(dec_count)], axis=0)
        out_ref[tail, :] = jnp.concatenate([kept, done.astype(jnp.bfloat16)], axis=0)


def attend(lens, parts, head_dim, key_prefix, value_prefix, key_cache, value_cache):
    count = len(parts)
    block_count = lax.axis_size("kv")
    queries, keys, values = [[part[at] for part in parts] for at in range(3)]
    tok_req = sum(part.shape[0] for part in queries)
    q_cols, kv_cols = queries[0].shape[1], keys[0].shape[1]
    dec_count, slots = key_cache.shape[:2]
    rows = tok_req // block_count

    def kernel(lens_ref, *refs):
        cuts = [refs[at * count : (at + 1) * count] for at in range(3)]
        attend_kernel(block_count, head_dim, lens_ref, *cuts, *refs[3 * count :])

    return pl.pallas_call(
        kernel,
        out_shape=jax.ShapeDtypeStruct((tok_req, q_cols), jnp.bfloat16),
        grid_spec=pltpu.PrefetchScalarGridSpec(
            num_scalar_prefetch=1,
            grid=(block_count // 2,),
            in_specs=[whole_spec(part.shape) for part in queries + keys + values]
            + [whole_spec(key_prefix.shape), whole_spec(value_prefix.shape)]
            + [pl.BlockSpec(memory_space=pl.ANY)] * 2,
            out_specs=whole_spec((tok_req, q_cols)),
            scratch_shapes=[
                pltpu.VMEM((tok_req, q_cols), jnp.bfloat16),
                pltpu.VMEM((tok_req, kv_cols), jnp.bfloat16),
                pltpu.VMEM((tok_req, kv_cols), jnp.bfloat16),
                pltpu.VMEM((q_cols // head_dim, 2 * rows, head_dim), jnp.float32),
                pltpu.VMEM((q_cols // head_dim, 2 * rows, 2 * head_dim), jnp.float32),
                pltpu.VMEM((dec_count, slots, kv_cols), jnp.bfloat16),
                pltpu.VMEM((dec_count, slots, kv_cols), jnp.bfloat16),
                pltpu.VMEM((dec_count, 1, q_cols + 2 * kv_cols), jnp.float32),
                pltpu.VMEM((dec_count, 1, q_cols), jnp.float32),
                pltpu.SemaphoreType.DMA((2, dec_count)),
            ],
        ),
        compiler_params=pltpu.CompilerParams(vmem_limit_bytes=VMEM_LIMIT),
        cost_estimate=BRIEF,
    )(lens, *queries, *keys, *values, key_prefix, value_prefix, key_cache, value_cache)


def join_kernel(count, kv_ref, *refs):
    pieces = refs[:count]
    weight_ref, rows_ref, last_ref, gain_ref = refs[count : count + 4]
    resid_ref, last_resid_ref, normed_ref, last_normed_ref, total = refs[count + 4 :]
    step = pl.program_id(0)
    for at in range(count):

        @pl.when(step == at)
        def _():
            part = matmul(pieces[at][...], weight_ref[...])
            total[...] = part if at == 0 else total[...] + part

    @pl.when(step == count - 1)
    def _():
        rows = jnp.concatenate([rows_ref[...], last_ref[...]], axis=0)
        resid = (rows.astype(jnp.float32) + total[...]).astype(jnp.bfloat16)
        wide = resid.astype(jnp.float32)
        scale = lax.rsqrt(jnp.mean(wide * wide, axis=-1, keepdims=True) + EPS)
        normed = (wide * scale * gain_ref[...]).astype(jnp.bfloat16)
        size = rows_ref.shape[0]
        resid_ref[...] = resid[:size]
        last_resid_ref[...] = resid[size:]
        normed_ref[...] = normed[:size]
        last_normed_ref[...] = normed[size:]


def join_heads(pieces, o_whole, rows, last_rows, gain, index):
    count = len(pieces)
    size, cols = pieces[0].shape
    shape = (size, rows.shape[1])
    outs = [rows.shape, last_rows.shape] * 2
    return pl.pallas_call(
        functools.partial(join_kernel, count),
        out_shape=[jax.ShapeDtypeStruct(out, jnp.bfloat16) for out in outs],
        grid_spec=pltpu.PrefetchScalarGridSpec(
            num_scalar_prefetch=1,
            grid=(count,),
            in_specs=[whole_spec(piece.shape) for piece in pieces]
            + [
                pl.BlockSpec((cols, shape[1]), lambda at, index_ref: (index_ref[0] ^ at, 0)),
                whole_spec(rows.shape),
                whole_spec(last_rows.shape),
                whole_spec((1, shape[1])),
            ],
            out_specs=[whole_spec(out) for out in outs],
            scratch_shapes=[pltpu.VMEM(shape, jnp.float32)],
        ),
        compiler_params=pltpu.CompilerParams(vmem_limit_bytes=VMEM_LIMIT),
        cost_estimate=BRIEF,
    )(index, *pieces, o_whole, rows, last_rows, gain[None, :])


def feed_kernel(sets, tiles, counts, *refs):
    pieces = len(counts)
    x_refs, weight_refs = refs[:pieces], refs[pieces : pieces + 3 * sets]
    out_refs = refs[-pieces - 2 : -2]
    x_all, total = refs[-2:]
    step = pl.program_id(0)
    cuts = [sum(counts[:at]) for at in range(pieces + 1)]

    @pl.when(step == 0)
    def _():
        for at, ref in enumerate(x_refs):
            x_all[cuts[at] : cuts[at + 1], :] = ref[...]

    for at in range(sets):
        gate_ref, up_ref, down_ref = weight_refs[3 * at : 3 * at + 3]

        @pl.when(step // tiles == at)
        def _():
            rows = x_all[...]
            tile = gate_ref.shape[-1]
            gate = matmul(rows, gate_ref[...].reshape(-1, tile))
            up = matmul(rows, up_ref[...].reshape(-1, tile))
            act = (gate / (1.0 + jnp.exp(-gate)) * up).astype(jnp.bfloat16)
            if len(down_ref.shape) == 2:
                downs = [down_ref[...]]
            else:
                downs = [down_ref[part] for part in range(down_ref.shape[0])]
            lane = 0
            for down in downs:
                lanes = slice(lane, lane + down.shape[1])
                lane += down.shape[1]
                part = matmul(act, down)
                if at:
                    total[:, lanes] += part
                else:
                    total[:, lanes] = jnp.where(step == 0, part, total[:, lanes] + part)

    @pl.when(step == sets * tiles - 1)
    def _():
        for at, ref in enumerate(out_refs):
            ref[...] = total[cuts[at] : cuts[at + 1], :].astype(ref.dtype)


def feed_forward(blocks, dtypes, own, far, follows=None):
    counts = [block.shape[0] for block in blocks]
    size, width = sum(counts), blocks[0].shape[1]
    hidden = own[0].shape[1]
    tile = far[0].shape[1] // 3
    tiles = hidden // tile
    sets = 1 + len(far)
    specs = [
        pl.BlockSpec((width, tile), lambda step: (0, jnp.minimum(step, tiles - 1))),
        pl.BlockSpec((width, tile), lambda step: (0, jnp.minimum(step, tiles - 1))),
        pl.BlockSpec((tile, width), lambda step: (jnp.minimum(step, tiles - 1), 0)),
    ]
    operands = list(own)
    for at, weights in enumerate(far, 1):
        shares = weights.shape[0]
        share = width // shares

        def place(step, at=at):
            return jnp.clip(step - at * tiles, 0, tiles - 1)

        specs += [
            pl.BlockSpec((shares, share, tile), lambda step, place=place: (0, 0, place(step))),
            pl.BlockSpec((shares, share, tile), lambda step, place=place: (0, 0, tiles + place(step))),
            pl.BlockSpec(
                (shares, tile, share), lambda step, place=place: (0, share // tile, place(step))
            ),
        ]
        operands += [weights] * 3
    waits = [] if follows is None else [follows]

    def kernel(*refs):
        given = len(blocks) + len(operands)
        feed_kernel(sets, tiles, counts, *refs[:given], *refs[given + len(waits) :])

    return pl.pallas_call(
        kernel,
        out_shape=[
            jax.ShapeDtypeStruct((count, width), dtype) for count, dtype in zip(counts, dtypes)
        ],
        grid=(sets * tiles,),
        in_specs=[whole_spec(block.shape) for block in blocks]
        + specs
        + [pl.BlockSpec(memory_space=pl.ANY)] * len(waits),
        out_specs=[whole_spec((count, width)) for count in counts],
        scratch_shapes=[
            pltpu.VMEM((size, width), jnp.bfloat16),
            pltpu.VMEM((size, width), jnp.float32),
        ],
        compiler_params=pltpu.CompilerParams(vmem_limit_bytes=VMEM_LIMIT),
        cost_estimate=BRIEF,
    )(*blocks, *operands, *waits)


def regroup(rows_in):
    return lax.all_to_all(rows_in, ("req", "kv"), split_axis=0, concat_axis=0, tiled=True)


def matmul(left, right):
    return jnp.dot(left, right, preferred_element_type=jnp.float32)


def routes(slot_tokens, self_index, devices, rows_dev, ready):
    per_pair = rows_dev // devices
    slot_table = slot_tokens.reshape(devices, rows_dev)
    source = slot_table // rows_dev
    places = jnp.arange(rows_dev, dtype=jnp.int32)
    before = (places[:, None] < places[None, :]).astype(jnp.bfloat16)
    from_self = source == self_index
    rank = matmul(from_self.astype(jnp.bfloat16), before).astype(jnp.int32)
    local = slot_table - self_index * rows_dev
    ranked = jnp.where(from_self, rank, -1)[:, None, :] == jnp.arange(per_pair, dtype=jnp.int32)[None, :, None]
    send_rows = jnp.sum(jnp.where(ranked, local[:, None, :], 0), axis=2).reshape(-1)
    send_hot = (send_rows[:, None] == places[None, :]).astype(jnp.bfloat16)
    own = lax.dynamic_index_in_dim(source, self_index, 0, keepdims=False)
    earlier = (own[:, None] == own[None, :]) & (places[:, None] > places[None, :])
    own_rank = jnp.sum(earlier.astype(jnp.int32), axis=1)
    slot_hot = ((own * per_pair + own_rank + ready)[:, None] == places[None, :]).astype(jnp.bfloat16)
    return send_hot, slot_hot


def pick(hot, rows, transposed=False):
    if transposed:
        return lax.dot_general(
            hot, rows, (((0,), (0,)), ((), ())), preferred_element_type=jnp.float32
        ).astype(rows.dtype)
    return matmul(hot, rows).astype(rows.dtype)


def shards(
    hidden_in,
    slot_tokens,
    cache_len,
    prefill_start,
    key_cache,
    value_cache,
    key_prefix,
    value_prefix,
    attn_gain,
    q_proj,
    k_proj,
    v_proj,
    q_gain,
    k_gain,
    o_proj,
    ffn_gain,
    w_gate,
    w_up,
    w_down,
    final_gain,
    lm_head,
):
    req_count = lax.axis_size("req")
    kv_count = lax.axis_size("kv")
    devices = req_count * kv_count
    rows_dev, width = hidden_in.shape
    kv_index = lax.axis_index("kv")
    self_index = lax.axis_index("req") * kv_count + kv_index
    kv_bits = bits_below(kv_count)
    near_bits = [bit for bit in bits_below(req_count) if bit < GROUP]
    far_bits = [bit for bit in bits_below(req_count) if bit >= GROUP]

    head_dim = q_gain.shape[0]
    dec_count = cache_len.shape[0]
    tok_req = rows_dev * kv_count
    fresh_count = tok_req - dec_count
    places = jnp.concatenate(
        [prefill_start[0] + jnp.arange(fresh_count, dtype=jnp.int32), cache_len]
    ).astype(jnp.float32)
    cosines, sines = angle_tables(places, head_dim)
    cosines = jnp.concatenate([cosines, cosines], axis=1)
    sines = jnp.concatenate([-sines, sines], axis=1)

    cosines, sines = lax.optimization_barrier((cosines, sines))
    ready = zero_after(cosines) + zero_after(sines)

    send_hot, slot_hot = routes(slot_tokens, self_index, devices, rows_dev, ready)
    arrived = regroup(pick(send_hot, hidden_in))
    owner_rows = pick(slot_hot, arrived)
    share = width // kv_count
    tile = share // 2
    from_row = (kv_index + zero_after(arrived)) * share
    own_down = lax.dynamic_slice_in_dim(w_down, from_row, share, 1)
    far_share = jnp.concatenate(
        [
            jnp.concatenate(
                [
                    lax.dynamic_slice_in_dim(w_gate, from_row, share, 0),
                    lax.dynamic_slice_in_dim(w_up, from_row, share, 0),
                ],
                axis=1,
            ),
            jnp.concatenate(
                [own_down[at : at + tile] for at in range(0, w_down.shape[0], tile)], axis=1
            ),
        ],
        axis=0,
    )
    far_shares = gather_xor(far_share, "req", far_bits)

    q_cols = q_proj.shape[1]

    def project_block(diff):
        block_at = (kv_index ^ diff) * rows_dev
        tables = [lax.dynamic_slice_in_dim(table, block_at, rows_dev, 0) for table in (cosines, sines)]
        return project([blocks[diff]], attn_gain, *tables, q_gain, k_gain, q_proj, k_proj, v_proj)

    even = gather_xor(owner_rows, "kv", kv_bits[:0:-1])
    blocks = {0: owner_rows, 1: swap(owner_rows, "kv", 1)}
    parts = [project_block(0), project_block(1)]
    for diff in range(2, kv_count, 2):
        blocks[diff] = held_until(even[diff], parts[1][2])
        blocks[diff + 1] = swap(blocks[diff], "kv", 1)
    for diff in range(2, kv_count):
        parts.append(project_block(diff))

    o_whole = lax.all_gather(o_proj, "kv", axis=0, tiled=True)
    lens = jnp.concatenate([kv_index[None], prefill_start, cache_len]).astype(jnp.int32)
    attended = attend(
        lens, parts, head_dim, key_prefix[0], value_prefix[0], key_cache, value_cache
    )
    last_at = (kv_index ^ (kv_count - 1)) * rows_dev + rows_dev - TAIL
    last_rows = lax.dynamic_slice_in_dim(attended, last_at, TAIL, 0)
    last_raw = blocks[0][rows_dev - TAIL :]
    pieces = []
    for diff in range(kv_count):
        block = jnp.concatenate([attended[diff * rows_dev : (diff + 1) * rows_dev], last_rows], axis=0)
        pieces.append(swap(block, "kv", diff) if diff else block)
        is_last = (kv_index ^ diff) == kv_count - 1
        last_raw = jnp.where(is_last, blocks[diff][rows_dev - TAIL :], last_raw)
    resid, last_resid, ffn_in, last_in = join_heads(
        pieces, o_whole, owner_rows, last_raw, ffn_gain, lens[:1]
    )

    own_weights = (w_gate, w_up, w_down)
    far_weights = [
        lax.all_gather(held_until(far_shares[diff], attended), "kv", axis=0)
        for diff in far_shares
        if diff
    ]

    last_near = gather_xor(last_in, "req", near_bits)
    near = {0: ffn_in, 1: swap(ffn_in, "req", 1), 2: swap(ffn_in, "req", 2)}
    f32, bf16 = jnp.float32, jnp.bfloat16
    own_part = feed_forward([ffn_in], [f32], own_weights, far_weights)[0]
    near[3] = swap(held_until(near[1], own_part), "req", 2)
    first, second, last_part, *last_parts = feed_forward(
        [near[1], near[2]] + [last_near[diff] for diff in range(GROUP)],
        [bf16, bf16, f32] + [bf16] * (GROUP - 1),
        own_weights,
        far_weights,
        follows=own_part,
    )
    rest = feed_forward([near[3]], [bf16], own_weights, far_weights, follows=first)
    ffn_part = own_part
    for diff, part in enumerate([first, second, *rest], 1):
        ffn_part = ffn_part + swap(part, "req", diff).astype(f32)
    out_rows = (resid.astype(jnp.float32) + ffn_part).astype(jnp.bfloat16)
    returned = regroup(pick(slot_hot, out_rows, transposed=True))
    layer_out = pick(send_hot, returned, transposed=True)

    tail_count = dec_count + 1
    for diff, part in enumerate(last_parts, 1):
        last_part = last_part + swap(part, "req", diff).astype(f32)
    last_rows = (last_resid.astype(f32) + last_part).astype(bf16)
    tails = norm_rows(last_rows, final_gain).astype(bf16)
    req_bits = bits_below(req_count)
    for bit in req_bits:
        tails = jnp.concatenate([tails, swap(tails, "req", bit)], axis=0)
    tails = held_until(tails, out_rows)
    peaks = jnp.max(matmul(tails, lm_head), axis=1).reshape(req_count, TAIL)
    peaks = peaks[:, TAIL - tail_count :]
    owners = jnp.arange(req_count, dtype=jnp.int32)
    found = (owners[:, None] ^ owners[None, :]) == lax.axis_index("req")
    peaks = jnp.sum(jnp.where(found[:, :, None], peaks[None], 0.0), axis=1).reshape(1, -1)
    for axis, bits in (("kv", kv_bits), ("req", req_bits)):
        for bit in bits:
            peaks = jnp.maximum(peaks, swap(peaks, axis, bit))
    return (layer_out, peaks[0])


def solution(mesh):
    placed = (
        P(("req", "kv"), None),
        P(),
        P("req"),
        P("req"),
        P("req", None, "kv"),
        P("req", None, "kv"),
        P("req", None, "kv"),
        P("req", None, "kv"),
        P(),
        P(None, "kv"),
        P(None, "kv"),
        P(None, "kv"),
        P(),
        P(),
        P("kv", None),
        P(),
        P(None, "req"),
        P(None, "req"),
        P("req", None),
        P(),
        P(None, ("req", "kv")),
    )
    return jax.shard_map(
        shards, mesh=mesh, in_specs=placed, out_specs=(P(("req", "kv"), None), P()), check_vma=False
    )
```

```python
import functools
import math

import jax
import jax.numpy as jnp
from jax import lax
from jax.experimental import pallas as pl
from jax.experimental.pallas import tpu as pltpu
from jax.sharding import PartitionSpec as P

EPS = 1e-06
NEG = -1e30
GROUP = 4
TAIL = 16
DECODE_GROUP = 4
KEY_BLOCK = 512
VMEM_LIMIT = 56 * 1024 * 1024
BRIEF = pl.CostEstimate(flops=1, bytes_accessed=1, transcendentals=0)


def swap(value, axis, bit):
    size = lax.axis_size(axis)
    return lax.ppermute(value, axis, [(i, i ^ bit) for i in range(size)])


def bits_below(size):
    return [1 << i for i in range(size.bit_length() - 1)]


def gather_xor(value, axis, bits):
    held = {0: value}
    for bit in bits:
        held.update({diff ^ bit: swap(block, axis, bit) for diff, block in list(held.items())})
    return held


def zero_after(value):
    first = value[(0,) * value.ndim]
    return (first != first).astype(jnp.int32)


def pin(value, *others):
    anywhere = pl.BlockSpec(memory_space=pl.ANY)
    return pl.pallas_call(
        lambda *refs: None,
        out_shape=jax.ShapeDtypeStruct(value.shape, value.dtype),
        in_specs=[anywhere] * (1 + len(others)),
        out_specs=anywhere,
        input_output_aliases={0: 0},
        cost_estimate=BRIEF,
    )(value, *others)


def norm_rows(values, gain_vec):
    wide = values.astype(jnp.float32)
    return wide * lax.rsqrt(jnp.mean(wide * wide, axis=-1, keepdims=True) + EPS) * gain_vec


def angle_tables(places, head_dim):
    half_dim = head_dim // 2
    freqs = 1000000.0 ** (-(jnp.arange(half_dim, dtype=jnp.float32) * 2.0 / head_dim))
    angles = places[:, None] * freqs[None, :]
    return jnp.cos(angles), jnp.sin(angles)


def contract_last(left, right):
    return lax.dot_general(left, right, (((1,), (1,)), ((), ())), preferred_element_type=jnp.float32)


def whole_spec(shape):
    return pl.BlockSpec(shape, lambda *_: (0,) * len(shape))


def project_kernel(block_count, head_dim, *refs):
    row_refs = refs[:block_count]
    (gain_ref, cos_ref, sin_ref, q_gain_ref, k_gain_ref, wq_hbm, wk_hbm, wv_hbm) = refs[
        block_count : block_count + 8
    ]
    q_ref, k_ref, v_ref, wq, wk, wv, sems = refs[-7:]
    copies = [
        pltpu.make_async_copy(hbm, vmem, sems.at[at])
        for at, (hbm, vmem) in enumerate(((wq_hbm, wq), (wk_hbm, wk), (wv_hbm, wv)))
    ]
    for copy in copies:
        copy.start()
    normed = []
    for ref in row_refs:
        wide = ref[...].astype(jnp.float32)
        scale = lax.rsqrt(jnp.mean(wide * wide, axis=-1, keepdims=True) + EPS)
        normed.append((wide * scale * gain_ref[...]).astype(jnp.bfloat16))
    rows = jnp.concatenate(normed, axis=0)
    cosine, sine = cos_ref[...], sin_ref[...]

    def heads(raw, gain, out_ref):
        for at in range(raw.shape[1] // head_dim):
            head = raw[:, at * head_dim : (at + 1) * head_dim]
            scale = lax.rsqrt(jnp.mean(head * head, axis=-1, keepdims=True) + EPS)
            head = head * scale * gain
            turned = head * cosine + pltpu.roll(head, head_dim // 2, 1) * sine
            out_ref[:, at * head_dim : (at + 1) * head_dim] = turned.astype(jnp.bfloat16)

    copies[0].wait()
    heads(matmul(rows, wq[...]), q_gain_ref[...], q_ref)
    copies[1].wait()
    heads(matmul(rows, wk[...]), k_gain_ref[...], k_ref)
    copies[2].wait()
    v_ref[...] = matmul(rows, wv[...]).astype(jnp.bfloat16)


def project(blocks, gain, cosine, sine, q_gain, k_gain, q_proj, k_proj, v_proj):
    head_dim = q_gain.shape[0]
    rows = sum(block.shape[0] for block in blocks)
    width = q_proj.shape[0]
    outs = (q_proj.shape[1], k_proj.shape[1], v_proj.shape[1])
    vectors = (gain[None, :], cosine, sine, q_gain[None, :], k_gain[None, :])
    return pl.pallas_call(
        functools.partial(project_kernel, len(blocks), head_dim),
        out_shape=[jax.ShapeDtypeStruct((rows, cols), jnp.bfloat16) for cols in outs],
        in_specs=[whole_spec(block.shape) for block in blocks]
        + [whole_spec(vector.shape) for vector in vectors]
        + [pl.BlockSpec(memory_space=pl.ANY)] * 3,
        out_specs=[whole_spec((rows, cols)) for cols in outs],
        grid=(1,),
        scratch_shapes=[pltpu.VMEM((width, cols), jnp.bfloat16) for cols in outs]
        + [pltpu.SemaphoreType.DMA((3,))],
        compiler_params=pltpu.CompilerParams(vmem_limit_bytes=VMEM_LIMIT),
        cost_estimate=BRIEF,
    )(*blocks, *vectors, q_proj, k_proj, v_proj)


def share_kernel(share, tile, index_ref, gate, up, down, _, out, sems):
    at = pl.ds(pl.multiple_of(index_ref[0] * share, share), share)
    hidden = gate.shape[1]
    copies = [(gate.at[at, :], out.at[pl.ds(0, share), pl.ds(0, hidden)])]
    copies.append((up.at[at, :], out.at[pl.ds(0, share), pl.ds(hidden, hidden)]))
    for step in range(hidden // tile):
        rows, lanes = pl.ds(step * tile, tile), pl.ds(step * share, share)
        copies.append((down.at[rows, at], out.at[pl.ds(share, tile), lanes]))
    copies = [pltpu.make_async_copy(*ends, sems.at[at]) for at, ends in enumerate(copies)]
    for copy in copies:
        copy.start()
    for copy in copies:
        copy.wait()


def share_of(index, share, gate, up, down, follows):
    hidden = gate.shape[1]
    tile = share // 2
    return pl.pallas_call(
        functools.partial(share_kernel, share, tile),
        out_shape=jax.ShapeDtypeStruct((share + tile, 2 * hidden), gate.dtype),
        in_specs=[pl.BlockSpec(memory_space=pltpu.SMEM)] + [pl.BlockSpec(memory_space=pl.ANY)] * 4,
        out_specs=pl.BlockSpec(memory_space=pl.ANY),
        scratch_shapes=[pltpu.SemaphoreType.DMA((2 + hidden // tile,))],
        cost_estimate=BRIEF,
    )(index, gate, up, down, follows)


def attend_kernel(pair, block_count, head_dim, lens_ref, *refs):
    q_refs, refs = refs[:2], refs[2:]
    k_refs, refs = refs[:block_count], refs[block_count:]
    v_refs, refs = refs[:block_count], refs[block_count:]
    sources, refs = refs[:3], refs[3 + 1 :]
    even_ref, odd_ref, last_ref, k_all, v_all, peak, acc, attended, kp, vp, weight, sems = refs
    copies = [
        pltpu.make_async_copy(source, target, sems.at[at])
        for at, (source, target) in enumerate(zip(sources, (kp, vp, weight)))
    ]
    for copy in copies:
        copy.start()
    kv_index, start = lens_ref[0], lens_ref[1]
    rows, q_cols = q_refs[0].shape
    kv_cols = k_all.shape[1]
    group = q_cols // kv_cols
    heads = q_cols // head_dim
    span = 2 * rows
    scale = head_dim**-0.5 * math.log2(math.e)
    for refs, whole in ((k_refs, k_all), (v_refs, v_all)):
        for at, ref in enumerate(refs):
            whole[at * rows : (at + 1) * rows, :] = ref[...]
    queries = [
        jnp.concatenate([ref[:, head * head_dim : (head + 1) * head_dim] for ref in q_refs], axis=0)
        for head in range(heads)
    ]
    peak[...] = jnp.full(peak.shape, NEG, jnp.float32)
    acc[...] = jnp.zeros(acc.shape, jnp.float32)

    def absorb(keys_ref, values_ref, place, size, allowed):
        for head in range(heads):
            lanes = slice(head // group * head_dim, (head // group + 1) * head_dim)
            keys = keys_ref[pl.ds(place, size), lanes]
            values = values_ref[pl.ds(place, size), lanes]
            wide = jnp.concatenate([values, jnp.ones_like(values)], axis=1)
            scores = contract_last(queries[head], keys)
            if allowed is not None:
                scores = jnp.where(allowed, scores, NEG)
            old = peak[head][:, :1]
            new = jnp.maximum(old, jnp.max(scores, axis=1, keepdims=True))
            weights = jnp.exp2((scores - new) * scale).astype(jnp.bfloat16)
            acc[head] = acc[head] * jnp.exp2((old - new) * scale) + matmul(weights, wide)
            peak[head] = jnp.broadcast_to(new, peak.shape[1:])

    turned = kv_index % 2

    def order(axis):
        ids = lax.broadcasted_iota(jnp.int32, (span, span), axis)
        swapped = jnp.where(ids < rows, ids + rows, ids - rows)
        return jnp.where(turned == 1, swapped, ids)

    absorb(k_all, v_all, pair * span, span, order(1) <= order(0))

    def fresh_block(at, carry):
        @pl.when(((kv_index // 2) ^ at) < ((kv_index // 2) ^ pair))
        def _():
            absorb(k_all, v_all, pl.multiple_of(at * span, span), span, None)

        return carry

    lax.fori_loop(0, block_count // 2, fresh_block, 0)
    copies[0].wait()
    copies[1].wait()
    full = start // KEY_BLOCK

    def prefix_block(at, carry):
        absorb(kp, vp, pl.multiple_of(at * KEY_BLOCK, KEY_BLOCK), KEY_BLOCK, None)
        return carry

    lax.fori_loop(0, full, prefix_block, 0)

    @pl.when(full * KEY_BLOCK < start)
    def _():
        place = pl.multiple_of(full * KEY_BLOCK, KEY_BLOCK)
        ids = lax.broadcasted_iota(jnp.int32, (span, KEY_BLOCK), 1)
        absorb(kp, vp, place, KEY_BLOCK, ids < start - place)

    for head in range(heads):
        attended[:, head * head_dim : (head + 1) * head_dim] = (
            acc[head][:, :head_dim] / acc[head][:, head_dim:]
        ).astype(jnp.bfloat16)
    copies[2].wait()
    width = weight.shape[1]
    for at in range(0, width, q_cols):
        part = matmul(attended[...], weight[:, at : at + q_cols])
        even_ref[:, at : at + q_cols] = part[:rows].astype(even_ref.dtype)
        odd_ref[:, at : at + q_cols] = part[rows:].astype(odd_ref.dtype)
    last = kv_index ^ (block_count - 1)
    here = pl.multiple_of((last % 2) * rows + rows - TAIL, TAIL)
    last_ref[:, :q_cols] = attended[pl.ds(here, TAIL), :]
    ends = [ref[rows - TAIL :, :] for ref in q_refs]
    last_ref[:, q_cols : 2 * q_cols] = jnp.where(last % 2 == 1, ends[1], ends[0])
    there = pl.ds(pl.multiple_of(last * rows + rows - TAIL, TAIL), TAIL)
    last_ref[:, 2 * q_cols : 2 * q_cols + kv_cols] = k_all[there, :]
    last_ref[:, 2 * q_cols + kv_cols :] = v_all[there, :]


def attend(pair, lens, parts, head_dim, key_prefix, value_prefix, o_proj, even_type, follows):
    block_count = len(parts)
    queries, keys, values = [[part[at] for part in parts] for at in range(3)]
    queries = queries[2 * pair : 2 * pair + 2]
    rows, q_cols = queries[0].shape
    kv_cols = keys[0].shape[1]
    width = o_proj.shape[1]
    heads = q_cols // head_dim
    outs = [
        jax.ShapeDtypeStruct((rows, width), even_type),
        jax.ShapeDtypeStruct((rows, width), jnp.bfloat16),
        jax.ShapeDtypeStruct((TAIL, 2 * q_cols + 2 * kv_cols), jnp.bfloat16),
    ]
    return pl.pallas_call(
        functools.partial(attend_kernel, pair, block_count, head_dim),
        out_shape=outs,
        grid_spec=pltpu.PrefetchScalarGridSpec(
            num_scalar_prefetch=1,
            grid=(1,),
            in_specs=[whole_spec(part.shape) for part in queries + keys + values]
            + [pl.BlockSpec(memory_space=pl.ANY)] * 4,
            out_specs=[whole_spec(out.shape) for out in outs],
            scratch_shapes=[
                pltpu.VMEM((rows * block_count, kv_cols), jnp.bfloat16),
                pltpu.VMEM((rows * block_count, kv_cols), jnp.bfloat16),
                pltpu.VMEM((heads, 2 * rows, head_dim), jnp.float32),
                pltpu.VMEM((heads, 2 * rows, 2 * head_dim), jnp.float32),
                pltpu.VMEM((2 * rows, q_cols), jnp.bfloat16),
                pltpu.VMEM(key_prefix.shape, jnp.bfloat16),
                pltpu.VMEM(value_prefix.shape, jnp.bfloat16),
                pltpu.VMEM(o_proj.shape, jnp.bfloat16),
                pltpu.SemaphoreType.DMA((3,)),
            ],
        ),
        compiler_params=pltpu.CompilerParams(vmem_limit_bytes=VMEM_LIMIT),
        cost_estimate=BRIEF,
    )(lens, *queries, *keys, *values, key_prefix, value_prefix, o_proj, follows)


def decode_kernel(pairs, block_count, head_dim, q_cols, kv_cols, lens_ref, *refs):
    last_refs, refs = refs[:pairs], refs[pairs:]
    o_hbm, kc_hbm, vc_hbm, out_ref, kc, vc, weight, dec_in, dec_out, sems, weight_sem = refs
    kv_index = lens_ref[0]
    dec_count, slots = kc.shape[:2]
    group = q_cols // kv_cols
    kv_heads = kv_cols // head_dim
    heads = q_cols // head_dim
    scale = head_dim**-0.5 * math.log2(math.e)
    sizes = (slots // 4, slots // 2, slots)

    def by_size(together, act):
        first = together * DECODE_GROUP
        length = lens_ref[2 + first]
        for at in range(1, DECODE_GROUP):
            length = jnp.maximum(length, lens_ref[2 + first + at])
        for at, size in enumerate(sizes):
            fits = length <= size
            if at:
                fits = fits & (length > sizes[at - 1])
            pl.when(fits)(functools.partial(act, first, size))

    def cache_copies(request, size):
        return (
            pltpu.make_async_copy(
                kc_hbm.at[request, pl.ds(0, size)], kc.at[request, pl.ds(0, size)], sems.at[0, request]
            ),
            pltpu.make_async_copy(
                vc_hbm.at[request, pl.ds(0, size)], vc.at[request, pl.ds(0, size)], sems.at[1, request]
            ),
        )

    def start_copies(first, size):
        for at in range(DECODE_GROUP):
            for copy in cache_copies(first + at, size):
                copy.start()

    for together in range(dec_count // DECODE_GROUP):
        by_size(together, start_copies)
    weight_copy = pltpu.make_async_copy(o_hbm, weight, weight_sem)
    weight_copy.start()
    held = last_refs[0][...]
    for at in range(1, pairs):
        held = jnp.where((kv_index ^ (block_count - 1)) // 2 == at, last_refs[at][...], held)
    rows_in = held[TAIL - dec_count :, q_cols:].astype(jnp.float32)
    for request in range(dec_count):
        dec_in[request] = rows_in[request : request + 1]

    def attend_some(first, size):
        for at in range(DECODE_GROUP):
            attend_one(first + at, size)

    def attend_one(request, size):
        for copy in cache_copies(request, size):
            copy.wait()
        row = dec_in[request]
        empty = jnp.zeros((1, head_dim), jnp.float32)
        spread = []
        for at in range(heads):
            parts = [empty] * kv_heads
            parts[at // group] = row[:, at * head_dim : (at + 1) * head_dim]
            spread.append(jnp.concatenate(parts, axis=1))
        spread += [jnp.zeros((1, kv_cols), jnp.float32)] * (8 - len(spread))
        q_rows = jnp.concatenate(spread, axis=0)
        key_self = row[:, q_cols : q_cols + kv_cols]
        value_self = row[:, q_cols + kv_cols :]
        past = contract_last(q_rows.astype(jnp.bfloat16), kc[request, :size, :])
        ids = lax.broadcasted_iota(jnp.int32, past.shape, 1)
        past = jnp.where(ids < lens_ref[2 + request], past, NEG)
        own = jnp.sum(q_rows * key_self, axis=1, keepdims=True)
        top = jnp.maximum(jnp.max(past, axis=1, keepdims=True), own)
        past = jnp.exp2((past - top) * scale)
        own = jnp.exp2((own - top) * scale)
        total = jnp.sum(past, axis=1, keepdims=True) + own
        past = (past / total).astype(jnp.bfloat16)
        own = (own / total).astype(jnp.bfloat16).astype(jnp.float32)
        summed = matmul(past, vc[request, :size, :]) + own * value_self
        outs = []
        for at in range(heads):
            lane = (at // group) * head_dim
            outs.append(summed[at : at + 1, lane : lane + head_dim])
        dec_out[request] = jnp.concatenate(outs, axis=1)

    for together in range(dec_count // DECODE_GROUP):
        by_size(together, attend_some)
    done = [dec_out[request] for request in range(dec_count)]
    rows = jnp.concatenate([held[: TAIL - dec_count, :q_cols].astype(jnp.float32)] + done, axis=0)
    weight_copy.wait()
    out_ref[...] = matmul(rows.astype(jnp.bfloat16), weight[...]).astype(jnp.bfloat16)


def decode(lens, lasts, head_dim, block_count, o_proj, key_cache, value_cache, follows):
    dec_count, slots, kv_cols = key_cache.shape
    q_cols, width = o_proj.shape
    pairs = len(lasts)

    def kernel(lens_ref, *refs):
        given = pairs + 3
        decode_kernel(
            pairs, block_count, head_dim, q_cols, kv_cols, lens_ref, *refs[:given], *refs[given + 1 :]
        )

    return pl.pallas_call(
        kernel,
        out_shape=jax.ShapeDtypeStruct((TAIL, width), jnp.bfloat16),
        grid_spec=pltpu.PrefetchScalarGridSpec(
            num_scalar_prefetch=1,
            grid=(1,),
            in_specs=[whole_spec(last.shape) for last in lasts]
            + [pl.BlockSpec(memory_space=pl.ANY)] * 4,
            out_specs=whole_spec((TAIL, width)),
            scratch_shapes=[
                pltpu.VMEM((dec_count, slots, kv_cols), jnp.bfloat16),
                pltpu.VMEM((dec_count, slots, kv_cols), jnp.bfloat16),
                pltpu.VMEM(o_proj.shape, jnp.bfloat16),
                pltpu.VMEM((dec_count, 1, q_cols + 2 * kv_cols), jnp.float32),
                pltpu.VMEM((dec_count, 1, q_cols), jnp.float32),
                pltpu.SemaphoreType.DMA((2, dec_count)),
                pltpu.SemaphoreType.DMA,
            ],
        ),
        compiler_params=pltpu.CompilerParams(vmem_limit_bytes=VMEM_LIMIT),
        cost_estimate=BRIEF,
    )(lens, *lasts, o_proj, key_cache, value_cache, follows)


def feed_kernel(tiles, counts, added, *refs):
    pieces = len(counts)
    x_refs, refs = refs[:pieces], refs[pieces:]
    add_refs, refs = refs[:added], refs[added:]
    weight_refs, refs = refs[: len(refs) - 2 - pieces], refs[len(refs) - 2 - pieces :]
    out_refs, (x_all, total) = refs[:pieces], refs[pieces:]
    step = pl.program_id(0)
    cuts = [sum(counts[:at]) for at in range(pieces + 1)]

    @pl.when(step == 0)
    def _():
        for at, ref in enumerate(x_refs):
            x_all[cuts[at] : cuts[at + 1], :] = ref[...]
        for at, ref in enumerate(add_refs):
            total[cuts[at] : cuts[at + 1], :] = ref[...]

    sets = len(weight_refs) // 3
    for at in range(sets):
        gate_ref, up_ref, down_ref = weight_refs[3 * at : 3 * at + 3]

        @pl.when(step // tiles == at)
        def _():
            rows = x_all[...]
            tile = gate_ref.shape[-1]
            gate = matmul(rows, gate_ref[...].reshape(-1, tile))
            up = matmul(rows, up_ref[...].reshape(-1, tile))
            act = (gate / (1.0 + jnp.exp(-gate)) * up).astype(jnp.bfloat16)
            if len(down_ref.shape) == 2:
                downs = [down_ref[...]]
            else:
                downs = [down_ref[part] for part in range(down_ref.shape[0])]
            lane = 0
            for down in downs:
                lanes = slice(lane, lane + down.shape[1])
                lane += down.shape[1]
                part = matmul(act, down)
                if at or added:
                    total[:, lanes] += part
                else:
                    total[:, lanes] = jnp.where(step == 0, part, total[:, lanes] + part)

    @pl.when(step == sets * tiles - 1)
    def _():
        for at, ref in enumerate(out_refs):
            ref[...] = total[cuts[at] : cuts[at + 1], :].astype(ref.dtype)


def feed_forward(blocks, dtypes, weights, follows, adds=()):
    counts = [block.shape[0] for block in blocks]
    size, width = sum(counts), blocks[0].shape[1]
    held = weights[0]
    hidden = held[0].shape[1] if isinstance(held, tuple) else held.shape[2] // 2
    tile = 256 if hidden % 256 == 0 else 128
    tiles = hidden // tile
    specs, operands = [], []
    for at, held in enumerate(weights):

        def place(step, at=at):
            return jnp.clip(step - at * tiles, 0, tiles - 1)

        if isinstance(held, tuple):
            specs += [
                pl.BlockSpec((width, tile), lambda step, place=place: (0, place(step))),
                pl.BlockSpec((width, tile), lambda step, place=place: (0, place(step))),
                pl.BlockSpec((tile, width), lambda step, place=place: (place(step), 0)),
            ]
            operands += held
            continue
        shares = held.shape[0]
        share = width // shares
        specs += [
            pl.BlockSpec((shares, share, tile), lambda step, place=place: (0, 0, place(step))),
            pl.BlockSpec((shares, share, tile), lambda step, place=place: (0, 0, tiles + place(step))),
            pl.BlockSpec(
                (shares, tile, share),
                lambda step, place=place, below=share // tile: (0, below, place(step)),
            ),
        ]
        operands += [held] * 3

    def kernel(*refs):
        given = len(blocks) + len(adds) + len(operands)
        feed_kernel(tiles, counts, len(adds), *refs[:given], *refs[given + len(follows) :])

    return pl.pallas_call(
        kernel,
        out_shape=[
            jax.ShapeDtypeStruct((count, width), dtype) for count, dtype in zip(counts, dtypes)
        ],
        grid=(len(weights) * tiles,),
        in_specs=[whole_spec(block.shape) for block in blocks]
        + [whole_spec(add.shape) for add in adds]
        + specs
        + [pl.BlockSpec(memory_space=pl.ANY)] * len(follows),
        out_specs=[whole_spec((count, width)) for count in counts],
        scratch_shapes=[
            pltpu.VMEM((size, width), jnp.bfloat16),
            pltpu.VMEM((size, width), jnp.float32),
        ],
        compiler_params=pltpu.CompilerParams(vmem_limit_bytes=VMEM_LIMIT),
        cost_estimate=BRIEF,
    )(*blocks, *adds, *operands, *follows)


def regroup(rows_in):
    return lax.all_to_all(rows_in, ("req", "kv"), split_axis=0, concat_axis=0, tiled=True)


def matmul(left, right):
    return jnp.dot(left, right, preferred_element_type=jnp.float32)


def routes(slot_tokens, self_index, devices, rows_dev, ready):
    per_pair = rows_dev // devices
    slot_table = slot_tokens.reshape(devices, rows_dev)
    source = slot_table // rows_dev
    places = jnp.arange(rows_dev, dtype=jnp.int32)
    before = (places[:, None] < places[None, :]).astype(jnp.bfloat16)
    from_self = source == self_index
    rank = matmul(from_self.astype(jnp.bfloat16), before).astype(jnp.int32)
    local = slot_table - self_index * rows_dev
    ranked = jnp.where(from_self, rank, -1)[:, None, :] == jnp.arange(per_pair, dtype=jnp.int32)[None, :, None]
    send_rows = jnp.sum(jnp.where(ranked, local[:, None, :], 0), axis=2).reshape(-1)
    send_hot = (send_rows[:, None] == places[None, :]).astype(jnp.bfloat16)
    own = lax.dynamic_index_in_dim(source, self_index, 0, keepdims=False)
    earlier = (own[:, None] == own[None, :]) & (places[:, None] > places[None, :])
    own_rank = jnp.sum(earlier.astype(jnp.int32), axis=1)
    slot_hot = ((own * per_pair + own_rank + ready)[:, None] == places[None, :]).astype(jnp.bfloat16)
    return send_hot, slot_hot


def pick(hot, rows, transposed=False):
    if transposed:
        return lax.dot_general(
            hot, rows, (((0,), (0,)), ((), ())), preferred_element_type=jnp.float32
        ).astype(rows.dtype)
    return matmul(hot, rows).astype(rows.dtype)


def shards(
    hidden_in,
    slot_tokens,
    cache_len,
    prefill_start,
    key_cache,
    value_cache,
    key_prefix,
    value_prefix,
    attn_gain,
    q_proj,
    k_proj,
    v_proj,
    q_gain,
    k_gain,
    o_proj,
    ffn_gain,
    w_gate,
    w_up,
    w_down,
    final_gain,
    lm_head,
):
    req_count = lax.axis_size("req")
    kv_count = lax.axis_size("kv")
    devices = req_count * kv_count
    rows_dev, width = hidden_in.shape
    kv_index = lax.axis_index("kv")
    self_index = lax.axis_index("req") * kv_count + kv_index
    kv_bits = bits_below(kv_count)
    near_bits = [bit for bit in bits_below(req_count) if bit < GROUP]

    head_dim = q_gain.shape[0]
    dec_count = cache_len.shape[0]
    tok_req = rows_dev * kv_count
    fresh_count = tok_req - dec_count
    places = jnp.concatenate(
        [prefill_start[0] + jnp.arange(fresh_count, dtype=jnp.int32), cache_len]
    ).astype(jnp.float32)
    cosines, sines = angle_tables(places, head_dim)
    cosines = jnp.concatenate([cosines, cosines], axis=1)
    sines = jnp.concatenate([-sines, sines], axis=1)

    cosines, sines = lax.optimization_barrier((cosines, sines))
    ready = sum(zero_after(each) for each in (cosines, sines))

    send_hot, slot_hot = routes(slot_tokens, self_index, devices, rows_dev, ready)
    sent = pick(send_hot, hidden_in)
    far_count = req_count // GROUP
    far_share = share_of(kv_index[None], width // kv_count, w_gate, w_up, w_down, sent)
    step = GROUP if far_count > 2 else GROUP // 2
    ring = [(i, (i + step) % req_count) for i in range(req_count)]
    far_shares = [far_share]
    for _ in range(max(2, far_count - 1)):
        far_shares.append(lax.ppermute(far_shares[-1], "req", ring))
    far_shares = far_shares[GROUP // step :]
    arrived = regroup(sent)
    owner_rows = pick(slot_hot, arrived)

    def project_block(diff):
        block_at = (kv_index ^ diff) * rows_dev
        tables = [lax.dynamic_slice_in_dim(table, block_at, rows_dev, 0) for table in (cosines, sines)]
        return project([blocks[diff]], attn_gain, *tables, q_gain, k_gain, q_proj, k_proj, v_proj)

    even = gather_xor(owner_rows, "kv", kv_bits[:0:-1])
    blocks = {0: owner_rows, 1: swap(owner_rows, "kv", 1)}
    parts = [project_block(0), project_block(1)]
    for diff in range(2, kv_count, 2):
        blocks[diff] = pin(even[diff], parts[1][2])
        blocks[diff + 1] = swap(blocks[diff], "kv", 1)
    for diff in range(2, kv_count):
        parts.append(project_block(diff))

    f32, bf16 = jnp.float32, jnp.bfloat16
    lens = jnp.concatenate([kv_index[None], prefill_start, cache_len]).astype(jnp.int32)
    follows, lasts, sums = parts[-1][2], {}, []
    for pair in range(kv_count // 2 - 1, -1, -1):
        sum_even, sum_odd, lasts[pair] = attend(
            pair,
            lens,
            parts,
            head_dim,
            key_prefix[0],
            value_prefix[0],
            o_proj,
            bf16 if pair else f32,
            follows,
        )
        if pair:
            both = sum_even.astype(f32) + swap(sum_odd, "kv", 1).astype(f32)
            follows = both.astype(bf16)
            sums.append(swap(follows, "kv", 2 * pair))
        else:
            sums.append(swap(pin(sum_odd, *sums), "kv", 1))
            own_sum = sum_even
    far_weights = [
        lax.all_gather(pin(held, own_sum, *sums[:-1]), "kv") for held in far_shares
    ]
    resid = owner_rows.astype(f32) + own_sum
    for each in sums:
        resid = resid + each.astype(f32)
    resid = resid.astype(bf16)
    ffn_in = norm_rows(resid, ffn_gain).astype(bf16)

    own_weights = (w_gate, w_up, w_down)
    near = {0: ffn_in, 1: swap(ffn_in, "req", 1), 2: swap(ffn_in, "req", 2)}

    last_sum = decode(
        lens,
        [lasts[pair] for pair in range(kv_count // 2)],
        head_dim,
        kv_count,
        o_proj,
        key_cache,
        value_cache,
        ffn_in,
    )
    last_raw = blocks[0][rows_dev - TAIL :]
    for diff in range(1, kv_count):
        is_last = (kv_index ^ diff) == kv_count - 1
        last_raw = jnp.where(is_last, blocks[diff][rows_dev - TAIL :], last_raw)
    last_resid = last_raw.astype(f32) + last_sum.astype(f32)
    for diff in range(1, kv_count):
        last_resid = last_resid + swap(last_sum, "kv", diff).astype(f32)
    last_resid = last_resid.astype(bf16)
    last_in = norm_rows(last_resid, ffn_gain).astype(bf16)

    last_near = gather_xor(last_in, "req", near_bits)
    lasts_in = [last_near[diff] for diff in range(GROUP)]

    zero = feed_forward([ffn_in], [f32], [own_weights], [last_sum])
    near[3] = swap(near[1], "req", 2)
    some = feed_forward([near[1], near[2]], [f32] * 2, [own_weights], [zero[0], *lasts_in])
    rest = feed_forward([near[3], *lasts_in], [f32] * (1 + GROUP), [own_weights], some[:1])
    first, second = feed_forward([near[1], near[2]], [bf16] * 2, far_weights, rest[:1], some)
    third, last_part, *last_parts = feed_forward(
        [near[3], *lasts_in], [bf16, f32] + [bf16] * (GROUP - 1), far_weights, [first], rest
    )
    backs = [swap(first, "req", 1), swap(second, "req", 2), swap(third, "req", 3)]
    (own_part,) = feed_forward([ffn_in], [f32], far_weights, [third, *backs[:2]], zero)
    for diff, part in enumerate(last_parts, 1):
        last_part = last_part + swap(part, "req", diff).astype(f32)
    last_rows = (last_resid.astype(f32) + last_part).astype(bf16)
    ffn_part = own_part
    for back in backs:
        ffn_part = ffn_part + back.astype(f32)
    out_rows = (resid.astype(f32) + ffn_part).astype(bf16)
    ends = jnp.where(kv_index == kv_count - 1, last_rows, out_rows[rows_dev - TAIL :])
    out_rows = jnp.concatenate([out_rows[: rows_dev - TAIL], ends], axis=0)
    returned = regroup(pick(slot_hot, out_rows, transposed=True))
    layer_out = pick(send_hot, returned, transposed=True)

    tail_count = dec_count + 1
    tails = pin(norm_rows(last_rows, final_gain).astype(bf16), own_part)
    req_bits = bits_below(req_count)
    for bit in req_bits:
        if bit == req_bits[-1]:
            tails = pin(tails, out_rows)
        tails = jnp.concatenate([tails, swap(tails, "req", bit)], axis=0)
    peaks = jnp.max(matmul(tails, lm_head), axis=1).reshape(req_count, TAIL)
    peaks = peaks[:, TAIL - tail_count :]
    owners = jnp.arange(req_count, dtype=jnp.int32)
    found = (owners[:, None] ^ owners[None, :]) == lax.axis_index("req")
    peaks = jnp.sum(jnp.where(found[:, :, None], peaks[None], 0.0), axis=1).reshape(1, -1)
    for axis, bits in (("kv", kv_bits), ("req", req_bits)):
        for bit in bits:
            peaks = jnp.maximum(peaks, swap(peaks, axis, bit))
    return (layer_out, peaks[0])


def solution(mesh):
    placed = (
        P(("req", "kv"), None),
        P(),
        P("req"),
        P("req"),
        P("req", None, "kv"),
        P("req", None, "kv"),
        P("req", None, "kv"),
        P("req", None, "kv"),
        P(),
        P(None, "kv"),
        P(None, "kv"),
        P(None, "kv"),
        P(),
        P(),
        P("kv", None),
        P(),
        P(None, "req"),
        P(None, "req"),
        P("req", None),
        P(),
        P(None, ("req", "kv")),
    )
    return jax.shard_map(
        shards, mesh=mesh, in_specs=placed, out_specs=(P(("req", "kv"), None), P()), check_vma=False
    )
```

```python
import functools
import math

import jax
import jax.numpy as jnp
from jax import lax
from jax.experimental import pallas as pl
from jax.experimental.pallas import tpu as pltpu
from jax.sharding import PartitionSpec as P

EPS = 1e-06
NEG = -1e30
GROUP = 4
TAIL = 16
DECODE_GROUP = 4
KEY_BLOCK = 512
VMEM_LIMIT = 56 * 1024 * 1024
BRIEF = pl.CostEstimate(flops=1, bytes_accessed=1, transcendentals=0)


def swap(value, axis, bit):
    size = lax.axis_size(axis)
    return lax.ppermute(value, axis, [(i, i ^ bit) for i in range(size)])


def bits_below(size):
    return [1 << i for i in range(size.bit_length() - 1)]


def gather_xor(value, axis, bits):
    held = {0: value}
    for bit in bits:
        held.update({diff ^ bit: swap(block, axis, bit) for diff, block in list(held.items())})
    return held


def zero_after(value):
    first = value[(0,) * value.ndim]
    return (first != first).astype(jnp.int32)


def pin(value, *others):
    anywhere = pl.BlockSpec(memory_space=pl.ANY)
    return pl.pallas_call(
        lambda *refs: None,
        out_shape=jax.ShapeDtypeStruct(value.shape, value.dtype),
        in_specs=[anywhere] * (1 + len(others)),
        out_specs=anywhere,
        input_output_aliases={0: 0},
        cost_estimate=BRIEF,
    )(value, *others)


def norm_rows(values, gain_vec):
    wide = values.astype(jnp.float32)
    return wide * lax.rsqrt(jnp.mean(wide * wide, axis=-1, keepdims=True) + EPS) * gain_vec


def angle_tables(places, head_dim):
    half_dim = head_dim // 2
    freqs = 1000000.0 ** (-(jnp.arange(half_dim, dtype=jnp.float32) * 2.0 / head_dim))
    angles = places[:, None] * freqs[None, :]
    return jnp.cos(angles), jnp.sin(angles)


def contract_last(left, right):
    return lax.dot_general(left, right, (((1,), (1,)), ((), ())), preferred_element_type=jnp.float32)


def whole_spec(shape):
    return pl.BlockSpec(shape, lambda *_: (0,) * len(shape))


def project_kernel(block_count, head_dim, *refs):
    row_refs = refs[:block_count]
    (gain_ref, cos_ref, sin_ref, q_gain_ref, k_gain_ref, wq_hbm, wk_hbm, wv_hbm) = refs[
        block_count : block_count + 8
    ]
    q_ref, k_ref, v_ref, wq, wk, wv, sems = refs[-7:]
    copies = [
        pltpu.make_async_copy(hbm, vmem, sems.at[at])
        for at, (hbm, vmem) in enumerate(((wq_hbm, wq), (wk_hbm, wk), (wv_hbm, wv)))
    ]
    for copy in copies:
        copy.start()
    normed = []
    for ref in row_refs:
        wide = ref[...].astype(jnp.float32)
        scale = lax.rsqrt(jnp.mean(wide * wide, axis=-1, keepdims=True) + EPS)
        normed.append((wide * scale * gain_ref[...]).astype(jnp.bfloat16))
    rows = jnp.concatenate(normed, axis=0)
    cosine, sine = cos_ref[...], sin_ref[...]

    def heads(raw, gain, out_ref):
        for at in range(raw.shape[1] // head_dim):
            head = raw[:, at * head_dim : (at + 1) * head_dim]
            scale = lax.rsqrt(jnp.mean(head * head, axis=-1, keepdims=True) + EPS)
            head = head * scale * gain
            turned = head * cosine + pltpu.roll(head, head_dim // 2, 1) * sine
            out_ref[:, at * head_dim : (at + 1) * head_dim] = turned.astype(jnp.bfloat16)

    copies[0].wait()
    heads(matmul(rows, wq[...]), q_gain_ref[...], q_ref)
    copies[1].wait()
    heads(matmul(rows, wk[...]), k_gain_ref[...], k_ref)
    copies[2].wait()
    v_ref[...] = matmul(rows, wv[...]).astype(jnp.bfloat16)


def project(blocks, gain, cosine, sine, q_gain, k_gain, q_proj, k_proj, v_proj, follows):
    head_dim = q_gain.shape[0]
    rows = sum(block.shape[0] for block in blocks)
    width = q_proj.shape[0]
    outs = (q_proj.shape[1], k_proj.shape[1], v_proj.shape[1])
    vectors = (gain[None, :], cosine, sine, q_gain[None, :], k_gain[None, :])
    return pl.pallas_call(
        functools.partial(project_kernel, len(blocks), head_dim),
        out_shape=[jax.ShapeDtypeStruct((rows, cols), jnp.bfloat16) for cols in outs],
        in_specs=[whole_spec(block.shape) for block in blocks]
        + [whole_spec(vector.shape) for vector in vectors]
        + [pl.BlockSpec(memory_space=pl.ANY)] * 4,
        out_specs=[whole_spec((rows, cols)) for cols in outs],
        grid=(1,),
        scratch_shapes=[pltpu.VMEM((width, cols), jnp.bfloat16) for cols in outs]
        + [pltpu.SemaphoreType.DMA((3,))],
        compiler_params=pltpu.CompilerParams(vmem_limit_bytes=VMEM_LIMIT),
        cost_estimate=BRIEF,
    )(*blocks, *vectors, q_proj, k_proj, v_proj, follows)


def share_kernel(share, tile, index_ref, gate, up, down, _, out, sems):
    at = pl.ds(pl.multiple_of(index_ref[0] * share, share), share)
    hidden = gate.shape[1]
    copies = [(gate.at[at, :], out.at[pl.ds(0, share), pl.ds(0, hidden)])]
    copies.append((up.at[at, :], out.at[pl.ds(0, share), pl.ds(hidden, hidden)]))
    for step in range(hidden // tile):
        rows, lanes = pl.ds(step * tile, tile), pl.ds(step * share, share)
        copies.append((down.at[rows, at], out.at[pl.ds(share, tile), lanes]))
    copies = [pltpu.make_async_copy(*ends, sems.at[at]) for at, ends in enumerate(copies)]
    for copy in copies:
        copy.start()
    for copy in copies:
        copy.wait()


def share_of(index, share, gate, up, down, follows):
    hidden = gate.shape[1]
    tile = share // 2
    return pl.pallas_call(
        functools.partial(share_kernel, share, tile),
        out_shape=jax.ShapeDtypeStruct((share + tile, 2 * hidden), gate.dtype),
        in_specs=[pl.BlockSpec(memory_space=pltpu.SMEM)] + [pl.BlockSpec(memory_space=pl.ANY)] * 4,
        out_specs=pl.BlockSpec(memory_space=pltpu.VMEM),
        scratch_shapes=[pltpu.SemaphoreType.DMA((2 + hidden // tile,))],
        cost_estimate=BRIEF,
    )(index, gate, up, down, follows)


def attend_kernel(pair, block_count, head_dim, lens_ref, *refs):
    q_refs, refs = refs[:2], refs[2:]
    k_refs, refs = refs[:block_count], refs[block_count:]
    v_refs, refs = refs[:block_count], refs[block_count:]
    sources, refs = refs[:3], refs[3 + 1 :]
    even_ref, *odd_refs, last_ref, k_all, v_all, peak, acc, attended, kp, vp, weight, sems = refs
    copies = [
        pltpu.make_async_copy(source, target, sems.at[at])
        for at, (source, target) in enumerate(zip(sources, (kp, vp, weight)))
    ]
    for copy in copies:
        copy.start()
    kv_index, start = lens_ref[0], lens_ref[1]
    rows, q_cols = q_refs[0].shape
    kv_cols = k_all.shape[1]
    group = q_cols // kv_cols
    heads = q_cols // head_dim
    span = 2 * rows
    scale = head_dim**-0.5 * math.log2(math.e)
    for refs, whole in ((k_refs, k_all), (v_refs, v_all)):
        for at, ref in enumerate(refs):
            whole[at * rows : (at + 1) * rows, :] = ref[...]
    queries = [
        jnp.concatenate([ref[:, head * head_dim : (head + 1) * head_dim] for ref in q_refs], axis=0)
        for head in range(heads)
    ]
    peak[...] = jnp.full(peak.shape, NEG, jnp.float32)
    acc[...] = jnp.zeros(acc.shape, jnp.float32)

    def absorb(keys_ref, values_ref, place, size, allowed):
        for head in range(heads):
            lanes = slice(head // group * head_dim, (head // group + 1) * head_dim)
            keys = keys_ref[pl.ds(place, size), lanes]
            values = values_ref[pl.ds(place, size), lanes]
            wide = jnp.concatenate([values, jnp.ones_like(values)], axis=1)
            scores = contract_last(queries[head], keys)
            if allowed is not None:
                scores = jnp.where(allowed, scores, NEG)
            old = peak[head][:, :1]
            new = jnp.maximum(old, jnp.max(scores, axis=1, keepdims=True))
            weights = jnp.exp2((scores - new) * scale).astype(jnp.bfloat16)
            acc[head] = acc[head] * jnp.exp2((old - new) * scale) + matmul(weights, wide)
            peak[head] = jnp.broadcast_to(new, peak.shape[1:])

    turned = kv_index % 2

    def order(axis):
        ids = lax.broadcasted_iota(jnp.int32, (span, span), axis)
        swapped = jnp.where(ids < rows, ids + rows, ids - rows)
        return jnp.where(turned == 1, swapped, ids)

    absorb(k_all, v_all, pair * span, span, order(1) <= order(0))

    def fresh_block(at, carry):
        @pl.when(((kv_index // 2) ^ at) < ((kv_index // 2) ^ pair))
        def _():
            absorb(k_all, v_all, pl.multiple_of(at * span, span), span, None)

        return carry

    lax.fori_loop(0, block_count // 2, fresh_block, 0)
    copies[0].wait()
    copies[1].wait()
    full = start // KEY_BLOCK

    def prefix_block(at, carry):
        absorb(kp, vp, pl.multiple_of(at * KEY_BLOCK, KEY_BLOCK), KEY_BLOCK, None)
        return carry

    lax.fori_loop(0, full, prefix_block, 0)

    @pl.when(full * KEY_BLOCK < start)
    def _():
        place = pl.multiple_of(full * KEY_BLOCK, KEY_BLOCK)
        ids = lax.broadcasted_iota(jnp.int32, (span, KEY_BLOCK), 1)
        absorb(kp, vp, place, KEY_BLOCK, ids < start - place)

    for head in range(heads):
        attended[:, head * head_dim : (head + 1) * head_dim] = (
            acc[head][:, :head_dim] / acc[head][:, head_dim:]
        ).astype(jnp.bfloat16)
    copies[2].wait()
    width = weight.shape[1]
    for at in range(0, width, q_cols):
        part = matmul(attended[...], weight[:, at : at + q_cols])
        even_ref[:, at : at + q_cols] = part[:rows].astype(even_ref.dtype)
        for half, odd_ref in enumerate(odd_refs):
            here = rows + half * (rows // 2)
            odd_ref[:, at : at + q_cols] = part[here : here + rows // 2].astype(odd_ref.dtype)
    last = kv_index ^ (block_count - 1)
    here = pl.multiple_of((last % 2) * rows + rows - TAIL, TAIL)
    last_ref[:, :q_cols] = attended[pl.ds(here, TAIL), :]
    ends = [ref[rows - TAIL :, :] for ref in q_refs]
    last_ref[:, q_cols : 2 * q_cols] = jnp.where(last % 2 == 1, ends[1], ends[0])
    there = pl.ds(pl.multiple_of(last * rows + rows - TAIL, TAIL), TAIL)
    last_ref[:, 2 * q_cols : 2 * q_cols + kv_cols] = k_all[there, :]
    last_ref[:, 2 * q_cols + kv_cols :] = v_all[there, :]


def attend(pair, lens, parts, head_dim, key_prefix, value_prefix, o_proj, even_type, follows):
    block_count = len(parts)
    queries, keys, values = [[part[at] for part in parts] for at in range(3)]
    queries = queries[2 * pair : 2 * pair + 2]
    rows, q_cols = queries[0].shape
    kv_cols = keys[0].shape[1]
    width = o_proj.shape[1]
    heads = q_cols // head_dim
    outs = [
        jax.ShapeDtypeStruct((rows, width), even_type),
        jax.ShapeDtypeStruct((rows // 2, width), jnp.bfloat16),
        jax.ShapeDtypeStruct((rows // 2, width), jnp.bfloat16),
        jax.ShapeDtypeStruct((TAIL, 2 * q_cols + 2 * kv_cols), jnp.bfloat16),
    ]
    return pl.pallas_call(
        functools.partial(attend_kernel, pair, block_count, head_dim),
        out_shape=outs,
        grid_spec=pltpu.PrefetchScalarGridSpec(
            num_scalar_prefetch=1,
            grid=(1,),
            in_specs=[whole_spec(part.shape) for part in queries + keys + values]
            + [pl.BlockSpec(memory_space=pl.ANY)] * 4,
            out_specs=[whole_spec(out.shape) for out in outs],
            scratch_shapes=[
                pltpu.VMEM((rows * block_count, kv_cols), jnp.bfloat16),
                pltpu.VMEM((rows * block_count, kv_cols), jnp.bfloat16),
                pltpu.VMEM((heads, 2 * rows, head_dim), jnp.float32),
                pltpu.VMEM((heads, 2 * rows, 2 * head_dim), jnp.float32),
                pltpu.VMEM((2 * rows, q_cols), jnp.bfloat16),
                pltpu.VMEM(key_prefix.shape, jnp.bfloat16),
                pltpu.VMEM(value_prefix.shape, jnp.bfloat16),
                pltpu.VMEM(o_proj.shape, jnp.bfloat16),
                pltpu.SemaphoreType.DMA((3,)),
            ],
        ),
        compiler_params=pltpu.CompilerParams(vmem_limit_bytes=VMEM_LIMIT),
        cost_estimate=BRIEF,
    )(lens, *queries, *keys, *values, key_prefix, value_prefix, o_proj, follows)


def decode_kernel(pairs, block_count, head_dim, q_cols, kv_cols, lens_ref, *refs):
    last_refs, refs = refs[:pairs], refs[pairs:]
    o_hbm, kc_hbm, vc_hbm, out_ref, kc, vc, weight, dec_in, dec_out, sems, weight_sem = refs
    kv_index = lens_ref[0]
    dec_count, slots = kc.shape[:2]
    group = q_cols // kv_cols
    kv_heads = kv_cols // head_dim
    heads = q_cols // head_dim
    scale = head_dim**-0.5 * math.log2(math.e)
    sizes = (slots // 4, slots // 2, slots)

    def by_size(together, act):
        first = together * DECODE_GROUP
        length = lens_ref[2 + first]
        for at in range(1, DECODE_GROUP):
            length = jnp.maximum(length, lens_ref[2 + first + at])
        for at, size in enumerate(sizes):
            fits = length <= size
            if at:
                fits = fits & (length > sizes[at - 1])
            pl.when(fits)(functools.partial(act, first, size))

    def cache_copies(request, size):
        return (
            pltpu.make_async_copy(
                kc_hbm.at[request, pl.ds(0, size)], kc.at[request, pl.ds(0, size)], sems.at[0, request]
            ),
            pltpu.make_async_copy(
                vc_hbm.at[request, pl.ds(0, size)], vc.at[request, pl.ds(0, size)], sems.at[1, request]
            ),
        )

    def start_copies(first, size):
        for at in range(DECODE_GROUP):
            for copy in cache_copies(first + at, size):
                copy.start()

    for together in range(dec_count // DECODE_GROUP):
        by_size(together, start_copies)
    weight_copy = pltpu.make_async_copy(o_hbm, weight, weight_sem)
    weight_copy.start()
    held = last_refs[0][...]
    for at in range(1, pairs):
        held = jnp.where((kv_index ^ (block_count - 1)) // 2 == at, last_refs[at][...], held)
    rows_in = held[TAIL - dec_count :, q_cols:].astype(jnp.float32)
    for request in range(dec_count):
        dec_in[request] = rows_in[request : request + 1]

    def attend_some(first, size):
        for at in range(DECODE_GROUP):
            attend_one(first + at, size)

    def attend_one(request, size):
        for copy in cache_copies(request, size):
            copy.wait()
        row = dec_in[request]
        empty = jnp.zeros((1, head_dim), jnp.float32)
        spread = []
        for at in range(heads):
            parts = [empty] * kv_heads
            parts[at // group] = row[:, at * head_dim : (at + 1) * head_dim]
            spread.append(jnp.concatenate(parts, axis=1))
        spread += [jnp.zeros((1, kv_cols), jnp.float32)] * (8 - len(spread))
        q_rows = jnp.concatenate(spread, axis=0)
        key_self = row[:, q_cols : q_cols + kv_cols]
        value_self = row[:, q_cols + kv_cols :]
        past = contract_last(q_rows.astype(jnp.bfloat16), kc[request, :size, :])
        ids = lax.broadcasted_iota(jnp.int32, past.shape, 1)
        past = jnp.where(ids < lens_ref[2 + request], past, NEG)
        own = jnp.sum(q_rows * key_self, axis=1, keepdims=True)
        top = jnp.maximum(jnp.max(past, axis=1, keepdims=True), own)
        past = jnp.exp2((past - top) * scale)
        own = jnp.exp2((own - top) * scale)
        total = jnp.sum(past, axis=1, keepdims=True) + own
        past = (past / total).astype(jnp.bfloat16)
        own = (own / total).astype(jnp.bfloat16).astype(jnp.float32)
        summed = matmul(past, vc[request, :size, :]) + own * value_self
        outs = []
        for at in range(heads):
            lane = (at // group) * head_dim
            outs.append(summed[at : at + 1, lane : lane + head_dim])
        dec_out[request] = jnp.concatenate(outs, axis=1)

    for together in range(dec_count // DECODE_GROUP):
        by_size(together, attend_some)
    done = [dec_out[request] for request in range(dec_count)]
    rows = jnp.concatenate([held[: TAIL - dec_count, :q_cols].astype(jnp.float32)] + done, axis=0)
    weight_copy.wait()
    out_ref[...] = matmul(rows.astype(jnp.bfloat16), weight[...]).astype(jnp.bfloat16)


def decode(lens, lasts, head_dim, block_count, o_proj, key_cache, value_cache, follows):
    dec_count, slots, kv_cols = key_cache.shape
    q_cols, width = o_proj.shape
    pairs = len(lasts)

    def kernel(lens_ref, *refs):
        given = pairs + 3
        decode_kernel(
            pairs, block_count, head_dim, q_cols, kv_cols, lens_ref, *refs[:given], *refs[given + 1 :]
        )

    return pl.pallas_call(
        kernel,
        out_shape=jax.ShapeDtypeStruct((TAIL, width), jnp.bfloat16),
        grid_spec=pltpu.PrefetchScalarGridSpec(
            num_scalar_prefetch=1,
            grid=(1,),
            in_specs=[whole_spec(last.shape) for last in lasts]
            + [pl.BlockSpec(memory_space=pl.ANY)] * 4,
            out_specs=whole_spec((TAIL, width)),
            scratch_shapes=[
                pltpu.VMEM((dec_count, slots, kv_cols), jnp.bfloat16),
                pltpu.VMEM((dec_count, slots, kv_cols), jnp.bfloat16),
                pltpu.VMEM(o_proj.shape, jnp.bfloat16),
                pltpu.VMEM((dec_count, 1, q_cols + 2 * kv_cols), jnp.float32),
                pltpu.VMEM((dec_count, 1, q_cols), jnp.float32),
                pltpu.SemaphoreType.DMA((2, dec_count)),
                pltpu.SemaphoreType.DMA,
            ],
        ),
        compiler_params=pltpu.CompilerParams(vmem_limit_bytes=VMEM_LIMIT),
        cost_estimate=BRIEF,
    )(lens, *lasts, o_proj, key_cache, value_cache, follows)


def feed_kernel(tiles, counts, added, *refs):
    pieces = len(counts)
    x_refs, refs = refs[:pieces], refs[pieces:]
    add_refs, refs = refs[:added], refs[added:]
    weight_refs, refs = refs[: len(refs) - 2 - pieces], refs[len(refs) - 2 - pieces :]
    out_refs, (x_all, total) = refs[:pieces], refs[pieces:]
    step = pl.program_id(0)
    cuts = [sum(counts[:at]) for at in range(pieces + 1)]

    @pl.when(step == 0)
    def _():
        for at, ref in enumerate(x_refs):
            x_all[cuts[at] : cuts[at + 1], :] = ref[...]
        for at, ref in enumerate(add_refs):
            total[cuts[at] : cuts[at + 1], :] = ref[...]

    sets = len(weight_refs) // 3
    for at in range(sets):
        gate_ref, up_ref, down_ref = weight_refs[3 * at : 3 * at + 3]

        @pl.when(step // tiles == at)
        def _():
            rows = x_all[...]
            tile = gate_ref.shape[-1]
            gate = matmul(rows, gate_ref[...].reshape(-1, tile))
            up = matmul(rows, up_ref[...].reshape(-1, tile))
            act = (gate / (1.0 + jnp.exp(-gate)) * up).astype(jnp.bfloat16)
            if len(down_ref.shape) == 2:
                downs = [down_ref[...]]
            else:
                downs = [down_ref[part] for part in range(down_ref.shape[0])]
            lane = 0
            for down in downs:
                lanes = slice(lane, lane + down.shape[1])
                lane += down.shape[1]
                part = matmul(act, down)
                if at or added:
                    total[:, lanes] += part
                else:
                    total[:, lanes] = jnp.where(step == 0, part, total[:, lanes] + part)

    @pl.when(step == sets * tiles - 1)
    def _():
        for at, ref in enumerate(out_refs):
            ref[...] = total[cuts[at] : cuts[at + 1], :].astype(ref.dtype)


def feed_forward(blocks, dtypes, weights, follows, adds=()):
    counts = [block.shape[0] for block in blocks]
    size, width = sum(counts), blocks[0].shape[1]
    held = weights[0]
    hidden = held[0].shape[1] if isinstance(held, tuple) else held.shape[2] // 2
    tile = 256 if hidden % 256 == 0 else 128
    tiles = hidden // tile
    specs, operands = [], []
    for at, held in enumerate(weights):

        def place(step, at=at):
            return jnp.clip(step - at * tiles, 0, tiles - 1)

        if isinstance(held, tuple):
            specs += [
                pl.BlockSpec((width, tile), lambda step, place=place: (0, place(step))),
                pl.BlockSpec((width, tile), lambda step, place=place: (0, place(step))),
                pl.BlockSpec((tile, width), lambda step, place=place: (place(step), 0)),
            ]
            operands += held
            continue
        shares = held.shape[0]
        share = width // shares
        specs += [
            pl.BlockSpec((shares, share, tile), lambda step, place=place: (0, 0, place(step))),
            pl.BlockSpec((shares, share, tile), lambda step, place=place: (0, 0, tiles + place(step))),
            pl.BlockSpec(
                (shares, tile, share),
                lambda step, place=place, below=share // tile: (0, below, place(step)),
            ),
        ]
        operands += [held] * 3

    def kernel(*refs):
        given = len(blocks) + len(adds) + len(operands)
        feed_kernel(tiles, counts, len(adds), *refs[:given], *refs[given + len(follows) :])

    return pl.pallas_call(
        kernel,
        out_shape=[
            jax.ShapeDtypeStruct((count, width), dtype) for count, dtype in zip(counts, dtypes)
        ],
        grid=(len(weights) * tiles,),
        in_specs=[whole_spec(block.shape) for block in blocks]
        + [whole_spec(add.shape) for add in adds]
        + specs
        + [pl.BlockSpec(memory_space=pl.ANY)] * len(follows),
        out_specs=[whole_spec((count, width)) for count in counts],
        scratch_shapes=[
            pltpu.VMEM((size, width), jnp.bfloat16),
            pltpu.VMEM((size, width), jnp.float32),
        ],
        compiler_params=pltpu.CompilerParams(vmem_limit_bytes=VMEM_LIMIT),
        cost_estimate=BRIEF,
    )(*blocks, *adds, *operands, *follows)


def regroup(rows_in):
    return lax.all_to_all(rows_in, ("req", "kv"), split_axis=0, concat_axis=0, tiled=True)


def matmul(left, right):
    return jnp.dot(left, right, preferred_element_type=jnp.float32)


def routes(slot_tokens, self_index, devices, rows_dev, ready):
    per_pair = rows_dev // devices
    slot_table = slot_tokens.reshape(devices, rows_dev)
    source = slot_table // rows_dev
    places = jnp.arange(rows_dev, dtype=jnp.int32)
    before = (places[:, None] < places[None, :]).astype(jnp.bfloat16)
    from_self = source == self_index
    rank = matmul(from_self.astype(jnp.bfloat16), before).astype(jnp.int32)
    local = slot_table - self_index * rows_dev
    ranked = jnp.where(from_self, rank, -1)[:, None, :] == jnp.arange(per_pair, dtype=jnp.int32)[None, :, None]
    send_rows = jnp.sum(jnp.where(ranked, local[:, None, :], 0), axis=2).reshape(-1)
    send_hot = (send_rows[:, None] == places[None, :]).astype(jnp.bfloat16)
    own = lax.dynamic_index_in_dim(source, self_index, 0, keepdims=False)
    earlier = (own[:, None] == own[None, :]) & (places[:, None] > places[None, :])
    own_rank = jnp.sum(earlier.astype(jnp.int32), axis=1)
    slot_hot = ((own * per_pair + own_rank + ready)[:, None] == places[None, :]).astype(jnp.bfloat16)
    return send_hot, slot_hot


def pick(hot, rows, transposed=False):
    if transposed:
        return lax.dot_general(
            hot, rows, (((0,), (0,)), ((), ())), preferred_element_type=jnp.float32
        ).astype(rows.dtype)
    return matmul(hot, rows).astype(rows.dtype)


def shards(
    hidden_in,
    slot_tokens,
    cache_len,
    prefill_start,
    key_cache,
    value_cache,
    key_prefix,
    value_prefix,
    attn_gain,
    q_proj,
    k_proj,
    v_proj,
    q_gain,
    k_gain,
    o_proj,
    ffn_gain,
    w_gate,
    w_up,
    w_down,
    final_gain,
    lm_head,
):
    req_count = lax.axis_size("req")
    kv_count = lax.axis_size("kv")
    devices = req_count * kv_count
    rows_dev, width = hidden_in.shape
    kv_index = lax.axis_index("kv")
    self_index = lax.axis_index("req") * kv_count + kv_index
    kv_bits = bits_below(kv_count)
    near_bits = [bit for bit in bits_below(req_count) if bit < GROUP]

    head_dim = q_gain.shape[0]
    dec_count = cache_len.shape[0]
    tok_req = rows_dev * kv_count
    fresh_count = tok_req - dec_count
    places = jnp.concatenate(
        [prefill_start[0] + jnp.arange(fresh_count, dtype=jnp.int32), cache_len]
    ).astype(jnp.float32)
    cosines, sines = angle_tables(places, head_dim)
    cosines = jnp.concatenate([cosines, cosines], axis=1)
    sines = jnp.concatenate([-sines, sines], axis=1)

    cosines, sines = lax.optimization_barrier((cosines, sines))
    ready = sum(zero_after(each) for each in (cosines, sines))

    send_hot, slot_hot = routes(slot_tokens, self_index, devices, rows_dev, ready)
    sent = pick(send_hot, hidden_in)
    far_count = req_count // GROUP
    far_share = share_of(kv_index[None], width // kv_count, w_gate, w_up, w_down, sent)
    step = GROUP if far_count > 2 else GROUP // 2
    ring = [(i, (i + step) % req_count) for i in range(req_count)]
    far_hops = [far_share]
    for _ in range(max(2, far_count - 1)):
        far_hops.append(lax.ppermute(far_hops[-1], "req", ring))
    far_shares = far_hops[GROUP // step :]
    arrived = regroup(sent)
    owner_rows = pick(slot_hot, arrived)

    def project_block(diff, follows):
        block_at = (kv_index ^ diff) * rows_dev
        tables = [lax.dynamic_slice_in_dim(table, block_at, rows_dev, 0) for table in (cosines, sines)]
        return project(
            [blocks[diff]], attn_gain, *tables, q_gain, k_gain, q_proj, k_proj, v_proj, follows
        )

    even = gather_xor(owner_rows, "kv", kv_bits[:0:-1])
    blocks = {0: owner_rows, 1: swap(owner_rows, "kv", 1)}
    parts = [project_block(0, owner_rows)]
    parts.append(project_block(1, parts[0][2]))
    for diff in range(2, kv_count, 2):
        blocks[diff] = pin(even[diff], parts[1][2])
        blocks[diff + 1] = swap(blocks[diff], "kv", 1)
    for diff in range(2, kv_count):
        parts.append(project_block(diff, far_hops[1] if diff == 2 else parts[-1][2]))

    f32, bf16 = jnp.float32, jnp.bfloat16
    lens = jnp.concatenate([kv_index[None], prefill_start, cache_len]).astype(jnp.int32)
    follows, lasts, sums = parts[-1][2], {}, []
    for pair in range(kv_count // 2 - 1, -1, -1):
        sum_even, *sum_odd, lasts[pair] = attend(
            pair,
            lens,
            parts,
            head_dim,
            key_prefix[0],
            value_prefix[0],
            o_proj,
            bf16 if pair else f32,
            follows,
        )
        if pair:
            other = jnp.concatenate([swap(half, "kv", 1) for half in sum_odd], axis=0)
            both = sum_even.astype(f32) + other.astype(f32)
            follows = both.astype(bf16)
            sums.append(swap(follows, "kv", 2 * pair))
        else:
            halves = [swap(pin(half, *sums, *far_shares), "kv", 1) for half in sum_odd]
            sums.append(jnp.concatenate(halves, axis=0))
            own_sum = sum_even
    far_weights = [
        lax.all_gather(pin(held, own_sum), "kv") for held in far_shares
    ]
    resid = owner_rows.astype(f32) + own_sum
    for each in sums:
        resid = resid + each.astype(f32)
    resid = resid.astype(bf16)
    ffn_in = norm_rows(resid, ffn_gain).astype(bf16)

    own_weights = (w_gate, w_up, w_down)
    near = {0: ffn_in, 1: swap(ffn_in, "req", 1), 2: swap(ffn_in, "req", 2)}

    last_sum = decode(
        lens,
        [lasts[pair] for pair in range(kv_count // 2)],
        head_dim,
        kv_count,
        o_proj,
        key_cache,
        value_cache,
        ffn_in,
    )
    last_raw = blocks[0][rows_dev - TAIL :]
    for diff in range(1, kv_count):
        is_last = (kv_index ^ diff) == kv_count - 1
        last_raw = jnp.where(is_last, blocks[diff][rows_dev - TAIL :], last_raw)
    last_resid = last_raw.astype(f32) + last_sum.astype(f32)
    for diff in range(1, kv_count):
        last_resid = last_resid + swap(last_sum, "kv", diff).astype(f32)
    last_resid = last_resid.astype(bf16)
    last_in = norm_rows(last_resid, ffn_gain).astype(bf16)

    last_near = gather_xor(last_in, "req", near_bits)
    lasts_in = [last_near[diff] for diff in range(GROUP)]

    zero = feed_forward([ffn_in], [f32], [own_weights], [last_sum])
    near[3] = swap(near[1], "req", 2)
    some = feed_forward([near[1], near[2]], [f32] * 2, [own_weights], [zero[0], last_near[1]])
    rest = feed_forward([near[3], *lasts_in], [f32] * (1 + GROUP), [own_weights], some[:1])
    first, second = feed_forward([near[1], near[2]], [bf16] * 2, far_weights, rest[:1], some)
    third, last_part, *last_parts = feed_forward(
        [near[3], *lasts_in], [bf16, f32] + [bf16] * (GROUP - 1), far_weights, [first], rest
    )
    backs = [swap(first, "req", 1), swap(second, "req", 2), swap(third, "req", 3)]
    (own_part,) = feed_forward([ffn_in], [f32], far_weights, [third, backs[0][:TAIL], backs[1][:TAIL]], zero)
    last_part = pin(last_part, own_part)
    for diff, part in enumerate(last_parts, 1):
        last_part = last_part + swap(part, "req", diff).astype(f32)
    last_rows = (last_resid.astype(f32) + last_part).astype(bf16)
    ffn_part = own_part
    for back in backs:
        ffn_part = ffn_part + back.astype(f32)
    out_rows = (resid.astype(f32) + ffn_part).astype(bf16)
    ends = jnp.where(kv_index == kv_count - 1, last_rows, out_rows[rows_dev - TAIL :])
    out_rows = jnp.concatenate([out_rows[: rows_dev - TAIL], ends], axis=0)
    returned = regroup(pick(slot_hot, out_rows, transposed=True))
    layer_out = pick(send_hot, returned, transposed=True)

    tail_count = dec_count + 1
    tails = norm_rows(last_rows, final_gain).astype(bf16)
    req_bits = bits_below(req_count)
    for bit in req_bits:
        tails = jnp.concatenate([tails, swap(tails, "req", bit)], axis=0)
    tails = pin(tails, out_rows)
    peaks = jnp.max(matmul(tails, lm_head), axis=1).reshape(req_count, TAIL)
    peaks = peaks[:, TAIL - tail_count :]
    owners = jnp.arange(req_count, dtype=jnp.int32)
    found = (owners[:, None] ^ owners[None, :]) == lax.axis_index("req")
    peaks = jnp.sum(jnp.where(found[:, :, None], peaks[None], 0.0), axis=1).reshape(1, -1)
    for axis, bits in (("kv", kv_bits), ("req", req_bits)):
        for bit in bits:
            peaks = jnp.maximum(peaks, swap(peaks, axis, bit))
    return (layer_out, peaks[0])


def solution(mesh):
    placed = (
        P(("req", "kv"), None),
        P(),
        P("req"),
        P("req"),
        P("req", None, "kv"),
        P("req", None, "kv"),
        P("req", None, "kv"),
        P("req", None, "kv"),
        P(),
        P(None, "kv"),
        P(None, "kv"),
        P(None, "kv"),
        P(),
        P(),
        P("kv", None),
        P(),
        P(None, "req"),
        P(None, "req"),
        P("req", None),
        P(),
        P(None, ("req", "kv")),
    )
    return jax.shard_map(
        shards, mesh=mesh, in_specs=placed, out_specs=(P(("req", "kv"), None), P()), check_vma=False
    )
```

```python
import functools
import math

import jax
import jax.numpy as jnp
from jax import lax
from jax.experimental import pallas as pl
from jax.experimental.pallas import tpu as pltpu
from jax.sharding import PartitionSpec as P

EPS = 1e-06
NEG = -1e30
GROUP = 4
TAIL = 16
DECODE_GROUP = 4
KEY_BLOCK = 512
VMEM_LIMIT = 56 * 1024 * 1024
BRIEF = pl.CostEstimate(flops=1, bytes_accessed=1, transcendentals=0)


def swap(value, axis, bit):
    size = lax.axis_size(axis)
    return lax.ppermute(value, axis, [(i, i ^ bit) for i in range(size)])


def bits_below(size):
    return [1 << i for i in range(size.bit_length() - 1)]


def gather_xor(value, axis, bits):
    held = {0: value}
    for bit in bits:
        held.update({diff ^ bit: swap(block, axis, bit) for diff, block in list(held.items())})
    return held


def zero_after(value):
    first = value[(0,) * value.ndim]
    return (first != first).astype(jnp.int32)


def pin(value, *others):
    anywhere = pl.BlockSpec(memory_space=pl.ANY)
    return pl.pallas_call(
        lambda *refs: None,
        out_shape=jax.ShapeDtypeStruct(value.shape, value.dtype),
        in_specs=[anywhere] * (1 + len(others)),
        out_specs=anywhere,
        input_output_aliases={0: 0},
        cost_estimate=BRIEF,
    )(value, *others)


def norm_rows(values, gain_vec):
    wide = values.astype(jnp.float32)
    return wide * lax.rsqrt(jnp.mean(wide * wide, axis=-1, keepdims=True) + EPS) * gain_vec


def angle_tables(places, head_dim):
    half_dim = head_dim // 2
    freqs = 1000000.0 ** (-(jnp.arange(half_dim, dtype=jnp.float32) * 2.0 / head_dim))
    angles = places[:, None] * freqs[None, :]
    return jnp.cos(angles), jnp.sin(angles)


def contract_last(left, right):
    return lax.dot_general(left, right, (((1,), (1,)), ((), ())), preferred_element_type=jnp.float32)


def whole_spec(shape):
    return pl.BlockSpec(shape, lambda *_: (0,) * len(shape))


def project_kernel(block_count, head_dim, *refs):
    row_refs = refs[:block_count]
    (gain_ref, cos_ref, sin_ref, q_gain_ref, k_gain_ref, wq_hbm, wk_hbm, wv_hbm) = refs[
        block_count : block_count + 8
    ]
    q_ref, k_ref, v_ref, wq, wk, wv, sems = refs[-7:]
    copies = [
        pltpu.make_async_copy(hbm, vmem, sems.at[at])
        for at, (hbm, vmem) in enumerate(((wq_hbm, wq), (wk_hbm, wk), (wv_hbm, wv)))
    ]
    for copy in copies:
        copy.start()
    normed = []
    for ref in row_refs:
        wide = ref[...].astype(jnp.float32)
        scale = lax.rsqrt(jnp.mean(wide * wide, axis=-1, keepdims=True) + EPS)
        normed.append((wide * scale * gain_ref[...]).astype(jnp.bfloat16))
    rows = jnp.concatenate(normed, axis=0)
    cosine, sine = cos_ref[...], sin_ref[...]

    def heads(raw, gain, out_ref):
        for at in range(raw.shape[1] // head_dim):
            head = raw[:, at * head_dim : (at + 1) * head_dim]
            scale = lax.rsqrt(jnp.mean(head * head, axis=-1, keepdims=True) + EPS)
            head = head * scale * gain
            turned = head * cosine + pltpu.roll(head, head_dim // 2, 1) * sine
            out_ref[:, at * head_dim : (at + 1) * head_dim] = turned.astype(jnp.bfloat16)

    copies[0].wait()
    heads(matmul(rows, wq[...]), q_gain_ref[...], q_ref)
    copies[1].wait()
    heads(matmul(rows, wk[...]), k_gain_ref[...], k_ref)
    copies[2].wait()
    v_ref[...] = matmul(rows, wv[...]).astype(jnp.bfloat16)


def project(blocks, gain, cosine, sine, q_gain, k_gain, q_proj, k_proj, v_proj, follows):
    head_dim = q_gain.shape[0]
    rows = sum(block.shape[0] for block in blocks)
    width = q_proj.shape[0]
    outs = (q_proj.shape[1], k_proj.shape[1], v_proj.shape[1])
    vectors = (gain[None, :], cosine, sine, q_gain[None, :], k_gain[None, :])
    return pl.pallas_call(
        functools.partial(project_kernel, len(blocks), head_dim),
        out_shape=[jax.ShapeDtypeStruct((rows, cols), jnp.bfloat16) for cols in outs],
        in_specs=[whole_spec(block.shape) for block in blocks]
        + [whole_spec(vector.shape) for vector in vectors]
        + [pl.BlockSpec(memory_space=pl.ANY)] * 4,
        out_specs=[whole_spec((rows, cols)) for cols in outs],
        grid=(1,),
        scratch_shapes=[pltpu.VMEM((width, cols), jnp.bfloat16) for cols in outs]
        + [pltpu.SemaphoreType.DMA((3,))],
        compiler_params=pltpu.CompilerParams(vmem_limit_bytes=VMEM_LIMIT),
        cost_estimate=BRIEF,
    )(*blocks, *vectors, q_proj, k_proj, v_proj, follows)


def share_kernel(share, tile, index_ref, gate, up, down, _, out, sems):
    at = pl.ds(pl.multiple_of(index_ref[0] * share, share), share)
    hidden = gate.shape[1]
    copies = [(gate.at[at, :], out.at[pl.ds(0, share), pl.ds(0, hidden)])]
    copies.append((up.at[at, :], out.at[pl.ds(0, share), pl.ds(hidden, hidden)]))
    for step in range(hidden // tile):
        rows, lanes = pl.ds(step * tile, tile), pl.ds(step * share, share)
        copies.append((down.at[rows, at], out.at[pl.ds(share, tile), lanes]))
    copies = [pltpu.make_async_copy(*ends, sems.at[at]) for at, ends in enumerate(copies)]
    for copy in copies:
        copy.start()
    for copy in copies:
        copy.wait()


def share_of(index, share, gate, up, down, follows):
    hidden = gate.shape[1]
    tile = share // 2
    return pl.pallas_call(
        functools.partial(share_kernel, share, tile),
        out_shape=jax.ShapeDtypeStruct((share + tile, 2 * hidden), gate.dtype),
        in_specs=[pl.BlockSpec(memory_space=pltpu.SMEM)] + [pl.BlockSpec(memory_space=pl.ANY)] * 4,
        out_specs=pl.BlockSpec(memory_space=pltpu.VMEM),
        scratch_shapes=[pltpu.SemaphoreType.DMA((2 + hidden // tile,))],
        cost_estimate=BRIEF,
    )(index, gate, up, down, follows)


def attend_kernel(pair, block_count, head_dim, lens_ref, *refs):
    q_refs, refs = refs[:2], refs[2:]
    k_refs, refs = refs[:block_count], refs[block_count:]
    v_refs, refs = refs[:block_count], refs[block_count:]
    sources, refs = refs[:3], refs[3 + 1 :]
    even_ref, *odd_refs, last_ref, k_all, v_all, peak, acc, attended, kp, vp, weight, sems = refs
    copies = [
        pltpu.make_async_copy(source, target, sems.at[at])
        for at, (source, target) in enumerate(zip(sources, (kp, vp, weight)))
    ]
    for copy in copies:
        copy.start()
    kv_index, start = lens_ref[0], lens_ref[1]
    rows, q_cols = q_refs[0].shape
    kv_cols = k_all.shape[1]
    group = q_cols // kv_cols
    heads = q_cols // head_dim
    span = 2 * rows
    scale = head_dim**-0.5 * math.log2(math.e)
    for refs, whole in ((k_refs, k_all), (v_refs, v_all)):
        for at, ref in enumerate(refs):
            whole[at * rows : (at + 1) * rows, :] = ref[...]
    queries = [
        jnp.concatenate([ref[:, head * head_dim : (head + 1) * head_dim] for ref in q_refs], axis=0)
        for head in range(heads)
    ]
    peak[...] = jnp.full(peak.shape, NEG, jnp.float32)
    acc[...] = jnp.zeros(acc.shape, jnp.float32)

    def absorb(keys_ref, values_ref, place, size, allowed):
        for head in range(heads):
            lanes = slice(head // group * head_dim, (head // group + 1) * head_dim)
            keys = keys_ref[pl.ds(place, size), lanes]
            values = values_ref[pl.ds(place, size), lanes]
            wide = jnp.concatenate([values, jnp.ones_like(values)], axis=1)
            scores = contract_last(queries[head], keys)
            if allowed is not None:
                scores = jnp.where(allowed, scores, NEG)
            old = peak[head][:, :1]
            new = jnp.maximum(old, jnp.max(scores, axis=1, keepdims=True))
            weights = jnp.exp2((scores - new) * scale).astype(jnp.bfloat16)
            acc[head] = acc[head] * jnp.exp2((old - new) * scale) + matmul(weights, wide)
            peak[head] = jnp.broadcast_to(new, peak.shape[1:])

    turned = kv_index % 2

    def order(axis):
        ids = lax.broadcasted_iota(jnp.int32, (span, span), axis)
        swapped = jnp.where(ids < rows, ids + rows, ids - rows)
        return jnp.where(turned == 1, swapped, ids)

    absorb(k_all, v_all, pair * span, span, order(1) <= order(0))

    def fresh_block(at, carry):
        @pl.when(((kv_index // 2) ^ at) < ((kv_index // 2) ^ pair))
        def _():
            absorb(k_all, v_all, pl.multiple_of(at * span, span), span, None)

        return carry

    lax.fori_loop(0, block_count // 2, fresh_block, 0)
    copies[0].wait()
    copies[1].wait()
    full = start // KEY_BLOCK

    def prefix_block(at, carry):
        absorb(kp, vp, pl.multiple_of(at * KEY_BLOCK, KEY_BLOCK), KEY_BLOCK, None)
        return carry

    lax.fori_loop(0, full, prefix_block, 0)

    @pl.when(full * KEY_BLOCK < start)
    def _():
        place = pl.multiple_of(full * KEY_BLOCK, KEY_BLOCK)
        ids = lax.broadcasted_iota(jnp.int32, (span, KEY_BLOCK), 1)
        absorb(kp, vp, place, KEY_BLOCK, ids < start - place)

    for head in range(heads):
        attended[:, head * head_dim : (head + 1) * head_dim] = (
            acc[head][:, :head_dim] / acc[head][:, head_dim:]
        ).astype(jnp.bfloat16)
    copies[2].wait()
    width = weight.shape[1]
    for at in range(0, width, q_cols):
        part = matmul(attended[...], weight[:, at : at + q_cols])
        even_ref[:, at : at + q_cols] = part[:rows].astype(even_ref.dtype)
        for half, odd_ref in enumerate(odd_refs):
            here = rows + half * (rows // 2)
            odd_ref[:, at : at + q_cols] = part[here : here + rows // 2].astype(odd_ref.dtype)
    last = kv_index ^ (block_count - 1)
    here = pl.multiple_of((last % 2) * rows + rows - TAIL, TAIL)
    last_ref[:, :q_cols] = attended[pl.ds(here, TAIL), :]
    ends = [ref[rows - TAIL :, :] for ref in q_refs]
    last_ref[:, q_cols : 2 * q_cols] = jnp.where(last % 2 == 1, ends[1], ends[0])
    there = pl.ds(pl.multiple_of(last * rows + rows - TAIL, TAIL), TAIL)
    last_ref[:, 2 * q_cols : 2 * q_cols + kv_cols] = k_all[there, :]
    last_ref[:, 2 * q_cols + kv_cols :] = v_all[there, :]


def attend(pair, lens, parts, head_dim, key_prefix, value_prefix, o_proj, even_type, follows):
    block_count = len(parts)
    queries, keys, values = [[part[at] for part in parts] for at in range(3)]
    queries = queries[2 * pair : 2 * pair + 2]
    rows, q_cols = queries[0].shape
    kv_cols = keys[0].shape[1]
    width = o_proj.shape[1]
    heads = q_cols // head_dim
    outs = [
        jax.ShapeDtypeStruct((rows, width), even_type),
        jax.ShapeDtypeStruct((rows // 2, width), jnp.bfloat16),
        jax.ShapeDtypeStruct((rows // 2, width), jnp.bfloat16),
        jax.ShapeDtypeStruct((TAIL, 2 * q_cols + 2 * kv_cols), jnp.bfloat16),
    ]
    return pl.pallas_call(
        functools.partial(attend_kernel, pair, block_count, head_dim),
        out_shape=outs,
        grid_spec=pltpu.PrefetchScalarGridSpec(
            num_scalar_prefetch=1,
            grid=(1,),
            in_specs=[whole_spec(part.shape) for part in queries + keys + values]
            + [pl.BlockSpec(memory_space=pl.ANY)] * 4,
            out_specs=[whole_spec(out.shape) for out in outs],
            scratch_shapes=[
                pltpu.VMEM((rows * block_count, kv_cols), jnp.bfloat16),
                pltpu.VMEM((rows * block_count, kv_cols), jnp.bfloat16),
                pltpu.VMEM((heads, 2 * rows, head_dim), jnp.float32),
                pltpu.VMEM((heads, 2 * rows, 2 * head_dim), jnp.float32),
                pltpu.VMEM((2 * rows, q_cols), jnp.bfloat16),
                pltpu.VMEM(key_prefix.shape, jnp.bfloat16),
                pltpu.VMEM(value_prefix.shape, jnp.bfloat16),
                pltpu.VMEM(o_proj.shape, jnp.bfloat16),
                pltpu.SemaphoreType.DMA((3,)),
            ],
        ),
        compiler_params=pltpu.CompilerParams(vmem_limit_bytes=VMEM_LIMIT),
        cost_estimate=BRIEF,
    )(lens, *queries, *keys, *values, key_prefix, value_prefix, o_proj, follows)


def decode_kernel(pairs, block_count, head_dim, q_cols, kv_cols, lens_ref, *refs):
    last_refs, refs = refs[:pairs], refs[pairs:]
    o_hbm, kc_hbm, vc_hbm, out_ref, kc, vc, weight, dec_in, dec_out, sems, weight_sem = refs
    kv_index = lens_ref[0]
    dec_count, slots = kc.shape[:2]
    group = q_cols // kv_cols
    kv_heads = kv_cols // head_dim
    heads = q_cols // head_dim
    scale = head_dim**-0.5 * math.log2(math.e)
    sizes = (slots // 4, slots // 2, slots)

    def by_size(together, act):
        first = together * DECODE_GROUP
        length = lens_ref[2 + first]
        for at in range(1, DECODE_GROUP):
            length = jnp.maximum(length, lens_ref[2 + first + at])
        for at, size in enumerate(sizes):
            fits = length <= size
            if at:
                fits = fits & (length > sizes[at - 1])
            pl.when(fits)(functools.partial(act, first, size))

    def cache_copies(request, size):
        return (
            pltpu.make_async_copy(
                kc_hbm.at[request, pl.ds(0, size)], kc.at[request, pl.ds(0, size)], sems.at[0, request]
            ),
            pltpu.make_async_copy(
                vc_hbm.at[request, pl.ds(0, size)], vc.at[request, pl.ds(0, size)], sems.at[1, request]
            ),
        )

    def start_copies(first, size):
        for at in range(DECODE_GROUP):
            for copy in cache_copies(first + at, size):
                copy.start()

    for together in range(dec_count // DECODE_GROUP):
        by_size(together, start_copies)
    weight_copy = pltpu.make_async_copy(o_hbm, weight, weight_sem)
    weight_copy.start()
    held = last_refs[0][...]
    for at in range(1, pairs):
        held = jnp.where((kv_index ^ (block_count - 1)) // 2 == at, last_refs[at][...], held)
    rows_in = held[TAIL - dec_count :, q_cols:].astype(jnp.float32)
    for request in range(dec_count):
        dec_in[request] = rows_in[request : request + 1]

    def attend_some(first, size):
        for at in range(DECODE_GROUP):
            attend_one(first + at, size)

    def attend_one(request, size):
        for copy in cache_copies(request, size):
            copy.wait()
        row = dec_in[request]
        empty = jnp.zeros((1, head_dim), jnp.float32)
        spread = []
        for at in range(heads):
            parts = [empty] * kv_heads
            parts[at // group] = row[:, at * head_dim : (at + 1) * head_dim]
            spread.append(jnp.concatenate(parts, axis=1))
        spread += [jnp.zeros((1, kv_cols), jnp.float32)] * (8 - len(spread))
        q_rows = jnp.concatenate(spread, axis=0)
        key_self = row[:, q_cols : q_cols + kv_cols]
        value_self = row[:, q_cols + kv_cols :]
        past = contract_last(q_rows.astype(jnp.bfloat16), kc[request, :size, :])
        ids = lax.broadcasted_iota(jnp.int32, past.shape, 1)
        past = jnp.where(ids < lens_ref[2 + request], past, NEG)
        own = jnp.sum(q_rows * key_self, axis=1, keepdims=True)
        top = jnp.maximum(jnp.max(past, axis=1, keepdims=True), own)
        past = jnp.exp2((past - top) * scale)
        own = jnp.exp2((own - top) * scale)
        total = jnp.sum(past, axis=1, keepdims=True) + own
        past = (past / total).astype(jnp.bfloat16)
        own = (own / total).astype(jnp.bfloat16).astype(jnp.float32)
        summed = matmul(past, vc[request, :size, :]) + own * value_self
        outs = []
        for at in range(heads):
            lane = (at // group) * head_dim
            outs.append(summed[at : at + 1, lane : lane + head_dim])
        dec_out[request] = jnp.concatenate(outs, axis=1)

    for together in range(dec_count // DECODE_GROUP):
        by_size(together, attend_some)
    done = [dec_out[request] for request in range(dec_count)]
    rows = jnp.concatenate([held[: TAIL - dec_count, :q_cols].astype(jnp.float32)] + done, axis=0)
    weight_copy.wait()
    out_ref[...] = matmul(rows.astype(jnp.bfloat16), weight[...]).astype(jnp.bfloat16)


def decode(lens, lasts, head_dim, block_count, o_proj, key_cache, value_cache, follows):
    dec_count, slots, kv_cols = key_cache.shape
    q_cols, width = o_proj.shape
    pairs = len(lasts)

    def kernel(lens_ref, *refs):
        given = pairs + 3
        decode_kernel(
            pairs, block_count, head_dim, q_cols, kv_cols, lens_ref, *refs[:given], *refs[given + 1 :]
        )

    return pl.pallas_call(
        kernel,
        out_shape=jax.ShapeDtypeStruct((TAIL, width), jnp.bfloat16),
        grid_spec=pltpu.PrefetchScalarGridSpec(
            num_scalar_prefetch=1,
            grid=(1,),
            in_specs=[whole_spec(last.shape) for last in lasts]
            + [pl.BlockSpec(memory_space=pl.ANY)] * 4,
            out_specs=whole_spec((TAIL, width)),
            scratch_shapes=[
                pltpu.VMEM((dec_count, slots, kv_cols), jnp.bfloat16),
                pltpu.VMEM((dec_count, slots, kv_cols), jnp.bfloat16),
                pltpu.VMEM(o_proj.shape, jnp.bfloat16),
                pltpu.VMEM((dec_count, 1, q_cols + 2 * kv_cols), jnp.float32),
                pltpu.VMEM((dec_count, 1, q_cols), jnp.float32),
                pltpu.SemaphoreType.DMA((2, dec_count)),
                pltpu.SemaphoreType.DMA,
            ],
        ),
        compiler_params=pltpu.CompilerParams(vmem_limit_bytes=VMEM_LIMIT),
        cost_estimate=BRIEF,
    )(lens, *lasts, o_proj, key_cache, value_cache, follows)


def feed_kernel(tiles, counts, added, *refs):
    pieces = len(counts)
    x_refs, refs = refs[:pieces], refs[pieces:]
    add_refs, refs = refs[:added], refs[added:]
    weight_refs, refs = refs[: len(refs) - 2 - pieces], refs[len(refs) - 2 - pieces :]
    out_refs, (x_all, total) = refs[:pieces], refs[pieces:]
    step = pl.program_id(0)
    cuts = [sum(counts[:at]) for at in range(pieces + 1)]

    @pl.when(step == 0)
    def _():
        for at, ref in enumerate(x_refs):
            x_all[cuts[at] : cuts[at + 1], :] = ref[...]
        for at, ref in enumerate(add_refs):
            total[cuts[at] : cuts[at + 1], :] = ref[...]

    sets = len(weight_refs) // 3
    for at in range(sets):
        gate_ref, up_ref, down_ref = weight_refs[3 * at : 3 * at + 3]

        @pl.when(step // tiles == at)
        def _():
            rows = x_all[...]
            tile = gate_ref.shape[-1]
            gate = matmul(rows, gate_ref[...].reshape(-1, tile))
            up = matmul(rows, up_ref[...].reshape(-1, tile))
            act = (gate / (1.0 + jnp.exp(-gate)) * up).astype(jnp.bfloat16)
            if len(down_ref.shape) == 2:
                downs = [down_ref[...]]
            else:
                downs = [down_ref[part] for part in range(down_ref.shape[0])]
            lane = 0
            for down in downs:
                lanes = slice(lane, lane + down.shape[1])
                lane += down.shape[1]
                part = matmul(act, down)
                if at or added:
                    total[:, lanes] += part
                else:
                    total[:, lanes] = jnp.where(step == 0, part, total[:, lanes] + part)

    @pl.when(step == sets * tiles - 1)
    def _():
        for at, ref in enumerate(out_refs):
            ref[...] = total[cuts[at] : cuts[at + 1], :].astype(ref.dtype)


def feed_forward(blocks, dtypes, weights, follows, adds=()):
    counts = [block.shape[0] for block in blocks]
    size, width = sum(counts), blocks[0].shape[1]
    held = weights[0]
    hidden = held[0].shape[1] if isinstance(held, tuple) else held.shape[2] // 2
    tile = 256 if hidden % 256 == 0 else 128
    tiles = hidden // tile
    specs, operands = [], []
    for at, held in enumerate(weights):

        def place(step, at=at):
            return jnp.clip(step - at * tiles, 0, tiles - 1)

        if isinstance(held, tuple):
            specs += [
                pl.BlockSpec((width, tile), lambda step, place=place: (0, place(step))),
                pl.BlockSpec((width, tile), lambda step, place=place: (0, place(step))),
                pl.BlockSpec((tile, width), lambda step, place=place: (place(step), 0)),
            ]
            operands += held
            continue
        shares = held.shape[0]
        share = width // shares
        specs += [
            pl.BlockSpec((shares, share, tile), lambda step, place=place: (0, 0, place(step))),
            pl.BlockSpec((shares, share, tile), lambda step, place=place: (0, 0, tiles + place(step))),
            pl.BlockSpec(
                (shares, tile, share),
                lambda step, place=place, below=share // tile: (0, below, place(step)),
            ),
        ]
        operands += [held] * 3

    def kernel(*refs):
        given = len(blocks) + len(adds) + len(operands)
        feed_kernel(tiles, counts, len(adds), *refs[:given], *refs[given + len(follows) :])

    return pl.pallas_call(
        kernel,
        out_shape=[
            jax.ShapeDtypeStruct((count, width), dtype) for count, dtype in zip(counts, dtypes)
        ],
        grid=(len(weights) * tiles,),
        in_specs=[whole_spec(block.shape) for block in blocks]
        + [whole_spec(add.shape) for add in adds]
        + specs
        + [pl.BlockSpec(memory_space=pl.ANY)] * len(follows),
        out_specs=[whole_spec((count, width)) for count in counts],
        scratch_shapes=[
            pltpu.VMEM((size, width), jnp.bfloat16),
            pltpu.VMEM((size, width), jnp.float32),
        ],
        compiler_params=pltpu.CompilerParams(vmem_limit_bytes=VMEM_LIMIT),
        cost_estimate=BRIEF,
    )(*blocks, *adds, *operands, *follows)


def regroup(rows_in):
    return lax.all_to_all(rows_in, ("req", "kv"), split_axis=0, concat_axis=0, tiled=True)


def matmul(left, right):
    return jnp.dot(left, right, preferred_element_type=jnp.float32)


def routes(slot_tokens, self_index, devices, rows_dev, ready):
    per_pair = rows_dev // devices
    slot_table = slot_tokens.reshape(devices, rows_dev)
    source = slot_table // rows_dev
    places = jnp.arange(rows_dev, dtype=jnp.int32)
    before = (places[:, None] < places[None, :]).astype(jnp.bfloat16)
    from_self = source == self_index
    rank = matmul(from_self.astype(jnp.bfloat16), before).astype(jnp.int32)
    local = slot_table - self_index * rows_dev
    ranked = jnp.where(from_self, rank, -1)[:, None, :] == jnp.arange(per_pair, dtype=jnp.int32)[None, :, None]
    send_rows = jnp.sum(jnp.where(ranked, local[:, None, :], 0), axis=2).reshape(-1)
    send_hot = (send_rows[:, None] == places[None, :]).astype(jnp.bfloat16)
    own = lax.dynamic_index_in_dim(source, self_index, 0, keepdims=False)
    earlier = (own[:, None] == own[None, :]) & (places[:, None] > places[None, :])
    own_rank = jnp.sum(earlier.astype(jnp.int32), axis=1)
    slot_hot = ((own * per_pair + own_rank + ready)[:, None] == places[None, :]).astype(jnp.bfloat16)
    return send_hot, slot_hot


def pick(hot, rows, transposed=False):
    if transposed:
        return lax.dot_general(
            hot, rows, (((0,), (0,)), ((), ())), preferred_element_type=jnp.float32
        ).astype(rows.dtype)
    return matmul(hot, rows).astype(rows.dtype)


def shards(
    hidden_in,
    slot_tokens,
    cache_len,
    prefill_start,
    key_cache,
    value_cache,
    key_prefix,
    value_prefix,
    attn_gain,
    q_proj,
    k_proj,
    v_proj,
    q_gain,
    k_gain,
    o_proj,
    ffn_gain,
    w_gate,
    w_up,
    w_down,
    final_gain,
    lm_head,
):
    req_count = lax.axis_size("req")
    kv_count = lax.axis_size("kv")
    devices = req_count * kv_count
    rows_dev, width = hidden_in.shape
    kv_index = lax.axis_index("kv")
    self_index = lax.axis_index("req") * kv_count + kv_index
    kv_bits = bits_below(kv_count)
    near_bits = [bit for bit in bits_below(req_count) if bit < GROUP]

    head_dim = q_gain.shape[0]
    dec_count = cache_len.shape[0]
    tok_req = rows_dev * kv_count
    fresh_count = tok_req - dec_count
    places = jnp.concatenate(
        [prefill_start[0] + jnp.arange(fresh_count, dtype=jnp.int32), cache_len]
    ).astype(jnp.float32)
    cosines, sines = angle_tables(places, head_dim)
    cosines = jnp.concatenate([cosines, cosines], axis=1)
    sines = jnp.concatenate([-sines, sines], axis=1)

    cosines, sines = lax.optimization_barrier((cosines, sines))
    ready = sum(zero_after(each) for each in (cosines, sines))

    send_hot, slot_hot = routes(slot_tokens, self_index, devices, rows_dev, ready)
    sent = pick(send_hot, hidden_in)
    arrived = regroup(sent)
    owner_rows = pick(slot_hot, arrived)
    far_count = req_count // GROUP
    far_share = share_of(kv_index[None], width // kv_count, w_gate, w_up, w_down, arrived)
    step = GROUP if far_count > 2 else GROUP // 2
    ring = [(i, (i + step) % req_count) for i in range(req_count)]
    far_hops = [far_share]
    for _ in range(max(2, far_count - 1)):
        far_hops.append(lax.ppermute(far_hops[-1], "req", ring))
    far_shares = far_hops[GROUP // step :]

    def project_block(diff, follows):
        block_at = (kv_index ^ diff) * rows_dev
        tables = [lax.dynamic_slice_in_dim(table, block_at, rows_dev, 0) for table in (cosines, sines)]
        return project(
            [blocks[diff]], attn_gain, *tables, q_gain, k_gain, q_proj, k_proj, v_proj, follows
        )

    even = gather_xor(owner_rows, "kv", kv_bits[:0:-1])
    blocks = {0: owner_rows, 1: swap(owner_rows, "kv", 1)}
    parts = [project_block(0, owner_rows)]
    parts.append(project_block(1, parts[0][2]))
    for diff in range(2, kv_count, 2):
        blocks[diff] = pin(even[diff], parts[1][2])
        blocks[diff + 1] = swap(blocks[diff], "kv", 1)
    for diff in range(2, kv_count):
        parts.append(project_block(diff, parts[-1][2]))

    f32, bf16 = jnp.float32, jnp.bfloat16
    lens = jnp.concatenate([kv_index[None], prefill_start, cache_len]).astype(jnp.int32)
    follows, lasts, sums = parts[-1][2], {}, []
    for pair in range(kv_count // 2 - 1, -1, -1):
        sum_even, *sum_odd, lasts[pair] = attend(
            pair,
            lens,
            parts,
            head_dim,
            key_prefix[0],
            value_prefix[0],
            o_proj,
            bf16 if pair else f32,
            follows,
        )
        if pair:
            halves = [swap(pin(half, far_hops[1]), "kv", 1) for half in sum_odd]
            other = jnp.concatenate(halves, axis=0)
            both = sum_even.astype(f32) + other.astype(f32)
            follows = both.astype(bf16)
            sums.append(swap(follows, "kv", 2 * pair))
        else:
            halves = [swap(pin(half, *sums), "kv", 1) for half in sum_odd]
            sums.append(jnp.concatenate(halves, axis=0))
            own_sum = sum_even
    resid = owner_rows.astype(f32) + own_sum
    for each in sums:
        resid = resid + each.astype(f32)
    resid = resid.astype(bf16)
    ffn_in = norm_rows(resid, ffn_gain).astype(bf16)

    own_weights = (w_gate, w_up, w_down)
    near = {0: ffn_in, 1: swap(ffn_in, "req", 1), 2: swap(ffn_in, "req", 2)}

    last_sum = decode(
        lens,
        [lasts[pair] for pair in range(kv_count // 2)],
        head_dim,
        kv_count,
        o_proj,
        key_cache,
        value_cache,
        ffn_in,
    )
    far_weights = [
        lax.all_gather(pin(held, last_sum), "kv") for held in far_shares
    ]
    last_raw = blocks[0][rows_dev - TAIL :]
    for diff in range(1, kv_count):
        is_last = (kv_index ^ diff) == kv_count - 1
        last_raw = jnp.where(is_last, blocks[diff][rows_dev - TAIL :], last_raw)
    last_resid = last_raw.astype(f32) + last_sum.astype(f32)
    for diff in range(1, kv_count):
        last_resid = last_resid + swap(last_sum, "kv", diff).astype(f32)
    last_resid = last_resid.astype(bf16)
    last_in = norm_rows(last_resid, ffn_gain).astype(bf16)

    last_near = gather_xor(last_in, "req", near_bits)
    lasts_in = [last_near[diff] for diff in range(GROUP)]

    zero = feed_forward([ffn_in], [f32], [own_weights], [last_sum])
    near[3] = swap(near[1], "req", 2)
    some = feed_forward([near[1], near[2]], [f32] * 2, [own_weights], [zero[0], last_near[1]])
    rest = feed_forward([near[3], *lasts_in], [f32] * (1 + GROUP), [own_weights], some[:1])
    first, second = feed_forward([near[1], near[2]], [bf16] * 2, far_weights, rest[:1], some)
    third, last_part, *last_parts = feed_forward(
        [near[3], *lasts_in], [bf16, f32] + [bf16] * (GROUP - 1), far_weights, [first], rest
    )
    backs = [swap(first, "req", 1), swap(second, "req", 2), swap(third, "req", 3)]
    (own_part,) = feed_forward([ffn_in], [f32], far_weights, [third], zero)
    last_part = pin(last_part, own_part, backs[0][:TAIL], backs[1][:TAIL])
    for diff, part in enumerate(last_parts, 1):
        last_part = last_part + swap(part, "req", diff).astype(f32)
    last_rows = (last_resid.astype(f32) + last_part).astype(bf16)
    ffn_part = own_part
    for back in backs:
        ffn_part = ffn_part + back.astype(f32)
    out_rows = (resid.astype(f32) + ffn_part).astype(bf16)
    ends = jnp.where(kv_index == kv_count - 1, last_rows, out_rows[rows_dev - TAIL :])
    out_rows = jnp.concatenate([out_rows[: rows_dev - TAIL], ends], axis=0)
    returned = regroup(pick(slot_hot, out_rows, transposed=True))
    layer_out = pick(send_hot, returned, transposed=True)

    tail_count = dec_count + 1
    tails = norm_rows(last_rows, final_gain).astype(bf16)
    req_bits = bits_below(req_count)
    for bit in req_bits:
        tails = jnp.concatenate([tails, swap(tails, "req", bit)], axis=0)
    tails = pin(tails, out_rows)
    peaks = jnp.max(matmul(tails, lm_head), axis=1).reshape(req_count, TAIL)
    peaks = peaks[:, TAIL - tail_count :]
    owners = jnp.arange(req_count, dtype=jnp.int32)
    found = (owners[:, None] ^ owners[None, :]) == lax.axis_index("req")
    peaks = jnp.sum(jnp.where(found[:, :, None], peaks[None], 0.0), axis=1).reshape(1, -1)
    for axis, bits in (("kv", kv_bits), ("req", req_bits)):
        for bit in bits:
            peaks = jnp.maximum(peaks, swap(peaks, axis, bit))
    return (layer_out, peaks[0])


def solution(mesh):
    placed = (
        P(("req", "kv"), None),
        P(),
        P("req"),
        P("req"),
        P("req", None, "kv"),
        P("req", None, "kv"),
        P("req", None, "kv"),
        P("req", None, "kv"),
        P(),
        P(None, "kv"),
        P(None, "kv"),
        P(None, "kv"),
        P(),
        P(),
        P("kv", None),
        P(),
        P(None, "req"),
        P(None, "req"),
        P("req", None),
        P(),
        P(None, ("req", "kv")),
    )
    return jax.shard_map(
        shards, mesh=mesh, in_specs=placed, out_specs=(P(("req", "kv"), None), P()), check_vma=False
    )
```

```python
import functools
import math

import jax
import jax.numpy as jnp
from jax import lax
from jax.experimental import pallas as pl
from jax.experimental.pallas import tpu as pltpu
from jax.sharding import PartitionSpec as P

EPS = 1e-06
NEG = -1e30
GROUP = 4
TAIL = 16
DECODE_GROUP = 4
KEY_BLOCK = 512
VMEM_LIMIT = 56 * 1024 * 1024
BRIEF = pl.CostEstimate(flops=1, bytes_accessed=1, transcendentals=0)


def swap(value, axis, bit):
    size = lax.axis_size(axis)
    return lax.ppermute(value, axis, [(i, i ^ bit) for i in range(size)])


def bits_below(size):
    return [1 << i for i in range(size.bit_length() - 1)]


def gather_xor(value, axis, bits):
    held = {0: value}
    for bit in bits:
        held.update({diff ^ bit: swap(block, axis, bit) for diff, block in list(held.items())})
    return held


def zero_after(value):
    first = value[(0,) * value.ndim]
    return (first != first).astype(jnp.int32)


def pin(value, *others):
    anywhere = pl.BlockSpec(memory_space=pl.ANY)
    return pl.pallas_call(
        lambda *refs: None,
        out_shape=jax.ShapeDtypeStruct(value.shape, value.dtype),
        in_specs=[anywhere] * (1 + len(others)),
        out_specs=anywhere,
        input_output_aliases={0: 0},
        cost_estimate=BRIEF,
    )(value, *others)


def norm_rows(values, gain_vec):
    wide = values.astype(jnp.float32)
    return wide * lax.rsqrt(jnp.mean(wide * wide, axis=-1, keepdims=True) + EPS) * gain_vec


def angle_tables(places, head_dim):
    half_dim = head_dim // 2
    freqs = 1000000.0 ** (-(jnp.arange(half_dim, dtype=jnp.float32) * 2.0 / head_dim))
    angles = places[:, None] * freqs[None, :]
    return jnp.cos(angles), jnp.sin(angles)


def contract_last(left, right):
    return lax.dot_general(left, right, (((1,), (1,)), ((), ())), preferred_element_type=jnp.float32)


def whole_spec(shape):
    return pl.BlockSpec(shape, lambda *_: (0,) * len(shape))


def project_kernel(block_count, head_dim, *refs):
    row_refs = refs[:block_count]
    (gain_ref, cos_ref, sin_ref, q_gain_ref, k_gain_ref, wq_hbm, wk_hbm, wv_hbm) = refs[
        block_count : block_count + 8
    ]
    q_ref, k_ref, v_ref, wq, wk, wv, sems = refs[-7:]
    copies = [
        pltpu.make_async_copy(hbm, vmem, sems.at[at])
        for at, (hbm, vmem) in enumerate(((wq_hbm, wq), (wk_hbm, wk), (wv_hbm, wv)))
    ]
    for copy in copies:
        copy.start()
    normed = []
    for ref in row_refs:
        wide = ref[...].astype(jnp.float32)
        scale = lax.rsqrt(jnp.mean(wide * wide, axis=-1, keepdims=True) + EPS)
        normed.append((wide * scale * gain_ref[...]).astype(jnp.bfloat16))
    rows = jnp.concatenate(normed, axis=0)
    cosine, sine = cos_ref[...], sin_ref[...]

    def heads(raw, gain, out_ref):
        for at in range(raw.shape[1] // head_dim):
            head = raw[:, at * head_dim : (at + 1) * head_dim]
            scale = lax.rsqrt(jnp.mean(head * head, axis=-1, keepdims=True) + EPS)
            head = head * scale * gain
            turned = head * cosine + pltpu.roll(head, head_dim // 2, 1) * sine
            out_ref[:, at * head_dim : (at + 1) * head_dim] = turned.astype(jnp.bfloat16)

    copies[0].wait()
    heads(matmul(rows, wq[...]), q_gain_ref[...], q_ref)
    copies[1].wait()
    heads(matmul(rows, wk[...]), k_gain_ref[...], k_ref)
    copies[2].wait()
    v_ref[...] = matmul(rows, wv[...]).astype(jnp.bfloat16)


def project(blocks, gain, cosine, sine, q_gain, k_gain, q_proj, k_proj, v_proj, follows):
    head_dim = q_gain.shape[0]
    rows = sum(block.shape[0] for block in blocks)
    width = q_proj.shape[0]
    outs = (q_proj.shape[1], k_proj.shape[1], v_proj.shape[1])
    vectors = (gain[None, :], cosine, sine, q_gain[None, :], k_gain[None, :])
    return pl.pallas_call(
        functools.partial(project_kernel, len(blocks), head_dim),
        out_shape=[jax.ShapeDtypeStruct((rows, cols), jnp.bfloat16) for cols in outs],
        in_specs=[whole_spec(block.shape) for block in blocks]
        + [whole_spec(vector.shape) for vector in vectors]
        + [pl.BlockSpec(memory_space=pl.ANY)] * 4,
        out_specs=[whole_spec((rows, cols)) for cols in outs],
        grid=(1,),
        scratch_shapes=[pltpu.VMEM((width, cols), jnp.bfloat16) for cols in outs]
        + [pltpu.SemaphoreType.DMA((3,))],
        compiler_params=pltpu.CompilerParams(vmem_limit_bytes=VMEM_LIMIT),
        cost_estimate=BRIEF,
    )(*blocks, *vectors, q_proj, k_proj, v_proj, follows)


def share_kernel(share, tile, index_ref, gate, up, down, _, out, sems):
    at = pl.ds(pl.multiple_of(index_ref[0] * share, share), share)
    hidden = gate.shape[1]
    copies = [(gate.at[at, :], out.at[pl.ds(0, share), pl.ds(0, hidden)])]
    copies.append((up.at[at, :], out.at[pl.ds(0, share), pl.ds(hidden, hidden)]))
    for step in range(hidden // tile):
        rows, lanes = pl.ds(step * tile, tile), pl.ds(step * share, share)
        copies.append((down.at[rows, at], out.at[pl.ds(share, tile), lanes]))
    copies = [pltpu.make_async_copy(*ends, sems.at[at]) for at, ends in enumerate(copies)]
    for copy in copies:
        copy.start()
    for copy in copies:
        copy.wait()


def share_of(index, share, gate, up, down, follows):
    hidden = gate.shape[1]
    tile = share // 2
    return pl.pallas_call(
        functools.partial(share_kernel, share, tile),
        out_shape=jax.ShapeDtypeStruct((share + tile, 2 * hidden), gate.dtype),
        in_specs=[pl.BlockSpec(memory_space=pltpu.SMEM)] + [pl.BlockSpec(memory_space=pl.ANY)] * 4,
        out_specs=pl.BlockSpec(memory_space=pltpu.VMEM),
        scratch_shapes=[pltpu.SemaphoreType.DMA((2 + hidden // tile,))],
        cost_estimate=BRIEF,
    )(index, gate, up, down, follows)


def attend_kernel(pair, block_count, head_dim, lens_ref, *refs):
    q_refs, refs = refs[:2], refs[2:]
    k_refs, refs = refs[:block_count], refs[block_count:]
    v_refs, refs = refs[:block_count], refs[block_count:]
    sources, refs = refs[:3], refs[3 + 1 :]
    even_ref, *odd_refs, last_ref, k_all, v_all, peak, acc, attended, kp, vp, weight, sems = refs
    copies = [
        pltpu.make_async_copy(source, target, sems.at[at])
        for at, (source, target) in enumerate(zip(sources, (kp, vp, weight)))
    ]
    for copy in copies:
        copy.start()
    kv_index, start = lens_ref[0], lens_ref[1]
    rows, q_cols = q_refs[0].shape
    kv_cols = k_all.shape[1]
    group = q_cols // kv_cols
    heads = q_cols // head_dim
    span = 2 * rows
    scale = head_dim**-0.5 * math.log2(math.e)
    for refs, whole in ((k_refs, k_all), (v_refs, v_all)):
        for at, ref in enumerate(refs):
            whole[at * rows : (at + 1) * rows, :] = ref[...]
    queries = [
        jnp.concatenate([ref[:, head * head_dim : (head + 1) * head_dim] for ref in q_refs], axis=0)
        for head in range(heads)
    ]
    peak[...] = jnp.full(peak.shape, NEG, jnp.float32)
    acc[...] = jnp.zeros(acc.shape, jnp.float32)

    def absorb(keys_ref, values_ref, place, size, allowed):
        for head in range(heads):
            lanes = slice(head // group * head_dim, (head // group + 1) * head_dim)
            keys = keys_ref[pl.ds(place, size), lanes]
            values = values_ref[pl.ds(place, size), lanes]
            wide = jnp.concatenate([values, jnp.ones_like(values)], axis=1)
            scores = contract_last(queries[head], keys)
            if allowed is not None:
                scores = jnp.where(allowed, scores, NEG)
            old = peak[head][:, :1]
            new = jnp.maximum(old, jnp.max(scores, axis=1, keepdims=True))
            weights = jnp.exp2((scores - new) * scale).astype(jnp.bfloat16)
            acc[head] = acc[head] * jnp.exp2((old - new) * scale) + matmul(weights, wide)
            peak[head] = jnp.broadcast_to(new, peak.shape[1:])

    turned = kv_index % 2

    def order(axis):
        ids = lax.broadcasted_iota(jnp.int32, (span, span), axis)
        swapped = jnp.where(ids < rows, ids + rows, ids - rows)
        return jnp.where(turned == 1, swapped, ids)

    absorb(k_all, v_all, pair * span, span, order(1) <= order(0))

    def fresh_block(at, carry):
        @pl.when(((kv_index // 2) ^ at) < ((kv_index // 2) ^ pair))
        def _():
            absorb(k_all, v_all, pl.multiple_of(at * span, span), span, None)

        return carry

    lax.fori_loop(0, block_count // 2, fresh_block, 0)
    copies[0].wait()
    copies[1].wait()
    full = start // KEY_BLOCK

    def prefix_block(at, carry):
        absorb(kp, vp, pl.multiple_of(at * KEY_BLOCK, KEY_BLOCK), KEY_BLOCK, None)
        return carry

    lax.fori_loop(0, full, prefix_block, 0)

    @pl.when(full * KEY_BLOCK < start)
    def _():
        place = pl.multiple_of(full * KEY_BLOCK, KEY_BLOCK)
        ids = lax.broadcasted_iota(jnp.int32, (span, KEY_BLOCK), 1)
        absorb(kp, vp, place, KEY_BLOCK, ids < start - place)

    for head in range(heads):
        attended[:, head * head_dim : (head + 1) * head_dim] = (
            acc[head][:, :head_dim] / acc[head][:, head_dim:]
        ).astype(jnp.bfloat16)
    copies[2].wait()
    width = weight.shape[1]
    for at in range(0, width, q_cols):
        part = matmul(attended[...], weight[:, at : at + q_cols])
        even_ref[:, at : at + q_cols] = part[:rows].astype(even_ref.dtype)
        for half, odd_ref in enumerate(odd_refs):
            here = rows + half * (rows // 2)
            odd_ref[:, at : at + q_cols] = part[here : here + rows // 2].astype(odd_ref.dtype)
    last = kv_index ^ (block_count - 1)
    here = pl.multiple_of((last % 2) * rows + rows - TAIL, TAIL)
    last_ref[:, :q_cols] = attended[pl.ds(here, TAIL), :]
    ends = [ref[rows - TAIL :, :] for ref in q_refs]
    last_ref[:, q_cols : 2 * q_cols] = jnp.where(last % 2 == 1, ends[1], ends[0])
    there = pl.ds(pl.multiple_of(last * rows + rows - TAIL, TAIL), TAIL)
    last_ref[:, 2 * q_cols : 2 * q_cols + kv_cols] = k_all[there, :]
    last_ref[:, 2 * q_cols + kv_cols :] = v_all[there, :]


def attend(pair, lens, parts, head_dim, key_prefix, value_prefix, o_proj, even_type, follows):
    block_count = len(parts)
    queries, keys, values = [[part[at] for part in parts] for at in range(3)]
    queries = queries[2 * pair : 2 * pair + 2]
    rows, q_cols = queries[0].shape
    kv_cols = keys[0].shape[1]
    width = o_proj.shape[1]
    heads = q_cols // head_dim
    outs = [
        jax.ShapeDtypeStruct((rows, width), even_type),
        jax.ShapeDtypeStruct((rows // 2, width), jnp.bfloat16),
        jax.ShapeDtypeStruct((rows // 2, width), jnp.bfloat16),
        jax.ShapeDtypeStruct((TAIL, 2 * q_cols + 2 * kv_cols), jnp.bfloat16),
    ]
    return pl.pallas_call(
        functools.partial(attend_kernel, pair, block_count, head_dim),
        out_shape=outs,
        grid_spec=pltpu.PrefetchScalarGridSpec(
            num_scalar_prefetch=1,
            grid=(1,),
            in_specs=[whole_spec(part.shape) for part in queries + keys + values]
            + [pl.BlockSpec(memory_space=pl.ANY)] * 4,
            out_specs=[whole_spec(out.shape) for out in outs],
            scratch_shapes=[
                pltpu.VMEM((rows * block_count, kv_cols), jnp.bfloat16),
                pltpu.VMEM((rows * block_count, kv_cols), jnp.bfloat16),
                pltpu.VMEM((heads, 2 * rows, head_dim), jnp.float32),
                pltpu.VMEM((heads, 2 * rows, 2 * head_dim), jnp.float32),
                pltpu.VMEM((2 * rows, q_cols), jnp.bfloat16),
                pltpu.VMEM(key_prefix.shape, jnp.bfloat16),
                pltpu.VMEM(value_prefix.shape, jnp.bfloat16),
                pltpu.VMEM(o_proj.shape, jnp.bfloat16),
                pltpu.SemaphoreType.DMA((3,)),
            ],
        ),
        compiler_params=pltpu.CompilerParams(vmem_limit_bytes=VMEM_LIMIT),
        cost_estimate=BRIEF,
    )(lens, *queries, *keys, *values, key_prefix, value_prefix, o_proj, follows)


def decode_kernel(pairs, block_count, head_dim, q_cols, kv_cols, lens_ref, *refs):
    last_refs, refs = refs[:pairs], refs[pairs:]
    o_hbm, kc_hbm, vc_hbm, out_ref, kc, vc, weight, dec_in, dec_out, sems, weight_sem = refs
    kv_index = lens_ref[0]
    dec_count, slots = kc.shape[:2]
    group = q_cols // kv_cols
    kv_heads = kv_cols // head_dim
    heads = q_cols // head_dim
    scale = head_dim**-0.5 * math.log2(math.e)
    sizes = (slots // 4, slots // 2, slots)

    def by_size(together, act):
        first = together * DECODE_GROUP
        length = lens_ref[2 + first]
        for at in range(1, DECODE_GROUP):
            length = jnp.maximum(length, lens_ref[2 + first + at])
        for at, size in enumerate(sizes):
            fits = length <= size
            if at:
                fits = fits & (length > sizes[at - 1])
            pl.when(fits)(functools.partial(act, first, size))

    def cache_copies(request, size):
        return (
            pltpu.make_async_copy(
                kc_hbm.at[request, pl.ds(0, size)], kc.at[request, pl.ds(0, size)], sems.at[0, request]
            ),
            pltpu.make_async_copy(
                vc_hbm.at[request, pl.ds(0, size)], vc.at[request, pl.ds(0, size)], sems.at[1, request]
            ),
        )

    def start_copies(first, size):
        for at in range(DECODE_GROUP):
            for copy in cache_copies(first + at, size):
                copy.start()

    for together in range(dec_count // DECODE_GROUP):
        by_size(together, start_copies)
    weight_copy = pltpu.make_async_copy(o_hbm, weight, weight_sem)
    weight_copy.start()
    held = last_refs[0][...]
    for at in range(1, pairs):
        held = jnp.where((kv_index ^ (block_count - 1)) // 2 == at, last_refs[at][...], held)
    rows_in = held[TAIL - dec_count :, q_cols:].astype(jnp.float32)
    for request in range(dec_count):
        dec_in[request] = rows_in[request : request + 1]

    def attend_some(first, size):
        for at in range(DECODE_GROUP):
            attend_one(first + at, size)

    def attend_one(request, size):
        for copy in cache_copies(request, size):
            copy.wait()
        row = dec_in[request]
        empty = jnp.zeros((1, head_dim), jnp.float32)
        spread = []
        for at in range(heads):
            parts = [empty] * kv_heads
            parts[at // group] = row[:, at * head_dim : (at + 1) * head_dim]
            spread.append(jnp.concatenate(parts, axis=1))
        spread += [jnp.zeros((1, kv_cols), jnp.float32)] * (8 - len(spread))
        q_rows = jnp.concatenate(spread, axis=0)
        key_self = row[:, q_cols : q_cols + kv_cols]
        value_self = row[:, q_cols + kv_cols :]
        past = contract_last(q_rows.astype(jnp.bfloat16), kc[request, :size, :])
        ids = lax.broadcasted_iota(jnp.int32, past.shape, 1)
        past = jnp.where(ids < lens_ref[2 + request], past, NEG)
        own = jnp.sum(q_rows * key_self, axis=1, keepdims=True)
        top = jnp.maximum(jnp.max(past, axis=1, keepdims=True), own)
        past = jnp.exp2((past - top) * scale)
        own = jnp.exp2((own - top) * scale)
        total = jnp.sum(past, axis=1, keepdims=True) + own
        past = (past / total).astype(jnp.bfloat16)
        own = (own / total).astype(jnp.bfloat16).astype(jnp.float32)
        summed = matmul(past, vc[request, :size, :]) + own * value_self
        outs = []
        for at in range(heads):
            lane = (at // group) * head_dim
            outs.append(summed[at : at + 1, lane : lane + head_dim])
        dec_out[request] = jnp.concatenate(outs, axis=1)

    for together in range(dec_count // DECODE_GROUP):
        by_size(together, attend_some)
    done = [dec_out[request] for request in range(dec_count)]
    rows = jnp.concatenate([held[: TAIL - dec_count, :q_cols].astype(jnp.float32)] + done, axis=0)
    weight_copy.wait()
    out_ref[...] = matmul(rows.astype(jnp.bfloat16), weight[...]).astype(jnp.bfloat16)


def decode(lens, lasts, head_dim, block_count, o_proj, key_cache, value_cache, follows):
    dec_count, slots, kv_cols = key_cache.shape
    q_cols, width = o_proj.shape
    pairs = len(lasts)

    def kernel(lens_ref, *refs):
        given = pairs + 3
        decode_kernel(
            pairs, block_count, head_dim, q_cols, kv_cols, lens_ref, *refs[:given], *refs[given + 1 :]
        )

    return pl.pallas_call(
        kernel,
        out_shape=jax.ShapeDtypeStruct((TAIL, width), jnp.bfloat16),
        grid_spec=pltpu.PrefetchScalarGridSpec(
            num_scalar_prefetch=1,
            grid=(1,),
            in_specs=[whole_spec(last.shape) for last in lasts]
            + [pl.BlockSpec(memory_space=pl.ANY)] * 4,
            out_specs=whole_spec((TAIL, width)),
            scratch_shapes=[
                pltpu.VMEM((dec_count, slots, kv_cols), jnp.bfloat16),
                pltpu.VMEM((dec_count, slots, kv_cols), jnp.bfloat16),
                pltpu.VMEM(o_proj.shape, jnp.bfloat16),
                pltpu.VMEM((dec_count, 1, q_cols + 2 * kv_cols), jnp.float32),
                pltpu.VMEM((dec_count, 1, q_cols), jnp.float32),
                pltpu.SemaphoreType.DMA((2, dec_count)),
                pltpu.SemaphoreType.DMA,
            ],
        ),
        compiler_params=pltpu.CompilerParams(vmem_limit_bytes=VMEM_LIMIT),
        cost_estimate=BRIEF,
    )(lens, *lasts, o_proj, key_cache, value_cache, follows)


def feed_kernel(tiles, counts, added, split, *refs):
    pieces = len(counts)
    x_refs, refs = refs[:pieces], refs[pieces:]
    add_refs, refs = refs[:added], refs[added:]
    weight_refs, refs = refs[: len(refs) - 2 - pieces], refs[len(refs) - 2 - pieces :]
    out_refs, (x_all, total) = refs[:pieces], refs[pieces:]
    step = pl.program_id(0)
    cuts = [sum(counts[:at]) for at in range(pieces + 1)]

    @pl.when(step == 0)
    def _():
        for at, ref in enumerate(x_refs):
            x_all[cuts[at] : cuts[at + 1], :] = ref[...]
        for at, ref in enumerate(add_refs):
            total[cuts[at] : cuts[at + 1], :] = ref[...]

    sets = len(weight_refs) // 3 // split
    for at in range(sets):
        triples = [weight_refs[3 * part : 3 * part + 3] for part in range(at * split, (at + 1) * split)]

        @pl.when(step // tiles == at)
        def _():
            width = x_all.shape[1] // split
            gate, up, downs = 0.0, 0.0, []
            for part, (gate_ref, up_ref, down_ref) in enumerate(triples):
                rows = x_all[:, part * width : (part + 1) * width]
                tile = gate_ref.shape[-1]
                gate += matmul(rows, gate_ref[...].reshape(-1, tile))
                up += matmul(rows, up_ref[...].reshape(-1, tile))
                if split == 1:
                    downs.append(down_ref[...])
                    continue
                share = down_ref.shape[-1] // 2
                for piece in range(down_ref.shape[0]):
                    halves = [down_ref[piece, :, :share], down_ref[piece, :, share:]]
                    downs.append(jnp.concatenate(halves, axis=0))
            act = (gate / (1.0 + jnp.exp(-gate)) * up).astype(jnp.bfloat16)
            lane = 0
            for down in downs:
                lanes = slice(lane, lane + down.shape[1])
                lane += down.shape[1]
                part = matmul(act, down)
                if at or added:
                    total[:, lanes] += part
                else:
                    total[:, lanes] = jnp.where(step == 0, part, total[:, lanes] + part)

    @pl.when(step == sets * tiles - 1)
    def _():
        for at, ref in enumerate(out_refs):
            ref[...] = total[cuts[at] : cuts[at + 1], :].astype(ref.dtype)


def feed_forward(blocks, dtypes, weights, follows, adds=()):
    counts = [block.shape[0] for block in blocks]
    size, width = sum(counts), blocks[0].shape[1]
    held = weights[0]
    hidden = held[0].shape[1] if len(held) == 3 else held[0].shape[2] // 2
    tile = 256 if hidden % 256 == 0 else 128
    tiles = hidden // tile
    specs, operands = [], []
    for at, held in enumerate(weights):

        def place(step, at=at):
            return jnp.clip(step - at * tiles, 0, tiles - 1)

        if len(held) == 3:
            specs += [
                pl.BlockSpec((width, tile), lambda step, place=place: (0, place(step))),
                pl.BlockSpec((width, tile), lambda step, place=place: (0, place(step))),
                pl.BlockSpec((tile, width), lambda step, place=place: (place(step), 0)),
            ]
            operands += held
            continue
        shares = held[0].shape[0]
        share = width // shares // 2
        for half in held:
            specs += [
                pl.BlockSpec((shares, share, tile), lambda step, place=place: (0, 0, place(step))),
                pl.BlockSpec(
                    (shares, share, tile), lambda step, place=place: (0, 0, tiles + place(step))
                ),
                pl.BlockSpec((shares, tile // 2, 2 * share), lambda step, place=place: (0, 2, place(step))),
            ]
            operands += [half] * 3
    assert len({len(held) for held in weights}) == 1

    def kernel(*refs):
        given = len(blocks) + len(adds) + len(operands)
        split = 1 if len(weights[0]) == 3 else 2
        feed_kernel(tiles, counts, len(adds), split, *refs[:given], *refs[given + len(follows) :])

    return pl.pallas_call(
        kernel,
        out_shape=[
            jax.ShapeDtypeStruct((count, width), dtype) for count, dtype in zip(counts, dtypes)
        ],
        grid=(len(weights) * tiles,),
        in_specs=[whole_spec(block.shape) for block in blocks]
        + [whole_spec(add.shape) for add in adds]
        + specs
        + [pl.BlockSpec(memory_space=pl.ANY)] * len(follows),
        out_specs=[whole_spec((count, width)) for count in counts],
        scratch_shapes=[
            pltpu.VMEM((size, width), jnp.bfloat16),
            pltpu.VMEM((size, width), jnp.float32),
        ],
        compiler_params=pltpu.CompilerParams(vmem_limit_bytes=VMEM_LIMIT),
        cost_estimate=BRIEF,
    )(*blocks, *adds, *operands, *follows)


def regroup(rows_in):
    return lax.all_to_all(rows_in, ("req", "kv"), split_axis=0, concat_axis=0, tiled=True)


def matmul(left, right):
    return jnp.dot(left, right, preferred_element_type=jnp.float32)


def routes(slot_tokens, self_index, devices, rows_dev, ready):
    per_pair = rows_dev // devices
    slot_table = slot_tokens.reshape(devices, rows_dev)
    source = slot_table // rows_dev
    places = jnp.arange(rows_dev, dtype=jnp.int32)
    before = (places[:, None] < places[None, :]).astype(jnp.bfloat16)
    from_self = source == self_index
    rank = matmul(from_self.astype(jnp.bfloat16), before).astype(jnp.int32)
    local = slot_table - self_index * rows_dev
    ranked = jnp.where(from_self, rank, -1)[:, None, :] == jnp.arange(per_pair, dtype=jnp.int32)[None, :, None]
    send_rows = jnp.sum(jnp.where(ranked, local[:, None, :], 0), axis=2).reshape(-1)
    send_hot = (send_rows[:, None] == places[None, :]).astype(jnp.bfloat16)
    own = lax.dynamic_index_in_dim(source, self_index, 0, keepdims=False)
    earlier = (own[:, None] == own[None, :]) & (places[:, None] > places[None, :])
    own_rank = jnp.sum(earlier.astype(jnp.int32), axis=1)
    slot_hot = ((own * per_pair + own_rank + ready)[:, None] == places[None, :]).astype(jnp.bfloat16)
    return send_hot, slot_hot


def pick(hot, rows, transposed=False):
    if transposed:
        return lax.dot_general(
            hot, rows, (((0,), (0,)), ((), ())), preferred_element_type=jnp.float32
        ).astype(rows.dtype)
    return matmul(hot, rows).astype(rows.dtype)


def shards(
    hidden_in,
    slot_tokens,
    cache_len,
    prefill_start,
    key_cache,
    value_cache,
    key_prefix,
    value_prefix,
    attn_gain,
    q_proj,
    k_proj,
    v_proj,
    q_gain,
    k_gain,
    o_proj,
    ffn_gain,
    w_gate,
    w_up,
    w_down,
    final_gain,
    lm_head,
):
    req_count = lax.axis_size("req")
    kv_count = lax.axis_size("kv")
    devices = req_count * kv_count
    rows_dev, width = hidden_in.shape
    kv_index = lax.axis_index("kv")
    self_index = lax.axis_index("req") * kv_count + kv_index
    kv_bits = bits_below(kv_count)
    near_bits = [bit for bit in bits_below(req_count) if bit < GROUP]

    head_dim = q_gain.shape[0]
    dec_count = cache_len.shape[0]
    tok_req = rows_dev * kv_count
    fresh_count = tok_req - dec_count
    places = jnp.concatenate(
        [prefill_start[0] + jnp.arange(fresh_count, dtype=jnp.int32), cache_len]
    ).astype(jnp.float32)
    cosines, sines = angle_tables(places, head_dim)
    cosines = jnp.concatenate([cosines, cosines], axis=1)
    sines = jnp.concatenate([-sines, sines], axis=1)

    cosines, sines = lax.optimization_barrier((cosines, sines))
    ready = sum(zero_after(each) for each in (cosines, sines))

    send_hot, slot_hot = routes(slot_tokens, self_index, devices, rows_dev, ready)
    sent = pick(send_hot, hidden_in)
    arrived = regroup(sent)
    owner_rows = pick(slot_hot, arrived)
    far_count = req_count // GROUP
    share = width // kv_count // 2
    weights = (w_gate, w_up, w_down)
    far_early = share_of(kv_index[None], share, *weights, owner_rows)
    far_late = share_of(kv_index[None] + kv_count, share, *weights, owner_rows)
    held_late = far_late

    def ring(value, step):
        pairs = [(i, (i + step) % req_count) for i in range(req_count)]
        return lax.ppermute(value, "req", pairs)

    early, late, halfway = [], [], []
    for _ in range(1, far_count):
        far_early = ring(far_early, GROUP)
        early.append(far_early)
        if far_count == 2:
            halfway.append(ring(far_late, GROUP // 2))
            far_late = ring(halfway[0], GROUP // 2)
        else:
            far_late = ring(far_late, GROUP)
        late.append(far_late)

    def project_block(diff, follows):
        block_at = (kv_index ^ diff) * rows_dev
        tables = [lax.dynamic_slice_in_dim(table, block_at, rows_dev, 0) for table in (cosines, sines)]
        return project(
            [blocks[diff]], attn_gain, *tables, q_gain, k_gain, q_proj, k_proj, v_proj, follows
        )

    even = gather_xor(owner_rows, "kv", kv_bits[:0:-1])
    blocks = {0: owner_rows, 1: swap(owner_rows, "kv", 1)}
    parts = [project_block(0, owner_rows)]
    parts.append(project_block(1, parts[0][2]))
    for diff in range(2, kv_count, 2):
        blocks[diff] = pin(even[diff], parts[1][2])
        blocks[diff + 1] = swap(blocks[diff], "kv", 1)
    for diff in range(2, kv_count):
        parts.append(project_block(diff, parts[-1][2]))

    f32, bf16 = jnp.float32, jnp.bfloat16
    lens = jnp.concatenate([kv_index[None], prefill_start, cache_len]).astype(jnp.int32)
    follows, lasts, sums = held_late, {}, []
    for pair in range(kv_count // 2 - 1, -1, -1):
        sum_even, *sum_odd, lasts[pair] = attend(
            pair,
            lens,
            parts,
            head_dim,
            key_prefix[0],
            value_prefix[0],
            o_proj,
            bf16 if pair else f32,
            follows,
        )
        if pair:
            halves = [swap(pin(half, *early), "kv", 1) for half in sum_odd]
            other = jnp.concatenate(halves, axis=0)
            both = sum_even.astype(f32) + other.astype(f32)
            follows = both.astype(bf16)
            sums.append(swap(follows, "kv", 2 * pair))
        else:
            halves = [swap(pin(half, *sums, *halfway), "kv", 1) for half in sum_odd]
            sums.append(jnp.concatenate(halves, axis=0))
            own_sum = sum_even
    early_whole = [lax.all_gather(pin(held, own_sum, *sums[:-1]), "kv") for held in early]
    resid = owner_rows.astype(f32) + own_sum
    for each in sums:
        resid = resid + each.astype(f32)
    resid = resid.astype(bf16)
    ffn_in = norm_rows(resid, ffn_gain).astype(bf16)

    own_weights = (w_gate, w_up, w_down)
    near = {0: ffn_in, 1: swap(ffn_in, "req", 1), 2: swap(ffn_in, "req", 2)}

    last_sum = decode(
        lens,
        [lasts[pair] for pair in range(kv_count // 2)],
        head_dim,
        kv_count,
        o_proj,
        key_cache,
        value_cache,
        ffn_in,
    )
    far_weights = [
        (whole, lax.all_gather(pin(held, near[1][:TAIL], last_sum), "kv"))
        for whole, held in zip(early_whole, late)
    ]
    last_raw = blocks[0][rows_dev - TAIL :]
    for diff in range(1, kv_count):
        is_last = (kv_index ^ diff) == kv_count - 1
        last_raw = jnp.where(is_last, blocks[diff][rows_dev - TAIL :], last_raw)
    last_resid = last_raw.astype(f32) + last_sum.astype(f32)
    for diff in range(1, kv_count):
        last_resid = last_resid + swap(last_sum, "kv", diff).astype(f32)
    last_resid = last_resid.astype(bf16)
    last_in = norm_rows(last_resid, ffn_gain).astype(bf16)

    last_near = gather_xor(last_in, "req", near_bits)
    lasts_in = [last_near[diff] for diff in range(GROUP)]

    zero = feed_forward([ffn_in], [f32], [own_weights], [last_sum])
    near[3] = swap(near[1], "req", 2)
    some = feed_forward([near[1], near[2]], [f32] * 2, [own_weights], [zero[0], last_near[1]])
    rest = feed_forward([near[3], *lasts_in], [f32] * (1 + GROUP), [own_weights], some[:1])
    first, second = feed_forward([near[1], near[2]], [bf16] * 2, far_weights, rest[:1], some)
    third, last_part, *last_parts = feed_forward(
        [near[3], *lasts_in], [bf16, f32] + [bf16] * (GROUP - 1), far_weights, [first], rest
    )
    backs = [swap(first, "req", 1), swap(second, "req", 2), swap(third, "req", 3)]
    (own_part,) = feed_forward([ffn_in], [f32], far_weights, [third], zero)
    last_part = pin(last_part, own_part, backs[0][:TAIL], backs[1][:TAIL])
    for diff, part in enumerate(last_parts, 1):
        last_part = last_part + swap(part, "req", diff).astype(f32)
    last_rows = (last_resid.astype(f32) + last_part).astype(bf16)
    ffn_part = own_part
    for back in backs:
        ffn_part = ffn_part + back.astype(f32)
    out_rows = (resid.astype(f32) + ffn_part).astype(bf16)
    ends = jnp.where(kv_index == kv_count - 1, last_rows, out_rows[rows_dev - TAIL :])
    out_rows = jnp.concatenate([out_rows[: rows_dev - TAIL], ends], axis=0)
    returned = regroup(pick(slot_hot, out_rows, transposed=True))
    layer_out = pick(send_hot, returned, transposed=True)

    tail_count = dec_count + 1
    tails = norm_rows(last_rows, final_gain).astype(bf16)
    req_bits = bits_below(req_count)
    for bit in req_bits:
        tails = jnp.concatenate([tails, swap(tails, "req", bit)], axis=0)
    tails = pin(tails, out_rows)
    peaks = jnp.max(matmul(tails, lm_head), axis=1).reshape(req_count, TAIL)
    peaks = peaks[:, TAIL - tail_count :]
    owners = jnp.arange(req_count, dtype=jnp.int32)
    found = (owners[:, None] ^ owners[None, :]) == lax.axis_index("req")
    peaks = jnp.sum(jnp.where(found[:, :, None], peaks[None], 0.0), axis=1).reshape(1, -1)
    for axis, bits in (("kv", kv_bits), ("req", req_bits)):
        for bit in bits:
            peaks = jnp.maximum(peaks, swap(peaks, axis, bit))
    return (layer_out, peaks[0])


def solution(mesh):
    placed = (
        P(("req", "kv"), None),
        P(),
        P("req"),
        P("req"),
        P("req", None, "kv"),
        P("req", None, "kv"),
        P("req", None, "kv"),
        P("req", None, "kv"),
        P(),
        P(None, "kv"),
        P(None, "kv"),
        P(None, "kv"),
        P(),
        P(),
        P("kv", None),
        P(),
        P(None, "req"),
        P(None, "req"),
        P("req", None),
        P(),
        P(None, ("req", "kv")),
    )
    return jax.shard_map(
        shards, mesh=mesh, in_specs=placed, out_specs=(P(("req", "kv"), None), P()), check_vma=False
    )
```

```python
import functools
import math

import jax
import jax.numpy as jnp
from jax import lax
from jax.experimental import pallas as pl
from jax.experimental.pallas import tpu as pltpu
from jax.sharding import PartitionSpec as P

EPS = 1e-06
NEG = -1e30
GROUP = 4
TAIL = 16
DECODE_GROUP = 4
KEY_BLOCK = 512
VMEM_LIMIT = 56 * 1024 * 1024
BRIEF = pl.CostEstimate(flops=1, bytes_accessed=1, transcendentals=0)


def swap(value, axis, bit):
    size = lax.axis_size(axis)
    return lax.ppermute(value, axis, [(i, i ^ bit) for i in range(size)])


def bits_below(size):
    return [1 << i for i in range(size.bit_length() - 1)]


def gather_xor(value, axis, bits):
    held = {0: value}
    for bit in bits:
        held.update({diff ^ bit: swap(block, axis, bit) for diff, block in list(held.items())})
    return held


def zero_after(value):
    first = value[(0,) * value.ndim]
    return (first != first).astype(jnp.int32)


def pin(value, *others):
    anywhere = pl.BlockSpec(memory_space=pl.ANY)
    return pl.pallas_call(
        lambda *refs: None,
        out_shape=jax.ShapeDtypeStruct(value.shape, value.dtype),
        in_specs=[anywhere] * (1 + len(others)),
        out_specs=anywhere,
        input_output_aliases={0: 0},
        cost_estimate=BRIEF,
    )(value, *others)


def norm_rows(values, gain_vec):
    wide = values.astype(jnp.float32)
    return wide * lax.rsqrt(jnp.mean(wide * wide, axis=-1, keepdims=True) + EPS) * gain_vec


def angle_tables(places, head_dim):
    half_dim = head_dim // 2
    freqs = 1000000.0 ** (-(jnp.arange(half_dim, dtype=jnp.float32) * 2.0 / head_dim))
    angles = places[:, None] * freqs[None, :]
    return jnp.cos(angles), jnp.sin(angles)


def contract_last(left, right):
    return lax.dot_general(left, right, (((1,), (1,)), ((), ())), preferred_element_type=jnp.float32)


def whole_spec(shape):
    return pl.BlockSpec(shape, lambda *_: (0,) * len(shape))


def project_kernel(block_count, head_dim, *refs):
    row_refs = refs[:block_count]
    (gain_ref, cos_ref, sin_ref, q_gain_ref, k_gain_ref, wq_hbm, wk_hbm, wv_hbm) = refs[
        block_count : block_count + 8
    ]
    q_ref, k_ref, v_ref, wq, wk, wv, sems = refs[-7:]
    copies = [
        pltpu.make_async_copy(hbm, vmem, sems.at[at])
        for at, (hbm, vmem) in enumerate(((wq_hbm, wq), (wk_hbm, wk), (wv_hbm, wv)))
    ]
    for copy in copies:
        copy.start()
    normed = []
    for ref in row_refs:
        wide = ref[...].astype(jnp.float32)
        scale = lax.rsqrt(jnp.mean(wide * wide, axis=-1, keepdims=True) + EPS)
        normed.append((wide * scale * gain_ref[...]).astype(jnp.bfloat16))
    rows = jnp.concatenate(normed, axis=0)
    cosine, sine = cos_ref[...], sin_ref[...]

    def heads(raw, gain, out_ref):
        for at in range(raw.shape[1] // head_dim):
            head = raw[:, at * head_dim : (at + 1) * head_dim]
            scale = lax.rsqrt(jnp.mean(head * head, axis=-1, keepdims=True) + EPS)
            head = head * scale * gain
            turned = head * cosine + pltpu.roll(head, head_dim // 2, 1) * sine
            out_ref[:, at * head_dim : (at + 1) * head_dim] = turned.astype(jnp.bfloat16)

    copies[0].wait()
    heads(matmul(rows, wq[...]), q_gain_ref[...], q_ref)
    copies[1].wait()
    heads(matmul(rows, wk[...]), k_gain_ref[...], k_ref)
    copies[2].wait()
    v_ref[...] = matmul(rows, wv[...]).astype(jnp.bfloat16)


def project(blocks, gain, cosine, sine, q_gain, k_gain, q_proj, k_proj, v_proj, follows):
    head_dim = q_gain.shape[0]
    rows = sum(block.shape[0] for block in blocks)
    width = q_proj.shape[0]
    outs = (q_proj.shape[1], k_proj.shape[1], v_proj.shape[1])
    vectors = (gain[None, :], cosine, sine, q_gain[None, :], k_gain[None, :])
    return pl.pallas_call(
        functools.partial(project_kernel, len(blocks), head_dim),
        out_shape=[jax.ShapeDtypeStruct((rows, cols), jnp.bfloat16) for cols in outs],
        in_specs=[whole_spec(block.shape) for block in blocks]
        + [whole_spec(vector.shape) for vector in vectors]
        + [pl.BlockSpec(memory_space=pl.ANY)] * 4,
        out_specs=[whole_spec((rows, cols)) for cols in outs],
        grid=(1,),
        scratch_shapes=[pltpu.VMEM((width, cols), jnp.bfloat16) for cols in outs]
        + [pltpu.SemaphoreType.DMA((3,))],
        compiler_params=pltpu.CompilerParams(vmem_limit_bytes=VMEM_LIMIT),
        cost_estimate=BRIEF,
    )(*blocks, *vectors, q_proj, k_proj, v_proj, follows)


def share_kernel(share, tile, index_ref, gate, up, down, _, out, sems):
    at = pl.ds(pl.multiple_of(index_ref[0] * share, share), share)
    hidden = gate.shape[1]
    copies = [(gate.at[at, :], out.at[pl.ds(0, share), pl.ds(0, hidden)])]
    copies.append((up.at[at, :], out.at[pl.ds(0, share), pl.ds(hidden, hidden)]))
    for step in range(hidden // tile):
        rows, lanes = pl.ds(step * tile, tile), pl.ds(step * share, share)
        copies.append((down.at[rows, at], out.at[pl.ds(share, tile), lanes]))
    copies = [pltpu.make_async_copy(*ends, sems.at[at]) for at, ends in enumerate(copies)]
    for copy in copies:
        copy.start()
    for copy in copies:
        copy.wait()


def share_of(index, share, gate, up, down, follows):
    hidden = gate.shape[1]
    tile = share // 2
    return pl.pallas_call(
        functools.partial(share_kernel, share, tile),
        out_shape=jax.ShapeDtypeStruct((share + tile, 2 * hidden), gate.dtype),
        in_specs=[pl.BlockSpec(memory_space=pltpu.SMEM)] + [pl.BlockSpec(memory_space=pl.ANY)] * 4,
        out_specs=pl.BlockSpec(memory_space=pltpu.VMEM),
        scratch_shapes=[pltpu.SemaphoreType.DMA((2 + hidden // tile,))],
        cost_estimate=BRIEF,
    )(index, gate, up, down, follows)


def attend_kernel(pair, block_count, head_dim, lens_ref, *refs):
    q_refs, refs = refs[:2], refs[2:]
    k_refs, refs = refs[:block_count], refs[block_count:]
    v_refs, refs = refs[:block_count], refs[block_count:]
    sources, refs = refs[:3], refs[3 + 1 :]
    even_ref, *odd_refs, last_ref, k_all, v_all, peak, acc, attended, kp, vp, weight, sems = refs
    copies = [
        pltpu.make_async_copy(source, target, sems.at[at])
        for at, (source, target) in enumerate(zip(sources, (kp, vp, weight)))
    ]
    for copy in copies:
        copy.start()
    kv_index, start = lens_ref[0], lens_ref[1]
    rows, q_cols = q_refs[0].shape
    kv_cols = k_all.shape[1]
    group = q_cols // kv_cols
    heads = q_cols // head_dim
    span = 2 * rows
    scale = head_dim**-0.5 * math.log2(math.e)
    for refs, whole in ((k_refs, k_all), (v_refs, v_all)):
        for at, ref in enumerate(refs):
            whole[at * rows : (at + 1) * rows, :] = ref[...]
    queries = [
        jnp.concatenate([ref[:, head * head_dim : (head + 1) * head_dim] for ref in q_refs], axis=0)
        for head in range(heads)
    ]
    peak[...] = jnp.full(peak.shape, NEG, jnp.float32)
    acc[...] = jnp.zeros(acc.shape, jnp.float32)

    def absorb(keys_ref, values_ref, place, size, allowed):
        for head in range(heads):
            lanes = slice(head // group * head_dim, (head // group + 1) * head_dim)
            keys = keys_ref[pl.ds(place, size), lanes]
            values = values_ref[pl.ds(place, size), lanes]
            wide = jnp.concatenate([values, jnp.ones_like(values)], axis=1)
            scores = contract_last(queries[head], keys)
            if allowed is not None:
                scores = jnp.where(allowed, scores, NEG)
            old = peak[head][:, :1]
            new = jnp.maximum(old, jnp.max(scores, axis=1, keepdims=True))
            weights = jnp.exp2((scores - new) * scale).astype(jnp.bfloat16)
            acc[head] = acc[head] * jnp.exp2((old - new) * scale) + matmul(weights, wide)
            peak[head] = jnp.broadcast_to(new, peak.shape[1:])

    turned = kv_index % 2

    def order(axis):
        ids = lax.broadcasted_iota(jnp.int32, (span, span), axis)
        swapped = jnp.where(ids < rows, ids + rows, ids - rows)
        return jnp.where(turned == 1, swapped, ids)

    absorb(k_all, v_all, pair * span, span, order(1) <= order(0))

    def fresh_block(at, carry):
        @pl.when(((kv_index // 2) ^ at) < ((kv_index // 2) ^ pair))
        def _():
            absorb(k_all, v_all, pl.multiple_of(at * span, span), span, None)

        return carry

    lax.fori_loop(0, block_count // 2, fresh_block, 0)
    copies[0].wait()
    copies[1].wait()
    full = start // KEY_BLOCK

    def prefix_block(at, carry):
        absorb(kp, vp, pl.multiple_of(at * KEY_BLOCK, KEY_BLOCK), KEY_BLOCK, None)
        return carry

    lax.fori_loop(0, full, prefix_block, 0)

    @pl.when(full * KEY_BLOCK < start)
    def _():
        place = pl.multiple_of(full * KEY_BLOCK, KEY_BLOCK)
        ids = lax.broadcasted_iota(jnp.int32, (span, KEY_BLOCK), 1)
        absorb(kp, vp, place, KEY_BLOCK, ids < start - place)

    for head in range(heads):
        attended[:, head * head_dim : (head + 1) * head_dim] = (
            acc[head][:, :head_dim] / acc[head][:, head_dim:]
        ).astype(jnp.bfloat16)
    copies[2].wait()
    width = weight.shape[1]
    for at in range(0, width, q_cols):
        part = matmul(attended[...], weight[:, at : at + q_cols])
        even_ref[:, at : at + q_cols] = part[:rows].astype(even_ref.dtype)
        for half, odd_ref in enumerate(odd_refs):
            here = rows + half * (rows // 2)
            odd_ref[:, at : at + q_cols] = part[here : here + rows // 2].astype(odd_ref.dtype)
    last = kv_index ^ (block_count - 1)
    here = pl.multiple_of((last % 2) * rows + rows - TAIL, TAIL)
    last_ref[:, :q_cols] = attended[pl.ds(here, TAIL), :]
    ends = [ref[rows - TAIL :, :] for ref in q_refs]
    last_ref[:, q_cols : 2 * q_cols] = jnp.where(last % 2 == 1, ends[1], ends[0])
    there = pl.ds(pl.multiple_of(last * rows + rows - TAIL, TAIL), TAIL)
    last_ref[:, 2 * q_cols : 2 * q_cols + kv_cols] = k_all[there, :]
    last_ref[:, 2 * q_cols + kv_cols :] = v_all[there, :]


def attend(pair, lens, parts, head_dim, key_prefix, value_prefix, o_proj, even_type, follows):
    block_count = len(parts)
    queries, keys, values = [[part[at] for part in parts] for at in range(3)]
    queries = queries[2 * pair : 2 * pair + 2]
    rows, q_cols = queries[0].shape
    kv_cols = keys[0].shape[1]
    width = o_proj.shape[1]
    heads = q_cols // head_dim
    outs = [
        jax.ShapeDtypeStruct((rows, width), even_type),
        jax.ShapeDtypeStruct((rows // 2, width), jnp.bfloat16),
        jax.ShapeDtypeStruct((rows // 2, width), jnp.bfloat16),
        jax.ShapeDtypeStruct((TAIL, 2 * q_cols + 2 * kv_cols), jnp.bfloat16),
    ]
    return pl.pallas_call(
        functools.partial(attend_kernel, pair, block_count, head_dim),
        out_shape=outs,
        grid_spec=pltpu.PrefetchScalarGridSpec(
            num_scalar_prefetch=1,
            grid=(1,),
            in_specs=[whole_spec(part.shape) for part in queries + keys + values]
            + [pl.BlockSpec(memory_space=pl.ANY)] * 4,
            out_specs=[whole_spec(out.shape) for out in outs],
            scratch_shapes=[
                pltpu.VMEM((rows * block_count, kv_cols), jnp.bfloat16),
                pltpu.VMEM((rows * block_count, kv_cols), jnp.bfloat16),
                pltpu.VMEM((heads, 2 * rows, head_dim), jnp.float32),
                pltpu.VMEM((heads, 2 * rows, 2 * head_dim), jnp.float32),
                pltpu.VMEM((2 * rows, q_cols), jnp.bfloat16),
                pltpu.VMEM(key_prefix.shape, jnp.bfloat16),
                pltpu.VMEM(value_prefix.shape, jnp.bfloat16),
                pltpu.VMEM(o_proj.shape, jnp.bfloat16),
                pltpu.SemaphoreType.DMA((3,)),
            ],
        ),
        compiler_params=pltpu.CompilerParams(vmem_limit_bytes=VMEM_LIMIT),
        cost_estimate=BRIEF,
    )(lens, *queries, *keys, *values, key_prefix, value_prefix, o_proj, follows)


def decode_kernel(pairs, block_count, head_dim, q_cols, kv_cols, lens_ref, *refs):
    last_refs, refs = refs[:pairs], refs[pairs:]
    o_hbm, kc_hbm, vc_hbm, out_ref, kc, vc, weight, dec_in, dec_out, sems, weight_sem = refs
    kv_index = lens_ref[0]
    dec_count, slots = kc.shape[:2]
    group = q_cols // kv_cols
    kv_heads = kv_cols // head_dim
    heads = q_cols // head_dim
    scale = head_dim**-0.5 * math.log2(math.e)
    sizes = (slots // 4, slots // 2, slots)

    def by_size(together, act):
        first = together * DECODE_GROUP
        length = lens_ref[2 + first]
        for at in range(1, DECODE_GROUP):
            length = jnp.maximum(length, lens_ref[2 + first + at])
        for at, size in enumerate(sizes):
            fits = length <= size
            if at:
                fits = fits & (length > sizes[at - 1])
            pl.when(fits)(functools.partial(act, first, size))

    def cache_copies(request, size):
        return (
            pltpu.make_async_copy(
                kc_hbm.at[request, pl.ds(0, size)], kc.at[request, pl.ds(0, size)], sems.at[0, request]
            ),
            pltpu.make_async_copy(
                vc_hbm.at[request, pl.ds(0, size)], vc.at[request, pl.ds(0, size)], sems.at[1, request]
            ),
        )

    def start_copies(first, size):
        for at in range(DECODE_GROUP):
            for copy in cache_copies(first + at, size):
                copy.start()

    for together in range(dec_count // DECODE_GROUP):
        by_size(together, start_copies)
    weight_copy = pltpu.make_async_copy(o_hbm, weight, weight_sem)
    weight_copy.start()
    held = last_refs[0][...]
    for at in range(1, pairs):
        held = jnp.where((kv_index ^ (block_count - 1)) // 2 == at, last_refs[at][...], held)
    rows_in = held[TAIL - dec_count :, q_cols:].astype(jnp.float32)
    for request in range(dec_count):
        dec_in[request] = rows_in[request : request + 1]

    def attend_some(first, size):
        for at in range(DECODE_GROUP):
            attend_one(first + at, size)

    def attend_one(request, size):
        for copy in cache_copies(request, size):
            copy.wait()
        row = dec_in[request]
        empty = jnp.zeros((1, head_dim), jnp.float32)
        spread = []
        for at in range(heads):
            parts = [empty] * kv_heads
            parts[at // group] = row[:, at * head_dim : (at + 1) * head_dim]
            spread.append(jnp.concatenate(parts, axis=1))
        spread += [jnp.zeros((1, kv_cols), jnp.float32)] * (8 - len(spread))
        q_rows = jnp.concatenate(spread, axis=0)
        key_self = row[:, q_cols : q_cols + kv_cols]
        value_self = row[:, q_cols + kv_cols :]
        past = contract_last(q_rows.astype(jnp.bfloat16), kc[request, :size, :])
        ids = lax.broadcasted_iota(jnp.int32, past.shape, 1)
        past = jnp.where(ids < lens_ref[2 + request], past, NEG)
        own = jnp.sum(q_rows * key_self, axis=1, keepdims=True)
        top = jnp.maximum(jnp.max(past, axis=1, keepdims=True), own)
        past = jnp.exp2((past - top) * scale)
        own = jnp.exp2((own - top) * scale)
        total = jnp.sum(past, axis=1, keepdims=True) + own
        past = (past / total).astype(jnp.bfloat16)
        own = (own / total).astype(jnp.bfloat16).astype(jnp.float32)
        summed = matmul(past, vc[request, :size, :]) + own * value_self
        outs = []
        for at in range(heads):
            lane = (at // group) * head_dim
            outs.append(summed[at : at + 1, lane : lane + head_dim])
        dec_out[request] = jnp.concatenate(outs, axis=1)

    for together in range(dec_count // DECODE_GROUP):
        by_size(together, attend_some)
    done = [dec_out[request] for request in range(dec_count)]
    rows = jnp.concatenate([held[: TAIL - dec_count, :q_cols].astype(jnp.float32)] + done, axis=0)
    weight_copy.wait()
    out_ref[...] = matmul(rows.astype(jnp.bfloat16), weight[...]).astype(jnp.bfloat16)


def decode(lens, lasts, head_dim, block_count, o_proj, key_cache, value_cache, follows):
    dec_count, slots, kv_cols = key_cache.shape
    q_cols, width = o_proj.shape
    pairs = len(lasts)

    def kernel(lens_ref, *refs):
        given = pairs + 3
        decode_kernel(
            pairs, block_count, head_dim, q_cols, kv_cols, lens_ref, *refs[:given], *refs[given + 1 :]
        )

    return pl.pallas_call(
        kernel,
        out_shape=jax.ShapeDtypeStruct((TAIL, width), jnp.bfloat16),
        grid_spec=pltpu.PrefetchScalarGridSpec(
            num_scalar_prefetch=1,
            grid=(1,),
            in_specs=[whole_spec(last.shape) for last in lasts]
            + [pl.BlockSpec(memory_space=pl.ANY)] * 4,
            out_specs=whole_spec((TAIL, width)),
            scratch_shapes=[
                pltpu.VMEM((dec_count, slots, kv_cols), jnp.bfloat16),
                pltpu.VMEM((dec_count, slots, kv_cols), jnp.bfloat16),
                pltpu.VMEM(o_proj.shape, jnp.bfloat16),
                pltpu.VMEM((dec_count, 1, q_cols + 2 * kv_cols), jnp.float32),
                pltpu.VMEM((dec_count, 1, q_cols), jnp.float32),
                pltpu.SemaphoreType.DMA((2, dec_count)),
                pltpu.SemaphoreType.DMA,
            ],
        ),
        compiler_params=pltpu.CompilerParams(vmem_limit_bytes=VMEM_LIMIT),
        cost_estimate=BRIEF,
    )(lens, *lasts, o_proj, key_cache, value_cache, follows)


def feed_kernel(tiles, counts, added, split, *refs):
    pieces = len(counts)
    x_refs, refs = refs[:pieces], refs[pieces:]
    add_refs, refs = refs[:added], refs[added:]
    weight_refs, refs = refs[: len(refs) - 2 - pieces], refs[len(refs) - 2 - pieces :]
    out_refs, (x_all, total) = refs[:pieces], refs[pieces:]
    step = pl.program_id(0)
    cuts = [sum(counts[:at]) for at in range(pieces + 1)]

    @pl.when(step == 0)
    def _():
        for at, ref in enumerate(x_refs):
            x_all[cuts[at] : cuts[at + 1], :] = ref[...]
        for at, ref in enumerate(add_refs):
            total[cuts[at] : cuts[at + 1], :] = ref[...]

    sets = len(weight_refs) // 3 // split
    for at in range(sets):
        triples = [weight_refs[3 * part : 3 * part + 3] for part in range(at * split, (at + 1) * split)]

        @pl.when(step // tiles == at)
        def _():
            width = x_all.shape[1] // split
            gate, up, downs = 0.0, 0.0, []
            for part, (gate_ref, up_ref, down_ref) in enumerate(triples):
                rows = x_all[:, part * width : (part + 1) * width]
                tile = gate_ref.shape[-1]
                gate += matmul(rows, gate_ref[...].reshape(-1, tile))
                up += matmul(rows, up_ref[...].reshape(-1, tile))
                if split == 1:
                    downs.append(down_ref[...])
                    continue
                share = down_ref.shape[-1] // 2
                for piece in range(down_ref.shape[0]):
                    halves = [down_ref[piece, :, :share], down_ref[piece, :, share:]]
                    downs.append(jnp.concatenate(halves, axis=0))
            act = (gate / (1.0 + jnp.exp(-gate)) * up).astype(jnp.bfloat16)
            lane = 0
            for down in downs:
                lanes = slice(lane, lane + down.shape[1])
                lane += down.shape[1]
                part = matmul(act, down)
                if at or added:
                    total[:, lanes] += part
                else:
                    total[:, lanes] = jnp.where(step == 0, part, total[:, lanes] + part)

    @pl.when(step == sets * tiles - 1)
    def _():
        for at, ref in enumerate(out_refs):
            ref[...] = total[cuts[at] : cuts[at + 1], :].astype(ref.dtype)


def feed_forward(blocks, dtypes, weights, follows, adds=()):
    counts = [block.shape[0] for block in blocks]
    size, width = sum(counts), blocks[0].shape[1]
    held = weights[0]
    hidden = held[0].shape[1] if len(held) == 3 else held[0].shape[2] // 2
    tile = 256 if hidden % 256 == 0 else 128
    tiles = hidden // tile
    specs, operands = [], []
    for at, held in enumerate(weights):

        def place(step, at=at):
            return jnp.clip(step - at * tiles, 0, tiles - 1)

        if len(held) == 3:
            specs += [
                pl.BlockSpec((width, tile), lambda step, place=place: (0, place(step))),
                pl.BlockSpec((width, tile), lambda step, place=place: (0, place(step))),
                pl.BlockSpec((tile, width), lambda step, place=place: (place(step), 0)),
            ]
            operands += held
            continue
        shares = held[0].shape[0]
        share = width // shares // 2
        for half in held:
            specs += [
                pl.BlockSpec((shares, share, tile), lambda step, place=place: (0, 0, place(step))),
                pl.BlockSpec(
                    (shares, share, tile), lambda step, place=place: (0, 0, tiles + place(step))
                ),
                pl.BlockSpec((shares, tile // 2, 2 * share), lambda step, place=place: (0, 2, place(step))),
            ]
            operands += [half] * 3
    assert len({len(held) for held in weights}) == 1

    def kernel(*refs):
        given = len(blocks) + len(adds) + len(operands)
        split = 1 if len(weights[0]) == 3 else 2
        feed_kernel(tiles, counts, len(adds), split, *refs[:given], *refs[given + len(follows) :])

    return pl.pallas_call(
        kernel,
        out_shape=[
            jax.ShapeDtypeStruct((count, width), dtype) for count, dtype in zip(counts, dtypes)
        ],
        grid=(len(weights) * tiles,),
        in_specs=[whole_spec(block.shape) for block in blocks]
        + [whole_spec(add.shape) for add in adds]
        + specs
        + [pl.BlockSpec(memory_space=pl.ANY)] * len(follows),
        out_specs=[whole_spec((count, width)) for count in counts],
        scratch_shapes=[
            pltpu.VMEM((size, width), jnp.bfloat16),
            pltpu.VMEM((size, width), jnp.float32),
        ],
        compiler_params=pltpu.CompilerParams(vmem_limit_bytes=VMEM_LIMIT),
        cost_estimate=BRIEF,
    )(*blocks, *adds, *operands, *follows)


def regroup(rows_in):
    return lax.all_to_all(rows_in, ("req", "kv"), split_axis=0, concat_axis=0, tiled=True)


def matmul(left, right):
    return jnp.dot(left, right, preferred_element_type=jnp.float32)


def routes(slot_tokens, self_index, devices, rows_dev, ready):
    per_pair = rows_dev // devices
    slot_table = slot_tokens.reshape(devices, rows_dev)
    source = slot_table // rows_dev
    places = jnp.arange(rows_dev, dtype=jnp.int32)
    before = (places[:, None] < places[None, :]).astype(jnp.bfloat16)
    from_self = source == self_index
    rank = matmul(from_self.astype(jnp.bfloat16), before).astype(jnp.int32)
    local = slot_table - self_index * rows_dev
    ranked = jnp.where(from_self, rank, -1)[:, None, :] == jnp.arange(per_pair, dtype=jnp.int32)[None, :, None]
    send_rows = jnp.sum(jnp.where(ranked, local[:, None, :], 0), axis=2).reshape(-1)
    send_hot = (send_rows[:, None] == places[None, :]).astype(jnp.bfloat16)
    own = lax.dynamic_index_in_dim(source, self_index, 0, keepdims=False)
    earlier = (own[:, None] == own[None, :]) & (places[:, None] > places[None, :])
    own_rank = jnp.sum(earlier.astype(jnp.int32), axis=1)
    slot_hot = ((own * per_pair + own_rank + ready)[:, None] == places[None, :]).astype(jnp.bfloat16)
    return send_hot, slot_hot


def pick(hot, rows, transposed=False):
    if transposed:
        return lax.dot_general(
            hot, rows, (((0,), (0,)), ((), ())), preferred_element_type=jnp.float32
        ).astype(rows.dtype)
    return matmul(hot, rows).astype(rows.dtype)


def shards(
    hidden_in,
    slot_tokens,
    cache_len,
    prefill_start,
    key_cache,
    value_cache,
    key_prefix,
    value_prefix,
    attn_gain,
    q_proj,
    k_proj,
    v_proj,
    q_gain,
    k_gain,
    o_proj,
    ffn_gain,
    w_gate,
    w_up,
    w_down,
    final_gain,
    lm_head,
):
    req_count = lax.axis_size("req")
    kv_count = lax.axis_size("kv")
    devices = req_count * kv_count
    rows_dev, width = hidden_in.shape
    kv_index = lax.axis_index("kv")
    self_index = lax.axis_index("req") * kv_count + kv_index
    kv_bits = bits_below(kv_count)
    near_bits = [bit for bit in bits_below(req_count) if bit < GROUP]

    head_dim = q_gain.shape[0]
    dec_count = cache_len.shape[0]
    tok_req = rows_dev * kv_count
    fresh_count = tok_req - dec_count
    places = jnp.concatenate(
        [prefill_start[0] + jnp.arange(fresh_count, dtype=jnp.int32), cache_len]
    ).astype(jnp.float32)
    cosines, sines = angle_tables(places, head_dim)
    cosines = jnp.concatenate([cosines, cosines], axis=1)
    sines = jnp.concatenate([-sines, sines], axis=1)

    cosines, sines = lax.optimization_barrier((cosines, sines))
    ready = sum(zero_after(each) for each in (cosines, sines))

    send_hot, slot_hot = routes(slot_tokens, self_index, devices, rows_dev, ready)
    sent = pick(send_hot, hidden_in)
    arrived = regroup(sent)
    owner_rows = pick(slot_hot, arrived)
    far_count = req_count // GROUP
    share = width // kv_count // 2
    weights = (w_gate, w_up, w_down)
    far_early = share_of(kv_index[None], share, *weights, owner_rows)
    far_late = share_of(kv_index[None] + kv_count, share, *weights, owner_rows)
    held_late = far_late

    def ring(value, step):
        pairs = [(i, (i + step) % req_count) for i in range(req_count)]
        return lax.ppermute(value, "req", pairs)

    early, late, halfway = [], [], []
    for _ in range(1, far_count):
        far_early = ring(far_early, GROUP)
        early.append(far_early)
        if far_count == 2:
            halfway.append(ring(far_late, GROUP // 2))
            far_late = ring(halfway[0], GROUP // 2)
        else:
            far_late = ring(far_late, GROUP)
        late.append(far_late)

    def project_block(diff, follows):
        block_at = (kv_index ^ diff) * rows_dev
        tables = [lax.dynamic_slice_in_dim(table, block_at, rows_dev, 0) for table in (cosines, sines)]
        return project(
            [blocks[diff]], attn_gain, *tables, q_gain, k_gain, q_proj, k_proj, v_proj, follows
        )

    even = gather_xor(owner_rows, "kv", kv_bits[:0:-1])
    blocks = {0: owner_rows, 1: swap(owner_rows, "kv", 1)}
    parts = [project_block(0, owner_rows)]
    parts.append(project_block(1, parts[0][2]))
    for diff in range(2, kv_count, 2):
        blocks[diff] = pin(even[diff], parts[1][2])
        blocks[diff + 1] = swap(blocks[diff], "kv", 1)
    for diff in range(2, kv_count):
        parts.append(project_block(diff, parts[-1][2]))

    f32, bf16 = jnp.float32, jnp.bfloat16
    lens = jnp.concatenate([kv_index[None], prefill_start, cache_len]).astype(jnp.int32)
    follows, lasts, sums = held_late, {}, []
    for pair in range(kv_count // 2 - 1, -1, -1):
        sum_even, *sum_odd, lasts[pair] = attend(
            pair,
            lens,
            parts,
            head_dim,
            key_prefix[0],
            value_prefix[0],
            o_proj,
            bf16 if pair else f32,
            follows,
        )
        if pair:
            halves = [swap(pin(half, *early), "kv", 1) for half in sum_odd]
            other = jnp.concatenate(halves, axis=0)
            both = sum_even.astype(f32) + other.astype(f32)
            follows = both.astype(bf16)
            sums.append(swap(follows, "kv", 2 * pair))
        else:
            halves = [swap(pin(half, *sums, *halfway), "kv", 1) for half in sum_odd]
            sums.append(jnp.concatenate(halves, axis=0))
            own_sum = sum_even
    resid = owner_rows.astype(f32) + own_sum
    for each in sums:
        resid = resid + each.astype(f32)
    resid = resid.astype(bf16)
    ffn_in = norm_rows(resid, ffn_gain).astype(bf16)

    early_whole = [lax.all_gather(pin(held, ffn_in), "kv") for held in early]

    own_weights = (w_gate, w_up, w_down)
    near = {0: ffn_in, 1: swap(ffn_in, "req", 1), 2: swap(ffn_in, "req", 2)}

    last_sum = decode(
        lens,
        [lasts[pair] for pair in range(kv_count // 2)],
        head_dim,
        kv_count,
        o_proj,
        key_cache,
        value_cache,
        ffn_in,
    )
    far_weights = [
        (whole, lax.all_gather(pin(held, near[1][:TAIL], last_sum), "kv"))
        for whole, held in zip(early_whole, late)
    ]
    last_raw = blocks[0][rows_dev - TAIL :]
    for diff in range(1, kv_count):
        is_last = (kv_index ^ diff) == kv_count - 1
        last_raw = jnp.where(is_last, blocks[diff][rows_dev - TAIL :], last_raw)
    last_resid = last_raw.astype(f32) + last_sum.astype(f32)
    for diff in range(1, kv_count):
        last_resid = last_resid + swap(last_sum, "kv", diff).astype(f32)
    last_resid = last_resid.astype(bf16)
    last_in = norm_rows(last_resid, ffn_gain).astype(bf16)

    last_near = gather_xor(last_in, "req", near_bits)
    lasts_in = [last_near[diff] for diff in range(GROUP)]

    zero = feed_forward([ffn_in], [f32], [own_weights], [last_sum])
    near[3] = swap(near[1], "req", 2)
    some = feed_forward([near[1], near[2]], [f32] * 2, [own_weights], [zero[0], last_near[1]])
    rest = feed_forward([near[3], *lasts_in], [f32] * (1 + GROUP), [own_weights], some[:1])
    first, second = feed_forward([near[1], near[2]], [bf16] * 2, far_weights, rest[:1], some)
    third, last_part, *last_parts = feed_forward(
        [near[3], *lasts_in], [bf16, f32] + [bf16] * (GROUP - 1), far_weights, [first], rest
    )
    backs = [swap(first, "req", 1), swap(second, "req", 2), swap(third, "req", 3)]
    (own_part,) = feed_forward([ffn_in], [f32], far_weights, [third], zero)
    last_part = pin(last_part, own_part, backs[0][:TAIL], backs[1][:TAIL])
    for diff, part in enumerate(last_parts, 1):
        last_part = last_part + swap(part, "req", diff).astype(f32)
    last_rows = (last_resid.astype(f32) + last_part).astype(bf16)
    ffn_part = own_part
    for back in backs:
        ffn_part = ffn_part + back.astype(f32)
    out_rows = (resid.astype(f32) + ffn_part).astype(bf16)
    ends = jnp.where(kv_index == kv_count - 1, last_rows, out_rows[rows_dev - TAIL :])
    out_rows = jnp.concatenate([out_rows[: rows_dev - TAIL], ends], axis=0)
    returned = regroup(pick(slot_hot, out_rows, transposed=True))
    layer_out = pick(send_hot, returned, transposed=True)

    tail_count = dec_count + 1
    tails = norm_rows(last_rows, final_gain).astype(bf16)
    req_bits = bits_below(req_count)
    for bit in req_bits:
        tails = jnp.concatenate([tails, swap(tails, "req", bit)], axis=0)
    tails = pin(tails, out_rows)
    peaks = jnp.max(matmul(tails, lm_head), axis=1).reshape(req_count, TAIL)
    peaks = peaks[:, TAIL - tail_count :]
    owners = jnp.arange(req_count, dtype=jnp.int32)
    found = (owners[:, None] ^ owners[None, :]) == lax.axis_index("req")
    peaks = jnp.sum(jnp.where(found[:, :, None], peaks[None], 0.0), axis=1).reshape(1, -1)
    for axis, bits in (("kv", kv_bits), ("req", req_bits)):
        for bit in bits:
            peaks = jnp.maximum(peaks, swap(peaks, axis, bit))
    return (layer_out, peaks[0])


def solution(mesh):
    placed = (
        P(("req", "kv"), None),
        P(),
        P("req"),
        P("req"),
        P("req", None, "kv"),
        P("req", None, "kv"),
        P("req", None, "kv"),
        P("req", None, "kv"),
        P(),
        P(None, "kv"),
        P(None, "kv"),
        P(None, "kv"),
        P(),
        P(),
        P("kv", None),
        P(),
        P(None, "req"),
        P(None, "req"),
        P("req", None),
        P(),
        P(None, ("req", "kv")),
    )
    return jax.shard_map(
        shards, mesh=mesh, in_specs=placed, out_specs=(P(("req", "kv"), None), P()), check_vma=False
    )
```

```python
import functools
import math

import jax
import jax.numpy as jnp
from jax import lax
from jax.experimental import pallas as pl
from jax.experimental.pallas import tpu as pltpu
from jax.sharding import PartitionSpec as P

EPS = 1e-06
NEG = -1e30
GROUP = 4
TAIL = 16
DECODE_GROUP = 4
KEY_BLOCK = 512
VMEM_LIMIT = 56 * 1024 * 1024
BRIEF = pl.CostEstimate(flops=1, bytes_accessed=1, transcendentals=0)


def swap(value, axis, bit):
    size = lax.axis_size(axis)
    return lax.ppermute(value, axis, [(i, i ^ bit) for i in range(size)])


def bits_below(size):
    return [1 << i for i in range(size.bit_length() - 1)]


def gather_xor(value, axis, bits):
    held = {0: value}
    for bit in bits:
        held.update({diff ^ bit: swap(block, axis, bit) for diff, block in list(held.items())})
    return held


def zero_after(value):
    first = value[(0,) * value.ndim]
    return (first != first).astype(jnp.int32)


def pin(value, *others):
    anywhere = pl.BlockSpec(memory_space=pl.ANY)
    return pl.pallas_call(
        lambda *refs: None,
        out_shape=jax.ShapeDtypeStruct(value.shape, value.dtype),
        in_specs=[anywhere] * (1 + len(others)),
        out_specs=anywhere,
        input_output_aliases={0: 0},
        cost_estimate=BRIEF,
    )(value, *others)


def norm_rows(values, gain_vec):
    wide = values.astype(jnp.float32)
    return wide * lax.rsqrt(jnp.mean(wide * wide, axis=-1, keepdims=True) + EPS) * gain_vec


def angle_tables(places, head_dim):
    half_dim = head_dim // 2
    freqs = 1000000.0 ** (-(jnp.arange(half_dim, dtype=jnp.float32) * 2.0 / head_dim))
    angles = places[:, None] * freqs[None, :]
    return jnp.cos(angles), jnp.sin(angles)


def contract_last(left, right):
    return lax.dot_general(left, right, (((1,), (1,)), ((), ())), preferred_element_type=jnp.float32)


def whole_spec(shape):
    return pl.BlockSpec(shape, lambda *_: (0,) * len(shape))


def project_kernel(block_count, head_dim, *refs):
    row_refs = refs[:block_count]
    (gain_ref, cos_ref, sin_ref, q_gain_ref, k_gain_ref, wq_hbm, wk_hbm, wv_hbm) = refs[
        block_count : block_count + 8
    ]
    q_ref, k_ref, v_ref, wq, wk, wv, sems = refs[-7:]
    copies = [
        pltpu.make_async_copy(hbm, vmem, sems.at[at])
        for at, (hbm, vmem) in enumerate(((wq_hbm, wq), (wk_hbm, wk), (wv_hbm, wv)))
    ]
    for copy in copies:
        copy.start()
    normed = []
    for ref in row_refs:
        wide = ref[...].astype(jnp.float32)
        scale = lax.rsqrt(jnp.mean(wide * wide, axis=-1, keepdims=True) + EPS)
        normed.append((wide * scale * gain_ref[...]).astype(jnp.bfloat16))
    rows = jnp.concatenate(normed, axis=0)
    cosine, sine = cos_ref[...], sin_ref[...]

    def heads(raw, gain, out_ref):
        for at in range(raw.shape[1] // head_dim):
            head = raw[:, at * head_dim : (at + 1) * head_dim]
            scale = lax.rsqrt(jnp.mean(head * head, axis=-1, keepdims=True) + EPS)
            head = head * scale * gain
            turned = head * cosine + pltpu.roll(head, head_dim // 2, 1) * sine
            out_ref[:, at * head_dim : (at + 1) * head_dim] = turned.astype(jnp.bfloat16)

    copies[0].wait()
    heads(matmul(rows, wq[...]), q_gain_ref[...], q_ref)
    copies[1].wait()
    heads(matmul(rows, wk[...]), k_gain_ref[...], k_ref)
    copies[2].wait()
    v_ref[...] = matmul(rows, wv[...]).astype(jnp.bfloat16)


def project(blocks, gain, cosine, sine, q_gain, k_gain, q_proj, k_proj, v_proj, follows):
    head_dim = q_gain.shape[0]
    rows = sum(block.shape[0] for block in blocks)
    width = q_proj.shape[0]
    outs = (q_proj.shape[1], k_proj.shape[1], v_proj.shape[1])
    vectors = (gain[None, :], cosine, sine, q_gain[None, :], k_gain[None, :])
    return pl.pallas_call(
        functools.partial(project_kernel, len(blocks), head_dim),
        out_shape=[jax.ShapeDtypeStruct((rows, cols), jnp.bfloat16) for cols in outs],
        in_specs=[whole_spec(block.shape) for block in blocks]
        + [whole_spec(vector.shape) for vector in vectors]
        + [pl.BlockSpec(memory_space=pl.ANY)] * 4,
        out_specs=[whole_spec((rows, cols)) for cols in outs],
        grid=(1,),
        scratch_shapes=[pltpu.VMEM((width, cols), jnp.bfloat16) for cols in outs]
        + [pltpu.SemaphoreType.DMA((3,))],
        compiler_params=pltpu.CompilerParams(vmem_limit_bytes=VMEM_LIMIT),
        cost_estimate=BRIEF,
    )(*blocks, *vectors, q_proj, k_proj, v_proj, follows)


def share_kernel(share, tile, index_ref, gate, up, down, _, out, sems):
    at = pl.ds(pl.multiple_of(index_ref[0] * share, share), share)
    hidden = gate.shape[1]
    copies = [(gate.at[at, :], out.at[pl.ds(0, share), pl.ds(0, hidden)])]
    copies.append((up.at[at, :], out.at[pl.ds(0, share), pl.ds(hidden, hidden)]))
    for step in range(hidden // tile):
        rows, lanes = pl.ds(step * tile, tile), pl.ds(step * share, share)
        copies.append((down.at[rows, at], out.at[pl.ds(share, tile), lanes]))
    copies = [pltpu.make_async_copy(*ends, sems.at[at]) for at, ends in enumerate(copies)]
    for copy in copies:
        copy.start()
    for copy in copies:
        copy.wait()


def share_of(index, share, gate, up, down, follows):
    hidden = gate.shape[1]
    tile = share // 2
    return pl.pallas_call(
        functools.partial(share_kernel, share, tile),
        out_shape=jax.ShapeDtypeStruct((share + tile, 2 * hidden), gate.dtype),
        in_specs=[pl.BlockSpec(memory_space=pltpu.SMEM)] + [pl.BlockSpec(memory_space=pl.ANY)] * 4,
        out_specs=pl.BlockSpec(memory_space=pltpu.VMEM),
        scratch_shapes=[pltpu.SemaphoreType.DMA((2 + hidden // tile,))],
        cost_estimate=BRIEF,
    )(index, gate, up, down, follows)


def attend_kernel(pair, block_count, head_dim, lens_ref, *refs):
    q_refs, refs = refs[:2], refs[2:]
    k_refs, refs = refs[:block_count], refs[block_count:]
    v_refs, refs = refs[:block_count], refs[block_count:]
    sources, refs = refs[:3], refs[3 + 1 :]
    even_ref, *odd_refs, last_ref, k_all, v_all, peak, acc, attended, kp, vp, weight, sems = refs
    copies = [
        pltpu.make_async_copy(source, target, sems.at[at])
        for at, (source, target) in enumerate(zip(sources, (kp, vp, weight)))
    ]
    for copy in copies:
        copy.start()
    kv_index, start = lens_ref[0], lens_ref[1]
    rows, q_cols = q_refs[0].shape
    kv_cols = k_all.shape[1]
    group = q_cols // kv_cols
    heads = q_cols // head_dim
    span = 2 * rows
    scale = head_dim**-0.5 * math.log2(math.e)
    for refs, whole in ((k_refs, k_all), (v_refs, v_all)):
        for at, ref in enumerate(refs):
            whole[at * rows : (at + 1) * rows, :] = ref[...]
    queries = [
        jnp.concatenate([ref[:, head * head_dim : (head + 1) * head_dim] for ref in q_refs], axis=0)
        for head in range(heads)
    ]
    peak[...] = jnp.full(peak.shape, NEG, jnp.float32)
    acc[...] = jnp.zeros(acc.shape, jnp.float32)

    def absorb(keys_ref, values_ref, place, size, allowed):
        for head in range(heads):
            lanes = slice(head // group * head_dim, (head // group + 1) * head_dim)
            keys = keys_ref[pl.ds(place, size), lanes]
            values = values_ref[pl.ds(place, size), lanes]
            wide = jnp.concatenate([values, jnp.ones_like(values)], axis=1)
            scores = contract_last(queries[head], keys)
            if allowed is not None:
                scores = jnp.where(allowed, scores, NEG)
            old = peak[head][:, :1]
            new = jnp.maximum(old, jnp.max(scores, axis=1, keepdims=True))
            weights = jnp.exp2((scores - new) * scale).astype(jnp.bfloat16)
            acc[head] = acc[head] * jnp.exp2((old - new) * scale) + matmul(weights, wide)
            peak[head] = jnp.broadcast_to(new, peak.shape[1:])

    turned = kv_index % 2

    def order(axis):
        ids = lax.broadcasted_iota(jnp.int32, (span, span), axis)
        swapped = jnp.where(ids < rows, ids + rows, ids - rows)
        return jnp.where(turned == 1, swapped, ids)

    absorb(k_all, v_all, pair * span, span, order(1) <= order(0))

    def fresh_block(at, carry):
        @pl.when(((kv_index // 2) ^ at) < ((kv_index // 2) ^ pair))
        def _():
            absorb(k_all, v_all, pl.multiple_of(at * span, span), span, None)

        return carry

    lax.fori_loop(0, block_count // 2, fresh_block, 0)
    copies[0].wait()
    copies[1].wait()
    full = start // KEY_BLOCK

    def prefix_block(at, carry):
        absorb(kp, vp, pl.multiple_of(at * KEY_BLOCK, KEY_BLOCK), KEY_BLOCK, None)
        return carry

    lax.fori_loop(0, full, prefix_block, 0)

    @pl.when(full * KEY_BLOCK < start)
    def _():
        place = pl.multiple_of(full * KEY_BLOCK, KEY_BLOCK)
        ids = lax.broadcasted_iota(jnp.int32, (span, KEY_BLOCK), 1)
        absorb(kp, vp, place, KEY_BLOCK, ids < start - place)

    for head in range(heads):
        attended[:, head * head_dim : (head + 1) * head_dim] = (
            acc[head][:, :head_dim] / acc[head][:, head_dim:]
        ).astype(jnp.bfloat16)
    copies[2].wait()
    width = weight.shape[1]
    for at in range(0, width, q_cols):
        part = matmul(attended[...], weight[:, at : at + q_cols])
        even_ref[:, at : at + q_cols] = part[:rows].astype(even_ref.dtype)
        for half, odd_ref in enumerate(odd_refs):
            here = rows + half * (rows // 2)
            odd_ref[:, at : at + q_cols] = part[here : here + rows // 2].astype(odd_ref.dtype)
    last = kv_index ^ (block_count - 1)
    here = pl.multiple_of((last % 2) * rows + rows - TAIL, TAIL)
    last_ref[:, :q_cols] = attended[pl.ds(here, TAIL), :]
    ends = [ref[rows - TAIL :, :] for ref in q_refs]
    last_ref[:, q_cols : 2 * q_cols] = jnp.where(last % 2 == 1, ends[1], ends[0])
    there = pl.ds(pl.multiple_of(last * rows + rows - TAIL, TAIL), TAIL)
    last_ref[:, 2 * q_cols : 2 * q_cols + kv_cols] = k_all[there, :]
    last_ref[:, 2 * q_cols + kv_cols :] = v_all[there, :]


def attend(pair, lens, parts, head_dim, key_prefix, value_prefix, o_proj, even_type, follows):
    block_count = len(parts)
    queries, keys, values = [[part[at] for part in parts] for at in range(3)]
    queries = queries[2 * pair : 2 * pair + 2]
    rows, q_cols = queries[0].shape
    kv_cols = keys[0].shape[1]
    width = o_proj.shape[1]
    heads = q_cols // head_dim
    outs = [
        jax.ShapeDtypeStruct((rows, width), even_type),
        jax.ShapeDtypeStruct((rows // 2, width), jnp.bfloat16),
        jax.ShapeDtypeStruct((rows // 2, width), jnp.bfloat16),
        jax.ShapeDtypeStruct((TAIL, 2 * q_cols + 2 * kv_cols), jnp.bfloat16),
    ]
    return pl.pallas_call(
        functools.partial(attend_kernel, pair, block_count, head_dim),
        out_shape=outs,
        grid_spec=pltpu.PrefetchScalarGridSpec(
            num_scalar_prefetch=1,
            grid=(1,),
            in_specs=[whole_spec(part.shape) for part in queries + keys + values]
            + [pl.BlockSpec(memory_space=pl.ANY)] * 4,
            out_specs=[whole_spec(out.shape) for out in outs],
            scratch_shapes=[
                pltpu.VMEM((rows * block_count, kv_cols), jnp.bfloat16),
                pltpu.VMEM((rows * block_count, kv_cols), jnp.bfloat16),
                pltpu.VMEM((heads, 2 * rows, head_dim), jnp.float32),
                pltpu.VMEM((heads, 2 * rows, 2 * head_dim), jnp.float32),
                pltpu.VMEM((2 * rows, q_cols), jnp.bfloat16),
                pltpu.VMEM(key_prefix.shape, jnp.bfloat16),
                pltpu.VMEM(value_prefix.shape, jnp.bfloat16),
                pltpu.VMEM(o_proj.shape, jnp.bfloat16),
                pltpu.SemaphoreType.DMA((3,)),
            ],
        ),
        compiler_params=pltpu.CompilerParams(vmem_limit_bytes=VMEM_LIMIT),
        cost_estimate=BRIEF,
    )(lens, *queries, *keys, *values, key_prefix, value_prefix, o_proj, follows)


def decode_kernel(pairs, block_count, head_dim, q_cols, kv_cols, lens_ref, *refs):
    last_refs, refs = refs[:pairs], refs[pairs:]
    o_hbm, kc_hbm, vc_hbm, out_ref, kc, vc, weight, dec_in, dec_out, sems, weight_sem = refs
    kv_index = lens_ref[0]
    dec_count, slots = kc.shape[:2]
    group = q_cols // kv_cols
    kv_heads = kv_cols // head_dim
    heads = q_cols // head_dim
    scale = head_dim**-0.5 * math.log2(math.e)
    sizes = (slots // 4, slots // 2, slots)

    def by_size(together, act):
        first = together * DECODE_GROUP
        length = lens_ref[2 + first]
        for at in range(1, DECODE_GROUP):
            length = jnp.maximum(length, lens_ref[2 + first + at])
        for at, size in enumerate(sizes):
            fits = length <= size
            if at:
                fits = fits & (length > sizes[at - 1])
            pl.when(fits)(functools.partial(act, first, size))

    def cache_copies(request, size):
        return (
            pltpu.make_async_copy(
                kc_hbm.at[request, pl.ds(0, size)], kc.at[request, pl.ds(0, size)], sems.at[0, request]
            ),
            pltpu.make_async_copy(
                vc_hbm.at[request, pl.ds(0, size)], vc.at[request, pl.ds(0, size)], sems.at[1, request]
            ),
        )

    def start_copies(first, size):
        for at in range(DECODE_GROUP):
            for copy in cache_copies(first + at, size):
                copy.start()

    for together in range(dec_count // DECODE_GROUP):
        by_size(together, start_copies)
    weight_copy = pltpu.make_async_copy(o_hbm, weight, weight_sem)
    weight_copy.start()
    held = last_refs[0][...]
    for at in range(1, pairs):
        held = jnp.where((kv_index ^ (block_count - 1)) // 2 == at, last_refs[at][...], held)
    rows_in = held[TAIL - dec_count :, q_cols:].astype(jnp.float32)
    for request in range(dec_count):
        dec_in[request] = rows_in[request : request + 1]

    def attend_some(first, size):
        for at in range(DECODE_GROUP):
            attend_one(first + at, size)

    def attend_one(request, size):
        for copy in cache_copies(request, size):
            copy.wait()
        row = dec_in[request]
        empty = jnp.zeros((1, head_dim), jnp.float32)
        spread = []
        for at in range(heads):
            parts = [empty] * kv_heads
            parts[at // group] = row[:, at * head_dim : (at + 1) * head_dim]
            spread.append(jnp.concatenate(parts, axis=1))
        spread += [jnp.zeros((1, kv_cols), jnp.float32)] * (8 - len(spread))
        q_rows = jnp.concatenate(spread, axis=0)
        key_self = row[:, q_cols : q_cols + kv_cols]
        value_self = row[:, q_cols + kv_cols :]
        past = contract_last(q_rows.astype(jnp.bfloat16), kc[request, :size, :])
        ids = lax.broadcasted_iota(jnp.int32, past.shape, 1)
        past = jnp.where(ids < lens_ref[2 + request], past, NEG)
        own = jnp.sum(q_rows * key_self, axis=1, keepdims=True)
        top = jnp.maximum(jnp.max(past, axis=1, keepdims=True), own)
        past = jnp.exp2((past - top) * scale)
        own = jnp.exp2((own - top) * scale)
        total = jnp.sum(past, axis=1, keepdims=True) + own
        past = (past / total).astype(jnp.bfloat16)
        own = (own / total).astype(jnp.bfloat16).astype(jnp.float32)
        summed = matmul(past, vc[request, :size, :]) + own * value_self
        outs = []
        for at in range(heads):
            lane = (at // group) * head_dim
            outs.append(summed[at : at + 1, lane : lane + head_dim])
        dec_out[request] = jnp.concatenate(outs, axis=1)

    for together in range(dec_count // DECODE_GROUP):
        by_size(together, attend_some)
    done = [dec_out[request] for request in range(dec_count)]
    rows = jnp.concatenate([held[: TAIL - dec_count, :q_cols].astype(jnp.float32)] + done, axis=0)
    weight_copy.wait()
    out_ref[...] = matmul(rows.astype(jnp.bfloat16), weight[...]).astype(jnp.bfloat16)


def decode(lens, lasts, head_dim, block_count, o_proj, key_cache, value_cache, follows):
    dec_count, slots, kv_cols = key_cache.shape
    q_cols, width = o_proj.shape
    pairs = len(lasts)

    def kernel(lens_ref, *refs):
        given = pairs + 3
        decode_kernel(
            pairs, block_count, head_dim, q_cols, kv_cols, lens_ref, *refs[:given], *refs[given + 1 :]
        )

    return pl.pallas_call(
        kernel,
        out_shape=jax.ShapeDtypeStruct((TAIL, width), jnp.bfloat16),
        grid_spec=pltpu.PrefetchScalarGridSpec(
            num_scalar_prefetch=1,
            grid=(1,),
            in_specs=[whole_spec(last.shape) for last in lasts]
            + [pl.BlockSpec(memory_space=pl.ANY)] * 4,
            out_specs=whole_spec((TAIL, width)),
            scratch_shapes=[
                pltpu.VMEM((dec_count, slots, kv_cols), jnp.bfloat16),
                pltpu.VMEM((dec_count, slots, kv_cols), jnp.bfloat16),
                pltpu.VMEM(o_proj.shape, jnp.bfloat16),
                pltpu.VMEM((dec_count, 1, q_cols + 2 * kv_cols), jnp.float32),
                pltpu.VMEM((dec_count, 1, q_cols), jnp.float32),
                pltpu.SemaphoreType.DMA((2, dec_count)),
                pltpu.SemaphoreType.DMA,
            ],
        ),
        compiler_params=pltpu.CompilerParams(vmem_limit_bytes=VMEM_LIMIT),
        cost_estimate=BRIEF,
    )(lens, *lasts, o_proj, key_cache, value_cache, follows)


def feed_kernel(tiles, counts, added, split, *refs):
    pieces = len(counts)
    x_refs, refs = refs[:pieces], refs[pieces:]
    add_refs, refs = refs[:added], refs[added:]
    weight_refs, refs = refs[: len(refs) - 2 - pieces], refs[len(refs) - 2 - pieces :]
    out_refs, (x_all, total) = refs[:pieces], refs[pieces:]
    step = pl.program_id(0)
    cuts = [sum(counts[:at]) for at in range(pieces + 1)]

    @pl.when(step == 0)
    def _():
        for at, ref in enumerate(x_refs):
            x_all[cuts[at] : cuts[at + 1], :] = ref[...]
        for at, ref in enumerate(add_refs):
            total[cuts[at] : cuts[at + 1], :] = ref[...]

    sets = len(weight_refs) // 3 // split
    for at in range(sets):
        triples = [weight_refs[3 * part : 3 * part + 3] for part in range(at * split, (at + 1) * split)]

        @pl.when(step // tiles == at)
        def _():
            width = x_all.shape[1] // split
            gate, up, downs = 0.0, 0.0, []
            for part, (gate_ref, up_ref, down_ref) in enumerate(triples):
                rows = x_all[:, part * width : (part + 1) * width]
                tile = gate_ref.shape[-1]
                gate += matmul(rows, gate_ref[...].reshape(-1, tile))
                up += matmul(rows, up_ref[...].reshape(-1, tile))
                if split == 1:
                    downs.append(down_ref[...])
                    continue
                share = down_ref.shape[-1] // 2
                for piece in range(down_ref.shape[0]):
                    halves = [down_ref[piece, :, :share], down_ref[piece, :, share:]]
                    downs.append(jnp.concatenate(halves, axis=0))
            act = (gate / (1.0 + jnp.exp(-gate)) * up).astype(jnp.bfloat16)
            lane = 0
            for down in downs:
                lanes = slice(lane, lane + down.shape[1])
                lane += down.shape[1]
                part = matmul(act, down)
                if at or added:
                    total[:, lanes] += part
                else:
                    total[:, lanes] = jnp.where(step == 0, part, total[:, lanes] + part)

    @pl.when(step == sets * tiles - 1)
    def _():
        for at, ref in enumerate(out_refs):
            ref[...] = total[cuts[at] : cuts[at + 1], :].astype(ref.dtype)


def feed_forward(blocks, dtypes, weights, follows, adds=()):
    counts = [block.shape[0] for block in blocks]
    size, width = sum(counts), blocks[0].shape[1]
    held = weights[0]
    hidden = held[0].shape[1] if len(held) == 3 else held[0].shape[2] // 2
    tile = 256 if hidden % 256 == 0 else 128
    tiles = hidden // tile
    specs, operands = [], []
    for at, held in enumerate(weights):

        def place(step, at=at):
            return jnp.clip(step - at * tiles, 0, tiles - 1)

        if len(held) == 3:
            specs += [
                pl.BlockSpec((width, tile), lambda step, place=place: (0, place(step))),
                pl.BlockSpec((width, tile), lambda step, place=place: (0, place(step))),
                pl.BlockSpec((tile, width), lambda step, place=place: (place(step), 0)),
            ]
            operands += held
            continue
        shares = held[0].shape[0]
        share = width // shares // 2
        for half in held:
            specs += [
                pl.BlockSpec((shares, share, tile), lambda step, place=place: (0, 0, place(step))),
                pl.BlockSpec(
                    (shares, share, tile), lambda step, place=place: (0, 0, tiles + place(step))
                ),
                pl.BlockSpec((shares, tile // 2, 2 * share), lambda step, place=place: (0, 2, place(step))),
            ]
            operands += [half] * 3
    assert len({len(held) for held in weights}) == 1

    def kernel(*refs):
        given = len(blocks) + len(adds) + len(operands)
        split = 1 if len(weights[0]) == 3 else 2
        feed_kernel(tiles, counts, len(adds), split, *refs[:given], *refs[given + len(follows) :])

    return pl.pallas_call(
        kernel,
        out_shape=[
            jax.ShapeDtypeStruct((count, width), dtype) for count, dtype in zip(counts, dtypes)
        ],
        grid=(len(weights) * tiles,),
        in_specs=[whole_spec(block.shape) for block in blocks]
        + [whole_spec(add.shape) for add in adds]
        + specs
        + [pl.BlockSpec(memory_space=pl.ANY)] * len(follows),
        out_specs=[whole_spec((count, width)) for count in counts],
        scratch_shapes=[
            pltpu.VMEM((size, width), jnp.bfloat16),
            pltpu.VMEM((size, width), jnp.float32),
        ],
        compiler_params=pltpu.CompilerParams(vmem_limit_bytes=VMEM_LIMIT),
        cost_estimate=BRIEF,
    )(*blocks, *adds, *operands, *follows)


def regroup(rows_in):
    return lax.all_to_all(rows_in, ("req", "kv"), split_axis=0, concat_axis=0, tiled=True)


def matmul(left, right):
    return jnp.dot(left, right, preferred_element_type=jnp.float32)


def routes(slot_tokens, self_index, devices, rows_dev, ready):
    per_pair = rows_dev // devices
    slot_table = slot_tokens.reshape(devices, rows_dev)
    source = slot_table // rows_dev
    places = jnp.arange(rows_dev, dtype=jnp.int32)
    before = (places[:, None] < places[None, :]).astype(jnp.bfloat16)
    from_self = source == self_index
    rank = matmul(from_self.astype(jnp.bfloat16), before).astype(jnp.int32)
    local = slot_table - self_index * rows_dev
    ranked = jnp.where(from_self, rank, -1)[:, None, :] == jnp.arange(per_pair, dtype=jnp.int32)[None, :, None]
    send_rows = jnp.sum(jnp.where(ranked, local[:, None, :], 0), axis=2).reshape(-1)
    send_hot = (send_rows[:, None] == places[None, :]).astype(jnp.bfloat16)
    own = lax.dynamic_index_in_dim(source, self_index, 0, keepdims=False)
    earlier = (own[:, None] == own[None, :]) & (places[:, None] > places[None, :])
    own_rank = jnp.sum(earlier.astype(jnp.int32), axis=1)
    slot_hot = ((own * per_pair + own_rank + ready)[:, None] == places[None, :]).astype(jnp.bfloat16)
    return send_hot, slot_hot


def pick(hot, rows, transposed=False):
    if transposed:
        return lax.dot_general(
            hot, rows, (((0,), (0,)), ((), ())), preferred_element_type=jnp.float32
        ).astype(rows.dtype)
    return matmul(hot, rows).astype(rows.dtype)


def shards(
    hidden_in,
    slot_tokens,
    cache_len,
    prefill_start,
    key_cache,
    value_cache,
    key_prefix,
    value_prefix,
    attn_gain,
    q_proj,
    k_proj,
    v_proj,
    q_gain,
    k_gain,
    o_proj,
    ffn_gain,
    w_gate,
    w_up,
    w_down,
    final_gain,
    lm_head,
):
    req_count = lax.axis_size("req")
    kv_count = lax.axis_size("kv")
    devices = req_count * kv_count
    rows_dev, width = hidden_in.shape
    kv_index = lax.axis_index("kv")
    self_index = lax.axis_index("req") * kv_count + kv_index
    kv_bits = bits_below(kv_count)
    near_bits = [bit for bit in bits_below(req_count) if bit < GROUP]

    head_dim = q_gain.shape[0]
    dec_count = cache_len.shape[0]
    tok_req = rows_dev * kv_count
    fresh_count = tok_req - dec_count
    places = jnp.concatenate(
        [prefill_start[0] + jnp.arange(fresh_count, dtype=jnp.int32), cache_len]
    ).astype(jnp.float32)
    cosines, sines = angle_tables(places, head_dim)
    cosines = jnp.concatenate([cosines, cosines], axis=1)
    sines = jnp.concatenate([-sines, sines], axis=1)

    cosines, sines = lax.optimization_barrier((cosines, sines))
    ready = sum(zero_after(each) for each in (cosines, sines))

    send_hot, slot_hot = routes(slot_tokens, self_index, devices, rows_dev, ready)
    sent = pick(send_hot, hidden_in)
    arrived = regroup(sent)
    owner_rows = pick(slot_hot, arrived)
    far_count = req_count // GROUP
    share = width // kv_count // 2
    weights = (w_gate, w_up, w_down)
    far_early = share_of(kv_index[None], share, *weights, owner_rows)
    far_late = share_of(kv_index[None] + kv_count, share, *weights, owner_rows)
    held_late = far_late

    def ring(value, step):
        pairs = [(i, (i + step) % req_count) for i in range(req_count)]
        return lax.ppermute(value, "req", pairs)

    early, late, halfway = [], [], []
    for _ in range(1, far_count):
        far_early = ring(far_early, GROUP)
        early.append(far_early)
        if far_count == 2:
            halfway.append(ring(far_late, GROUP // 2))
            far_late = ring(halfway[0], GROUP // 2)
        else:
            far_late = ring(far_late, GROUP)
        late.append(far_late)

    def project_block(diff, follows):
        block_at = (kv_index ^ diff) * rows_dev
        tables = [lax.dynamic_slice_in_dim(table, block_at, rows_dev, 0) for table in (cosines, sines)]
        return project(
            [blocks[diff]], attn_gain, *tables, q_gain, k_gain, q_proj, k_proj, v_proj, follows
        )

    even = gather_xor(owner_rows, "kv", kv_bits[:0:-1])
    blocks = {0: owner_rows, 1: swap(owner_rows, "kv", 1)}
    parts = [project_block(0, owner_rows)]
    parts.append(project_block(1, parts[0][2]))
    for diff in range(2, kv_count, 2):
        blocks[diff] = pin(even[diff], parts[1][2])
        blocks[diff + 1] = swap(blocks[diff], "kv", 1)
    for diff in range(2, kv_count):
        parts.append(project_block(diff, parts[-1][2]))

    f32, bf16 = jnp.float32, jnp.bfloat16
    lens = jnp.concatenate([kv_index[None], prefill_start, cache_len]).astype(jnp.int32)
    follows, lasts, sums = held_late, {}, []
    for pair in range(kv_count // 2 - 1, -1, -1):
        sum_even, *sum_odd, lasts[pair] = attend(
            pair,
            lens,
            parts,
            head_dim,
            key_prefix[0],
            value_prefix[0],
            o_proj,
            bf16 if pair else f32,
            follows,
        )
        if pair:
            halves = [swap(pin(half, *early), "kv", 1) for half in sum_odd]
            other = jnp.concatenate(halves, axis=0)
            both = sum_even.astype(f32) + other.astype(f32)
            follows = both.astype(bf16)
            sums.append(swap(follows, "kv", 2 * pair))
        else:
            halves = [swap(pin(half, *sums, *halfway), "kv", 1) for half in sum_odd]
            sums.append(jnp.concatenate(halves, axis=0))
            own_sum = sum_even
    resid = owner_rows.astype(f32) + own_sum
    for each in sums:
        resid = resid + each.astype(f32)
    resid = resid.astype(bf16)
    ffn_in = norm_rows(resid, ffn_gain).astype(bf16)

    early_whole = [lax.all_gather(pin(held, ffn_in), "kv") for held in early]

    own_weights = (w_gate, w_up, w_down)
    near = {0: ffn_in, 1: swap(ffn_in, "req", 1), 2: swap(ffn_in, "req", 2)}

    last_sum = decode(
        lens,
        [lasts[pair] for pair in range(kv_count // 2)],
        head_dim,
        kv_count,
        o_proj,
        key_cache,
        value_cache,
        ffn_in,
    )
    far_weights = [
        (whole, lax.all_gather(pin(held, near[1][:TAIL], last_sum), "kv"))
        for whole, held in zip(early_whole, late)
    ]
    last_raw = blocks[0][rows_dev - TAIL :]
    for diff in range(1, kv_count):
        is_last = (kv_index ^ diff) == kv_count - 1
        last_raw = jnp.where(is_last, blocks[diff][rows_dev - TAIL :], last_raw)
    last_resid = last_raw.astype(f32) + last_sum.astype(f32)
    for diff in range(1, kv_count):
        last_resid = last_resid + swap(last_sum, "kv", diff).astype(f32)
    last_resid = last_resid.astype(bf16)
    last_in = norm_rows(last_resid, ffn_gain).astype(bf16)

    last_near = gather_xor(last_in, "req", near_bits)
    lasts_in = [last_near[diff] for diff in range(GROUP)]

    zero = feed_forward([ffn_in], [f32], [own_weights], [last_sum])
    near[3] = swap(near[1], "req", 2)
    some = feed_forward([near[1], near[2]], [f32] * 2, [own_weights], [zero[0], last_near[1]])
    first, second = feed_forward([near[1], near[2]], [bf16] * 2, far_weights, [some[0], *lasts_in[2:]], some)
    rest = feed_forward([near[3], *lasts_in], [f32] * (1 + GROUP), [own_weights], [first])
    third, last_part, *last_parts = feed_forward(
        [near[3], *lasts_in], [bf16, f32] + [bf16] * (GROUP - 1), far_weights, [first], rest
    )
    backs = [swap(first, "req", 1), swap(second, "req", 2), swap(third, "req", 3)]
    (own_part,) = feed_forward([ffn_in], [f32], far_weights, [third], zero)
    last_part = pin(last_part, own_part, backs[0][:TAIL], backs[1][:TAIL])
    for diff, part in enumerate(last_parts, 1):
        last_part = last_part + swap(part, "req", diff).astype(f32)
    last_rows = (last_resid.astype(f32) + last_part).astype(bf16)
    ffn_part = own_part
    for back in backs:
        ffn_part = ffn_part + back.astype(f32)
    out_rows = (resid.astype(f32) + ffn_part).astype(bf16)
    ends = jnp.where(kv_index == kv_count - 1, last_rows, out_rows[rows_dev - TAIL :])
    out_rows = jnp.concatenate([out_rows[: rows_dev - TAIL], ends], axis=0)
    returned = regroup(pick(slot_hot, out_rows, transposed=True))
    layer_out = pick(send_hot, returned, transposed=True)

    tail_count = dec_count + 1
    tails = norm_rows(last_rows, final_gain).astype(bf16)
    req_bits = bits_below(req_count)
    for bit in req_bits:
        tails = jnp.concatenate([tails, swap(tails, "req", bit)], axis=0)
    tails = pin(tails, out_rows)
    peaks = jnp.max(matmul(tails, lm_head), axis=1).reshape(req_count, TAIL)
    peaks = peaks[:, TAIL - tail_count :]
    owners = jnp.arange(req_count, dtype=jnp.int32)
    found = (owners[:, None] ^ owners[None, :]) == lax.axis_index("req")
    peaks = jnp.sum(jnp.where(found[:, :, None], peaks[None], 0.0), axis=1).reshape(1, -1)
    for axis, bits in (("kv", kv_bits), ("req", req_bits)):
        for bit in bits:
            peaks = jnp.maximum(peaks, swap(peaks, axis, bit))
    return (layer_out, peaks[0])


def solution(mesh):
    placed = (
        P(("req", "kv"), None),
        P(),
        P("req"),
        P("req"),
        P("req", None, "kv"),
        P("req", None, "kv"),
        P("req", None, "kv"),
        P("req", None, "kv"),
        P(),
        P(None, "kv"),
        P(None, "kv"),
        P(None, "kv"),
        P(),
        P(),
        P("kv", None),
        P(),
        P(None, "req"),
        P(None, "req"),
        P("req", None),
        P(),
        P(None, ("req", "kv")),
    )
    return jax.shard_map(
        shards, mesh=mesh, in_specs=placed, out_specs=(P(("req", "kv"), None), P()), check_vma=False
    )
```
